32 devices in a mesh: grp: 2 (over y), sp: 4 (over z), fr: 2 (over x), dr: 2 (over core).
Axes of the slice: x: 2, y: 2, z: 4, core: 2. Of those that a mesh axis runs over, the one named last changes fastest.
Arguments:
- grid_spec: float32 [36, 36, 32, 128], P('fr', 'dr', ('grp', 'sp')), parts along dimension 2, may hold values from 0 to 2
- mesh_spec: float32 [36, 36, 4096], P('fr', 'dr', ('grp', 'sp')), parts along dimension 2, may hold values from 0 to 2
- grid_sea: int32 [32, 128], P(('grp', 'sp')), parts along dimension 0, may hold values 0 or 1
- grid_speed: float32 [32, 128], P(('grp', 'sp')), parts along dimension 0, may hold values from 0.5 to 1
- nb_index: int32 [4, 4096], P(None, ('grp', 'sp')), parts along dimension 1, may hold values from 0 to 767, as said below
- nb_angle: float32 [4, 4096], P(None, ('grp', 'sp')), parts along dimension 1, may hold values from -3.140625 to 3.140625
- nb_coef: float32 [4, 4096], P(None, ('grp', 'sp')), parts along dimension 1, may hold values from 0.05 to 0.35
- halo_list: int32 [2, 1024], P(None, ('grp', 'sp')), parts along dimension 1, may hold values from 0 to 511
- w_in: bfloat16 [36, 36, 256], P('fr', 'dr'), may hold values from -0.15625 to 0.15625
- w_out: bfloat16 [256, 36, 36], P(None, 'fr', 'dr'), may hold values from -0.375 to 0.375
- g2m_index: int32 [4, 8, 4, 128], P(None, ('grp', 'sp')), parts along dimension 1, may hold values from 0 to 511
- g2m_weight: float32 [4, 8, 4, 128], P(None, ('grp', 'sp')), parts along dimension 1, may hold values from 0.05 to 0.3
- g2m_count: int32 [8, 4], P(('grp', 'sp')), parts along dimension 0, may hold values from 0 to 128, as said below
- g2m_target: int32 [8, 4, 128], P(('grp', 'sp')), parts along dimension 0, may hold values from 0 to 511
- m2g_index: int32 [3, 8, 4, 128], P(None, ('grp', 'sp')), parts along dimension 1, may hold values from 0 to 511
- m2g_weight: float32 [3, 8, 4, 128], P(None, ('grp', 'sp')), parts along dimension 1, may hold values from 0.05 to 0.4
- m2g_count: int32 [8, 4], P(('grp', 'sp')), parts along dimension 0, may hold values from 0 to 128, as said below
- m2g_target: int32 [8, 4, 128], P(('grp', 'sp')), parts along dimension 0, may hold values from 0 to 511
Outputs:
- grid_out: float32 [36, 36, 32, 128], P('fr', 'dr', ('grp', 'sp')), parts along dimension 2
- mesh_out: float32 [36, 36, 4096], P('fr', 'dr', ('grp', 'sp')), parts along dimension 2
The draws below stay inside these ranges and needn't reach their ends.
There are 2 independent parts, one for each index of `grp`. The reference program is written for one: setup_inputs(seed, part) draws one part's arguments, and reference() takes and returns one part's arrays. A program takes and returns all parts, laid end to end along the dimension named above; an argument that names none is the same for every part. Nothing has to cross between parts.
Inputs may be any that keep to these rules, and one draw needn't show every extreme that they name: `nb_index`: each entry is a position in its sp index's extended list: below 512 an own node, 512 + i the i-th node from the next lower index, 640 + i the i-th from the next higher index. `g2m_count`: every sender has some receiver with all 128 slots live. `m2g_count`: every sender has some receiver with all 128 slots live.
All inputs are finite; a program needn't handle non-finite values. No bound on the sum of `grid_sea` on one device may be relied on, other than what follows from the above.
Results may differ from the reference program's by a relative error of at most 0.0015.
Values may be sent and summed in bfloat16 or wider, within the bound.
No kernel may reach another device: no remote copies, remote signals or barrier semaphores. Data moves between devices by JAX's collectives and lax.ppermute only.
A program may use at most 64 MiB of HBM per device.

```python
import math
import jax
import jax.numpy as jnp

NF = 36
ND = 36
HID = 256
GX = 4
GY = 128
M = 512
B = 128
K = 4
CAP = 128
NSUB = 2
NX = 16
NM = 2048
NB = 512
N_SP = 4


def pair_loads(key):
    base_key, scale_key = jax.random.split(key)
    base_load = jax.random.randint(base_key, (N_SP, N_SP), 0, CAP // 2 + 1)
    factor = jax.random.randint(scale_key, (N_SP, 1), 1, 5)
    capped = jnp.minimum(base_load * factor, CAP)
    row_ids = jnp.arange(N_SP)[:, None]
    column_ids = jnp.arange(N_SP)[None, :]
    return jnp.where(column_ids == (row_ids + 1) % N_SP, CAP, capped).astype(jnp.int32)


def draw_g2m_count(key, part):
    key = jax.random.fold_in(key, 21)
    return pair_loads(key)


def draw_m2g_count(key, part):
    key = jax.random.fold_in(key, 37)
    return pair_loads(key)


def draw_nb_index(key, part):
    key = jax.random.fold_in(key, 11)
    picks = jax.random.randint(key, (K, NM), 0, M + 2 * B)
    return picks.at[0, 0].set(M + 2 * B - 1).astype(jnp.int32)


def plant(drawn, key, low, largest):
    longest = drawn.shape.index(max(drawn.shape))
    spots = []
    for shift in (0, 1):
        where = [jax.random.randint(jax.random.fold_in(key, axis), (), 0, length) for axis, length in enumerate(drawn.shape)]
        where[longest] = (where[longest] + shift) % drawn.shape[longest]
        spots.append(tuple(where))
    return drawn.at[spots[0]].set(low).at[spots[1]].set(largest)


def block_levels(rng, dims, pieces, low, high):
    loudness = 1.0
    for position, shards_of in pieces:
        draws = jax.random.uniform(jax.random.fold_in(jax.random.fold_in(rng, 6), position), (shards_of,), jnp.float32, low / len(pieces), high / len(pieces))
        loudness = loudness * jnp.repeat(jnp.exp(draws), dims[position] // shards_of).reshape((-1,) + (1,) * (len(dims) - 1 - position))
    return loudness


def centred(rng, extent, width, reach, cuts=(), dtype=jnp.bfloat16):
    values = width * jax.random.normal(rng, extent, jnp.float32)
    if cuts:
        values = values * block_levels(rng, extent, cuts, -0.22, 0.18)
    return jnp.clip(values, -reach, reach).astype(dtype)


def setup_inputs(seed: int = 0, part: int = 0) -> dict:
    streams_of = jax.random.split(jax.random.key(seed), 19)
    part_keys = jax.random.split(jax.random.fold_in(streams_of[18], part), 19)
    return {
        "grid_spec": jnp.clip(2.0 * jax.random.uniform(part_keys[0], (NF, ND, NX, GY), jnp.float32) ** block_levels(part_keys[0], (NF, ND, NX, GY), ((0, 2), (1, 2), (2, 4)), -0.2, 0.2), 0.0, 2.0),
        "mesh_spec": jnp.clip(2.0 * jax.random.uniform(part_keys[1], (NF, ND, NM), jnp.float32) ** block_levels(part_keys[1], (NF, ND, NM), ((0, 2), (1, 2), (2, 4)), -0.2, 0.2), 0.0, 2.0),
        "grid_sea": plant((jax.random.randint(part_keys[2], (NX, GY), 0, 10) < 9).astype(jnp.int32), jax.random.fold_in(part_keys[2], 1), 0, 1),
        "grid_speed": jnp.clip(0.5 + 0.5 * jax.random.uniform(part_keys[3], (NX, GY), jnp.float32) ** block_levels(part_keys[3], (NX, GY), ((0, 4),), -0.2, 0.2), 0.5, 1.0),
        "nb_index": draw_nb_index(jax.random.fold_in(jax.random.fold_in(streams_of[18], part), 71), part),
        "nb_angle": jnp.clip(jax.random.uniform(part_keys[5], (K, NM), jnp.float32, -3.140625, 3.140625), -3.140625, 3.140625),
        "nb_coef": jnp.clip(jnp.exp(math.log(0.35) - 1.9459101 * jax.random.uniform(part_keys[6], (K, NM), jnp.float32) ** block_levels(part_keys[6], (K, NM), ((1, 4),), -0.2, 0.2)), 0.05, 0.35),
        "halo_list": plant(jax.random.randint(part_keys[7], (2, NB), 0, M), jax.random.fold_in(part_keys[7], 1), 0, M - 1).astype(jnp.int32),
        "w_in": centred(streams_of[8], (NF, ND, HID), (NF * ND) ** -0.5, 0.15625, ((0, 2), (1, 2))),
        "w_out": centred(streams_of[9], (HID, NF, ND), HID ** -0.5, 0.375, ((1, 2), (2, 2))),
        "g2m_index": plant(jax.random.randint(part_keys[10], (4, N_SP, N_SP, CAP), 0, GX * GY), jax.random.fold_in(part_keys[10], 1), 0, (GX * GY) - 1).astype(jnp.int32),
        "g2m_weight": jnp.clip(0.05 + 0.25 * jax.random.uniform(part_keys[11], (4, N_SP, N_SP, CAP), jnp.float32) ** block_levels(part_keys[11], (4, N_SP, N_SP, CAP), ((1, 4),), -0.2, 0.2), 0.05, 0.3),
        "g2m_count": draw_g2m_count(jax.random.fold_in(jax.random.fold_in(streams_of[18], part), 71), part),
        "g2m_target": plant(jax.random.randint(part_keys[13], (N_SP, N_SP, CAP), 0, M), jax.random.fold_in(part_keys[13], 1), 0, M - 1).astype(jnp.int32),
        "m2g_index": plant(jax.random.randint(part_keys[14], (3, N_SP, N_SP, CAP), 0, M), jax.random.fold_in(part_keys[14], 1), 0, M - 1).astype(jnp.int32),
        "m2g_weight": jnp.clip(0.05 + 0.35 * jax.random.uniform(part_keys[15], (3, N_SP, N_SP, CAP), jnp.float32) ** block_levels(part_keys[15], (3, N_SP, N_SP, CAP), ((1, 4),), -0.2, 0.2), 0.05, 0.4),
        "m2g_count": draw_m2g_count(jax.random.fold_in(jax.random.fold_in(streams_of[18], part), 71), part),
        "m2g_target": plant(jax.random.randint(part_keys[17], (N_SP, N_SP, CAP), 0, GX * GY), jax.random.fold_in(part_keys[17], 1), 0, (GX * GY) - 1).astype(jnp.int32),
    }


DT_STEP = 0.1
BLEND_RATE = 0.5


def wave_speeds():
    freq_values = jnp.arange(NF).astype(jnp.float32)
    group_speed = 0.7 * jnp.power(1.1, -freq_values)
    headings = 2.0 * jnp.pi * (jnp.arange(ND).astype(jnp.float32) + 0.5) / ND
    return group_speed, headings


def upwind(field, lower_x, upper_x, sea_mask, grid_speed, group_speed, headings):
    along_x = group_speed[:, None, None, None] * jnp.cos(headings)[None, :, None, None] * grid_speed[None, None]
    along_y = group_speed[:, None, None, None] * jnp.sin(headings)[None, :, None, None] * grid_speed[None, None]
    padded_y = jnp.pad(field, ((0, 0), (0, 0), (0, 0), (1, 1)))
    lower_y = padded_y[:, :, :, :-2]
    upper_y = padded_y[:, :, :, 2:]
    moved = field - jnp.maximum(along_x, 0.0) * (field - lower_x) - jnp.maximum(-along_x, 0.0) * (field - upper_x)
    moved = moved - jnp.maximum(along_y, 0.0) * (field - lower_y) - jnp.maximum(-along_y, 0.0) * (field - upper_y)
    return moved * sea_mask


def grid_move(field, sea_mask, grid_speed, group_speed, headings):
    padded_x = jnp.pad(field, ((0, 0), (0, 0), (1, 1), (0, 0)))
    return upwind(field, padded_x[:, :, :-2], padded_x[:, :, 2:], sea_mask, grid_speed, group_speed, headings)


def mesh_move(mesh, nb_index, nb_angle, nb_coef, halo_list, group_speed, headings):
    freq_count, dir_count = mesh.shape[0], mesh.shape[1]
    node_blocks = mesh.reshape(freq_count, dir_count, N_SP, M)
    lists = halo_list.reshape(2, N_SP, B)
    to_lower = jnp.take_along_axis(node_blocks, jnp.broadcast_to(lists[0], (freq_count, dir_count, N_SP, B)), axis=3)
    to_upper = jnp.take_along_axis(node_blocks, jnp.broadcast_to(lists[1], (freq_count, dir_count, N_SP, B)), axis=3)
    nothing = jnp.zeros((freq_count, dir_count, 1, B), jnp.float32)
    from_lower = jnp.concatenate([nothing, to_upper[:, :, :-1]], axis=2)
    from_upper = jnp.concatenate([to_lower[:, :, 1:], nothing], axis=2)
    extended = jnp.concatenate([node_blocks, from_lower, from_upper], axis=3)
    positions = nb_index.reshape(K, N_SP, M)
    bearings = nb_angle.reshape(K, N_SP, M)
    coefficients = nb_coef.reshape(K, N_SP, M)
    result = node_blocks
    for k in range(K):
        nearby = jnp.take_along_axis(extended, jnp.broadcast_to(positions[k], (freq_count, dir_count, N_SP, M)), axis=3)
        weight = group_speed[:, None, None, None] * coefficients[k] * jnp.maximum(-jnp.cos(headings[:, None, None] - bearings[k]), 0.0)
        result = result + weight * (nearby - node_blocks)
    return result.reshape(freq_count, dir_count, N_SP * M)


def transfer_term(field, w_in, w_out):
    freq_count, dir_count, point_count = field.shape
    features = field.astype(jnp.bfloat16).reshape(freq_count * dir_count, point_count)
    first = w_in.reshape(freq_count * dir_count, HID).T
    hidden = jax.nn.silu(jnp.dot(first, features, preferred_element_type=jnp.float32)).astype(jnp.bfloat16)
    second = w_out.reshape(HID, freq_count * dir_count).T
    output = jnp.dot(second, hidden, preferred_element_type=jnp.float32).astype(jnp.bfloat16)
    return output.reshape(freq_count, dir_count, point_count)


def pack_slots(source, index, weight, count):
    freq_count, dir_count = source.shape[0], source.shape[1]
    live = (jnp.arange(CAP)[None, None, :] < count[:, :, None]).astype(jnp.float32)
    scaled = weight * live[None]
    values = jnp.zeros((freq_count, dir_count, N_SP, N_SP, CAP), jnp.float32)
    for j in range(index.shape[0]):
        flat_index = jnp.broadcast_to(index[j].reshape(N_SP, N_SP * CAP), (freq_count, dir_count, N_SP, N_SP * CAP))
        picked = jnp.take_along_axis(source, flat_index, axis=3).reshape(freq_count, dir_count, N_SP, N_SP, CAP)
        values = values + scaled[j] * picked
    return values, jnp.sum(scaled, axis=0)


def land_slots(values, weight_sums, target, state):
    freq_count, dir_count = values.shape[0], values.shape[1]
    length = state.shape[3]
    incoming = jnp.transpose(values, (0, 1, 3, 2, 4)).reshape(freq_count, dir_count, N_SP, N_SP * CAP)
    arriving = jnp.transpose(weight_sums, (1, 0, 2)).reshape(N_SP, N_SP * CAP)
    places = target.reshape(N_SP, N_SP * CAP)

    def land_block(slot_values, slot_weights, spots, block):
        gathered_sum = jnp.zeros((freq_count, dir_count, length), jnp.float32).at[:, :, spots].add(slot_values)
        coverage = jnp.zeros((length,), jnp.float32).at[spots].add(slot_weights)
        return block + BLEND_RATE * (gathered_sum - coverage * block) / (1.0 + coverage)

    return jax.vmap(land_block, in_axes=(2, 0, 0, 2), out_axes=2)(incoming, arriving, places, state)


def reference(grid_spec, mesh_spec, grid_sea, grid_speed, nb_index, nb_angle, nb_coef, halo_list, w_in, w_out, g2m_index, g2m_weight, g2m_count, g2m_target, m2g_index, m2g_weight, m2g_count, m2g_target):
    group_speed, headings = wave_speeds()
    sea_mask = grid_sea.astype(jnp.float32)
    grid = grid_spec
    mesh = mesh_spec
    for substep in range(NSUB):
        grid = grid_move(grid, sea_mask, grid_speed, group_speed, headings)
        mesh = mesh_move(mesh, nb_index, nb_angle, nb_coef, halo_list, group_speed, headings)
        grid_source = transfer_term(grid.reshape(NF, ND, NX * GY), w_in, w_out)
        mesh_source = transfer_term(mesh, w_in, w_out)
        grid = grid + DT_STEP * grid_source.astype(jnp.float32).reshape(NF, ND, NX, GY)
        mesh = mesh + DT_STEP * mesh_source.astype(jnp.float32)
    grid_blocks = grid.reshape(NF, ND, N_SP, GX * GY)
    mesh_blocks = mesh.reshape(NF, ND, N_SP, M)
    grid_values, grid_sums = pack_slots(grid_blocks, g2m_index, g2m_weight, g2m_count)
    mesh_values, mesh_sums = pack_slots(mesh_blocks, m2g_index, m2g_weight, m2g_count)
    mesh_out = land_slots(grid_values, grid_sums, g2m_target, mesh_blocks).reshape(NF, ND, NM)
    grid_out = land_slots(mesh_values, mesh_sums, m2g_target, grid_blocks).reshape(NF, ND, NX, GY) * sea_mask
    return grid_out, mesh_out
```

```python
import functools

import jax
import jax.numpy as jnp
import numpy as np
from jax import lax
from jax.experimental import pallas as pl
from jax.experimental.pallas import tpu as pltpu
from jax.sharding import PartitionSpec as P

NSUB = 2
DT_STEP = 0.1
BLEND_RATE = 0.5
F32 = jnp.float32
BF16 = jnp.bfloat16
CHUNK = 16


def kernel_call(body, outs, scratch=(), flops=0, nbytes=4 << 20):
    spec = pl.BlockSpec(memory_space=pltpu.VMEM)

    def run(*args):
        return pl.pallas_call(
            body,
            out_shape=[jax.ShapeDtypeStruct(s, t) for s, t in outs],
            in_specs=[spec] * len(args),
            out_specs=[spec] * len(outs),
            scratch_shapes=[pltpu.VMEM(s, t) for s, t in scratch],
            compiler_params=pltpu.CompilerParams(vmem_limit_bytes=24 << 20),
            cost_estimate=pl.CostEstimate(flops=flops, bytes_accessed=nbytes, transcendentals=0),
        )(*args)

    return run


def dot(a, b):
    return jnp.dot(a, b, preferred_element_type=F32)


def one_hot(row, length):
    spots = lax.broadcasted_iota(jnp.int32, (length, row.shape[1]), 0)
    return jnp.where(spots == row, 1.0, 0.0).astype(BF16)


def shift(array, axis, by):
    size = lax.axis_size(axis)
    return lax.ppermute(array, axis, [(i, i + by) for i in range(size) if 0 <= i + by < size])


def peer_pairs(size, step):
    if size & (size - 1) == 0:
        return [(i, i ^ step) for i in range(size)]
    return [(i, (step - i) % size) for i in range(size)]


def peer_of(me, size, step):
    if size & (size - 1) == 0:
        return lax.bitwise_xor(me, step)
    return lax.rem(step - me + size, size)


def messages(state_ref, halo_ref, up_ref, down_ref, grid_points, cols):
    nodes = state_ref.shape[1] - grid_points
    listed = halo_ref.shape[1]
    mesh = state_ref[:, grid_points:].astype(BF16)
    for msg, row, which in ((up_ref, grid_points - cols, 1), (down_ref, 0, 0)):
        msg[:, :cols] = state_ref[:, row : row + cols].astype(BF16)
        picked = dot(mesh, one_hot(halo_ref[which : which + 1, :], nodes))
        msg[:, cols : cols + listed] = picked.astype(BF16)


def begin_kernel(grid_ref, mesh_ref, halo_ref, state_ref, up_ref, down_ref, *, rows, cols):
    freqs, dirs, _ = mesh_ref.shape
    bands = freqs * dirs
    gp = rows * cols
    padded = state_ref.shape[0]
    state_ref[bands:, :] = jnp.zeros((padded - bands, state_ref.shape[1]), F32)
    for x in range(rows):
        state_ref[:bands, x * cols : (x + 1) * cols] = grid_ref[pl.ds(x, bands, stride=rows), :]
    for f in range(freqs):
        state_ref[f * dirs : (f + 1) * dirs, gp:] = mesh_ref[f]
    messages(state_ref, halo_ref, up_ref, down_ref, gp, cols)


def hot_kernel(index_ref, hot_ref):
    for k in range(index_ref.shape[0]):
        hot_ref[k] = one_hot(index_ref[k : k + 1, :], hot_ref.shape[1])


def move_kernel(
    state_ref, lower_ref, upper_ref, hot_ref, pq_ref, band_ref, sea_ref, speed_ref, win_ref,
    moved_ref, keep_ref, send_ref, ext_ref, near_ref, feat_ref,
):
    padded, points = state_ref.shape
    rows, cols = sea_ref.shape
    gp = rows * cols
    nodes = points - gp
    neighbours = hot_ref.shape[0]
    listed = lower_ref.shape[1] - cols
    ext_ref[:, :nodes] = state_ref[:, gp:].astype(BF16)
    ext_ref[:, nodes : nodes + listed] = lower_ref[:, cols:]
    ext_ref[:, nodes + listed :] = upper_ref[:, cols:]
    for k in range(neighbours):
        near_ref[k] = dot(ext_ref[...], hot_ref[k])
    sea = sea_ref[...].astype(F32)
    lane = lax.broadcasted_iota(jnp.int32, (CHUNK, cols), 1)
    for c in range(padded // CHUNK):
        here = slice(c * CHUNK, (c + 1) * CHUNK)
        cx = band_ref[here, 0:1]
        cy = band_ref[here, 1:2]
        for x in range(rows):
            g = state_ref[here, x * cols : (x + 1) * cols]
            if x == 0:
                low = lower_ref[here, :cols].astype(F32)
            else:
                low = state_ref[here, (x - 1) * cols : x * cols]
            if x == rows - 1:
                high = upper_ref[here, :cols].astype(F32)
            else:
                high = state_ref[here, (x + 1) * cols : (x + 2) * cols]
            west = jnp.where(lane == 0, 0.0, pltpu.roll(g, 1, 1))
            east = jnp.where(lane == cols - 1, 0.0, pltpu.roll(g, cols - 1, 1))
            out = g - jnp.abs(cx) * speed_ref[x : x + 1, :] * (g - jnp.where(cx > 0, low, high))
            out = out - jnp.abs(cy) * speed_ref[x : x + 1, :] * (g - jnp.where(cy > 0, west, east))
            out = out * sea[x : x + 1, :]
            moved_ref[here, x * cols : (x + 1) * cols] = out
            feat_ref[here, x * cols : (x + 1) * cols] = out.astype(BF16)
        e = state_ref[here, gp:]
        out = e
        for k in range(neighbours):
            w = cx * pq_ref[k : k + 1, :] + cy * pq_ref[neighbours + k : neighbours + k + 1, :]
            out = out + jnp.maximum(w, 0.0) * (near_ref[k, here, :] - e)
        moved_ref[here, gp:] = out
        feat_ref[here, gp:] = out.astype(BF16)
    half = keep_ref.shape[0]
    keep_ref[...] = dot(win_ref[:half, :], feat_ref[...])
    send_ref[...] = dot(win_ref[half:, :], feat_ref[...]).astype(BF16)


def add_transfer(moved_ref, mine_ref, other_ref, wout_ref, hid_ref, state_ref):
    half = mine_ref.shape[0]
    hid_ref[:half, :] = mine_ref[...]
    hid_ref[half:, :] = other_ref[...]
    state_ref[...] = moved_ref[...] + DT_STEP * dot(wout_ref[...], hid_ref[...])


def next_kernel(
    moved_ref, mine_ref, other_ref, wout_ref, halo_ref, state_ref, up_ref, down_ref, hid_ref,
    *, grid_points, cols,
):
    add_transfer(moved_ref, mine_ref, other_ref, wout_ref, hid_ref, state_ref)
    messages(state_ref, halo_ref, up_ref, down_ref, grid_points, cols)


def slots_kernel(
    gi_ref, gw_ref, gc_ref, gt_ref, mi_ref, mw_ref, mc_ref, mt_ref,
    gmix_ref, mmix_ref, sums_ref, gland_ref, mland_ref,
):
    me = lax.axis_index("sp")
    _, _, peers, cap = gi_ref.shape
    groups = (
        (gi_ref, gw_ref, gc_ref, gt_ref, gmix_ref, gland_ref, 0),
        (mi_ref, mw_ref, mc_ref, mt_ref, mmix_ref, mland_ref, 1),
    )
    for index_ref, weight_ref, count_ref, target_ref, mix_ref, land_ref, kind in groups:
        length = mix_ref.shape[0]
        spots = lax.broadcasted_iota(jnp.int32, (length, cap), 0)
        slot = lax.broadcasted_iota(jnp.int32, (1, cap), 1)
        for p in range(peers):
            peer = peer_of(me, peers, p)
            count = jnp.sum(
                jnp.where(
                    lax.broadcasted_iota(jnp.int32, (1, peers), 1) == peer, count_ref[...], 0
                ),
                axis=1,
                keepdims=True,
            )
            live = jnp.where(slot < count, 1.0, 0.0)
            mix = jnp.zeros((length, cap), F32)
            total = jnp.zeros((1, cap), F32)
            for j in range(index_ref.shape[0]):
                scaled = weight_ref[j, 0, pl.ds(peer, 1), :] * live
                mix = mix + jnp.where(spots == index_ref[j, 0, pl.ds(peer, 1), :], scaled, 0.0)
                total = total + scaled
            mix_ref[:, p * cap : (p + 1) * cap] = mix.astype(BF16)
            sums_ref[kind : kind + 1, p * cap : (p + 1) * cap] = total
            land_ref[:, p * cap : (p + 1) * cap] = one_hot(
                target_ref[0, pl.ds(peer, 1), :], land_ref.shape[0]
            )


def mix_kernel(
    moved_ref, mine_ref, other_ref, wout_ref, gmix_ref, mmix_ref, sums_ref, state_ref, *rest,
    bands,
):
    out_refs, hid_ref = rest[:-1], rest[-1]
    add_transfer(moved_ref, mine_ref, other_ref, wout_ref, hid_ref, state_ref)
    gp = gmix_ref.shape[0]
    peers = len(out_refs)
    cap = gmix_ref.shape[1] // peers
    grid = state_ref[:, :gp].astype(BF16)
    mesh = state_ref[:, gp:].astype(BF16)
    row = lax.broadcasted_iota(jnp.int32, (state_ref.shape[0], cap), 0)
    for p in range(peers):
        cut = slice(p * cap, (p + 1) * cap)
        for kind, source, mix_ref in ((0, grid, gmix_ref), (1, mesh, mmix_ref)):
            value = dot(source, mix_ref[:, cut])
            value = jnp.where(row == bands, sums_ref[kind : kind + 1, cut], value)
            out_refs[p][:, kind * cap : (kind + 1) * cap] = value.astype(BF16)


def land(values, land_ref):
    return lax.dot_general(
        values, land_ref[...], (((1,), (1,)), ((), ())), preferred_element_type=F32
    )


def end_kernel(state_ref, gland_ref, mland_ref, sea_ref, *rest, bands):
    got_refs, (grid_ref, mesh_ref, values_ref, sum_ref) = rest[:-4], rest[-4:]
    rows, cols = sea_ref.shape
    gp = rows * cols
    freqs, dirs, _ = mesh_ref.shape
    cap = got_refs[0].shape[1] // 2
    for kind in (0, 1):
        for p, got in enumerate(got_refs):
            values_ref[kind, :, p * cap : (p + 1) * cap] = got[:, kind * cap : (kind + 1) * cap]
    sum_ref[:, :gp] = land(values_ref[1], mland_ref)
    sum_ref[:, gp:] = land(values_ref[0], gland_ref)
    cover = sum_ref[bands : bands + 1, :]
    rate = BLEND_RATE / (1.0 + cover)
    sea = sea_ref[...].astype(F32)
    for x in range(rows):
        cut = slice(x * cols, (x + 1) * cols)
        g = state_ref[:bands, cut]
        out = g + rate[:, cut] * (sum_ref[:bands, cut] - cover[:, cut] * g)
        grid_ref[pl.ds(x, bands, stride=rows), :] = out * sea[x : x + 1, :]
    for f in range(freqs):
        here = slice(f * dirs, (f + 1) * dirs)
        e = state_ref[here, gp:]
        mesh_ref[f] = e + rate[:, gp:] * (sum_ref[here, gp:] - cover[:, gp:] * e)


def band_table(freqs, dirs, n_fr, n_dr, padded):
    speed = (0.7 * np.power(np.float32(1.1), -np.arange(freqs * n_fr, dtype=np.float32))).astype(np.float32)
    total = dirs * n_dr
    heading = (2.0 * np.pi * (np.arange(total, dtype=np.float64) + 0.5) / total)
    table = np.zeros((n_fr, n_dr, padded, 2), np.float32)
    for i in range(n_fr):
        for j in range(n_dr):
            s = speed[i * freqs : (i + 1) * freqs, None]
            h = heading[None, j * dirs : (j + 1) * dirs]
            table[i, j, : freqs * dirs, 0] = (s * np.cos(h)).reshape(-1)
            table[i, j, : freqs * dirs, 1] = (s * np.sin(h)).reshape(-1)
    return table


def reduce_hidden(keep, send):
    got = lax.ppermute(send, "dr", [(0, 1), (1, 0)])
    total = keep + got.astype(F32)
    size = lax.axis_size("fr")
    step = 1
    while step < size:
        total = total + lax.ppermute(
            total.astype(BF16), "fr", [(i, i ^ step) for i in range(size)]
        ).astype(F32)
        step *= 2
    hidden = (total / (1.0 + jnp.exp(-total))).astype(BF16)
    return hidden, lax.ppermute(hidden, "dr", [(0, 1), (1, 0)])


def per_device(
    grid_spec, mesh_spec, grid_sea, grid_speed, nb_index, nb_angle, nb_coef, halo_list, w_in, w_out,
    g2m_index, g2m_weight, g2m_count, g2m_target, m2g_index, m2g_weight, m2g_count, m2g_target,
):
    freqs, dirs, rows, cols = grid_spec.shape
    nodes = mesh_spec.shape[2]
    listed = halo_list.shape[1]
    hid = w_in.shape[2]
    half = hid // 2
    bands = freqs * dirs
    padded = (bands // CHUNK + 1) * CHUNK
    gp = rows * cols
    points = gp + nodes
    neighbours = nb_index.shape[0]
    peers, cap = g2m_index.shape[2:]
    n_fr, n_dr = lax.axis_size("fr"), lax.axis_size("dr")
    dr = lax.axis_index("dr")

    table = jnp.asarray(band_table(freqs, dirs, n_fr, n_dr, padded))
    band = table[lax.axis_index("fr"), dr]
    pq = jnp.concatenate([-nb_coef * jnp.cos(nb_angle), -nb_coef * jnp.sin(nb_angle)], axis=0)
    pad = ((0, padded - bands), (0, 0))
    win = jnp.pad(w_in.reshape(bands, hid), pad).T
    wout = jnp.pad(w_out.reshape(hid, bands).T, pad)
    win = jnp.where(dr == 0, win, jnp.roll(win, half, axis=0))
    wout = jnp.where(dr == 0, wout, jnp.roll(wout, half, axis=1))

    message = ((padded, cols + listed), BF16)
    state_shape = ((padded, points), F32)
    hid_scratch = ((hid, points), BF16)
    state, up, down = kernel_call(
        functools.partial(begin_kernel, rows=rows, cols=cols),
        [state_shape, message, message],
        flops=2 * padded * nodes * 2 * listed,
    )(grid_spec.reshape(bands * rows, cols), mesh_spec, halo_list)
    (hot,) = kernel_call(hot_kernel, [((neighbours, nodes + 2 * listed, nodes), BF16)])(nb_index)
    gmix, mmix, sums, gland, mland = kernel_call(
        slots_kernel,
        [
            ((gp, peers * cap), BF16),
            ((nodes, peers * cap), BF16),
            ((2, peers * cap), F32),
            ((nodes, peers * cap), BF16),
            ((gp, peers * cap), BF16),
        ],
    )(g2m_index, g2m_weight, g2m_count, g2m_target, m2g_index, m2g_weight, m2g_count, m2g_target)

    for substep in range(NSUB):
        lower = shift(up, "sp", 1)
        upper = shift(down, "sp", -1)
        moved, keep, send = kernel_call(
            move_kernel,
            [state_shape, ((half, points), F32), ((half, points), BF16)],
            [
                ((padded, nodes + 2 * listed), BF16),
                ((neighbours, padded, nodes), F32),
                ((padded, points), BF16),
            ],
            flops=2 * padded * (neighbours * nodes * (nodes + 2 * listed) + hid * points),
        )(state, lower, upper, hot, pq, band, grid_sea, grid_speed, win)
        mine, other = reduce_hidden(keep, send)
        if substep < NSUB - 1:
            state, up, down = kernel_call(
                functools.partial(next_kernel, grid_points=gp, cols=cols),
                [state_shape, message, message],
                [hid_scratch],
                flops=2 * padded * hid * points,
            )(moved, mine, other, wout, halo_list)

    state, *values = kernel_call(
        functools.partial(mix_kernel, bands=bands),
        [state_shape] + [((padded, 2 * cap), BF16)] * peers,
        [hid_scratch],
        flops=2 * padded * (hid * points + points * peers * cap),
    )(moved, mine, other, wout, gmix, mmix, sums)
    got = [
        lax.ppermute(v, "sp", peer_pairs(peers, p)) if p else v for p, v in enumerate(values)
    ]
    if peers & (peers - 1):
        got[0] = lax.ppermute(values[0], "sp", peer_pairs(peers, 0))
    grid_out, mesh_out = kernel_call(
        functools.partial(end_kernel, bands=bands),
        [((bands * rows, cols), F32), ((freqs, dirs, nodes), F32)],
        [((2, padded, peers * cap), BF16), state_shape],
        flops=2 * padded * points * peers * cap,
    )(state, gland, mland, grid_sea, *got)
    return grid_out.reshape(grid_spec.shape), mesh_out


def solution(mesh):
    return jax.shard_map(
        per_device,
        mesh=mesh,
        in_specs=(
            P("fr", "dr", ("grp", "sp"), None),
            P("fr", "dr", ("grp", "sp")),
            P(("grp", "sp"), None),
            P(("grp", "sp"), None),
            P(None, ("grp", "sp")),
            P(None, ("grp", "sp")),
            P(None, ("grp", "sp")),
            P(None, ("grp", "sp")),
            P("fr", "dr", None),
            P(None, "fr", "dr"),
            P(None, ("grp", "sp"), None, None),
            P(None, ("grp", "sp"), None, None),
            P(("grp", "sp"), None),
            P(("grp", "sp"), None, None),
            P(None, ("grp", "sp"), None, None),
            P(None, ("grp", "sp"), None, None),
            P(("grp", "sp"), None),
            P(("grp", "sp"), None, None),
        ),
        out_specs=(P("fr", "dr", ("grp", "sp"), None), P("fr", "dr", ("grp", "sp"))),
        check_vma=False,
    )
```

```python
import functools

import jax
import jax.numpy as jnp
import numpy as np
from jax import lax
from jax.experimental import pallas as pl
from jax.experimental.pallas import tpu as pltpu
from jax.sharding import PartitionSpec as P

NSUB = 2
DT_STEP = 0.1
BLEND_RATE = 0.5
F32 = jnp.float32
BF16 = jnp.bfloat16
CHUNK = 16


VMEM = pltpu.MemorySpace.VMEM
HBM = pltpu.MemorySpace.HBM


def kernel_call(body, outs, scratch=(), flops=0, nbytes=2 << 20, spaces=None):
    def run(*args):
        where = spaces or [VMEM] * len(args)
        return pl.pallas_call(
            body,
            out_shape=[jax.ShapeDtypeStruct(s, t) for s, t in outs],
            in_specs=[pl.BlockSpec(memory_space=space) for space in where],
            out_specs=[pl.BlockSpec(memory_space=VMEM)] * len(outs),
            scratch_shapes=[s if hasattr(s, "dtype") else pltpu.VMEM(*s) for s in scratch],
            compiler_params=pltpu.CompilerParams(vmem_limit_bytes=16 << 20),
            cost_estimate=pl.CostEstimate(flops=flops, bytes_accessed=nbytes, transcendentals=0),
        )(*args)

    return run


def dot(a, b):
    return jnp.dot(a, b, preferred_element_type=F32)


def one_hot(row, length):
    spots = lax.broadcasted_iota(jnp.int32, (length, row.shape[1]), 0)
    return jnp.where(spots == row, 1.0, 0.0).astype(BF16)


def pair_swap(array, axis, first):
    size = lax.axis_size(axis)
    pairs = [(i, i + 1) for i in range(first, size - 1, 2)]
    return lax.ppermute(array, axis, pairs + [(j, i) for i, j in pairs])


def peer_pairs(size, step):
    if size & (size - 1) == 0:
        return [(i, i ^ step) for i in range(size)]
    return [(i, (step - i) % size) for i in range(size)]


def peer_of(me, size, step):
    if size & (size - 1) == 0:
        return lax.bitwise_xor(me, step)
    return lax.rem(step - me + size, size)


def on_even():
    return lax.rem(lax.axis_index("sp"), 2) == 0


def messages(mesh, low_row, high_row, halo_ref, even_ref, odd_ref):
    even = on_even()
    nodes = mesh.shape[1]
    cols = low_row.shape[1]
    to_lower = dot(mesh, one_hot(halo_ref[0:1, :], nodes)).astype(BF16)
    to_upper = dot(mesh, one_hot(halo_ref[1:2, :], nodes)).astype(BF16)
    even_ref[:, :cols] = jnp.where(even, high_row, low_row)
    odd_ref[:, :cols] = jnp.where(even, low_row, high_row)
    even_ref[:, cols:] = jnp.where(even, to_upper, to_lower)
    odd_ref[:, cols:] = jnp.where(even, to_lower, to_upper)


def pack_rows(source_ref, packed_ref, at):
    freqs, dirs, width = source_ref.shape
    for f in range(freqs):
        packed_ref[f * dirs : (f + 1) * dirs, at : at + width] = source_ref[f].astype(F32)
    packed_ref[freqs * dirs :, at : at + width] = jnp.zeros(
        (packed_ref.shape[0] - freqs * dirs, width), F32
    )


def begin_kernel(
    grid_hbm, mesh_hbm, halo_hbm, even_ref, odd_ref, grid_ref, mesh_ref, halo_ref, packed_ref, sem,
    *, rows,
):
    copies = [
        pltpu.make_async_copy(halo_hbm, halo_ref, sem.at[0]),
        pltpu.make_async_copy(mesh_hbm, mesh_ref, sem.at[1]),
        pltpu.make_async_copy(grid_hbm, grid_ref, sem.at[2]),
    ]
    for copy in copies:
        copy.start()
    bands = grid_ref.shape[0] // rows
    blank = jnp.zeros((packed_ref.shape[0] - bands, grid_ref.shape[1]), F32)
    copies[0].wait()
    copies[1].wait()
    pack_rows(mesh_ref, packed_ref, 0)
    copies[2].wait()
    low = jnp.concatenate([grid_ref[pl.ds(0, bands, stride=rows), :], blank], axis=0)
    high = jnp.concatenate([grid_ref[pl.ds(rows - 1, bands, stride=rows), :], blank], axis=0)
    messages(
        packed_ref[...].astype(BF16), low.astype(BF16), high.astype(BF16), halo_ref, even_ref, odd_ref
    )


def own_grid(state_ref, band_ref, sea_ref, speed_ref, part_ref):
    rows, cols = sea_ref.shape
    sea = sea_ref[...].astype(F32)
    lane = lax.broadcasted_iota(jnp.int32, (CHUNK, cols), 1)
    for c in range(state_ref.shape[0] // CHUNK):
        here = slice(c * CHUNK, (c + 1) * CHUNK)
        cx = band_ref[here, 0:1]
        cy = band_ref[here, 1:2]
        for x in range(rows):
            g = state_ref[here, x * cols : (x + 1) * cols]
            low = 0.0 if x == 0 else state_ref[here, (x - 1) * cols : x * cols]
            high = 0.0 if x == rows - 1 else state_ref[here, (x + 1) * cols : (x + 2) * cols]
            west = jnp.where(lane == 0, 0.0, pltpu.roll(g, 1, 1))
            east = jnp.where(lane == cols - 1, 0.0, pltpu.roll(g, cols - 1, 1))
            out = g - jnp.abs(cx) * speed_ref[x : x + 1, :] * (g - jnp.where(cx > 0, low, high))
            out = out - jnp.abs(cy) * speed_ref[x : x + 1, :] * (g - jnp.where(cy > 0, west, east))
            part_ref[here, x * cols : (x + 1) * cols] = out * sea[x : x + 1, :]


def own_mesh(state_ref, hot_ref, weight_ref, part_ref, near_ref):
    neighbours, padded, nodes = weight_ref.shape
    gp = state_ref.shape[1] - nodes
    mesh = state_ref[:, gp:].astype(BF16)
    for k in range(neighbours):
        near_ref[k] = dot(mesh, hot_ref[k, :nodes, :])
    for c in range(padded // CHUNK):
        here = slice(c * CHUNK, (c + 1) * CHUNK)
        e = state_ref[here, gp:]
        out = e
        for k in range(neighbours):
            out = out + weight_ref[k, here, :] * (near_ref[k, here, :] - e)
        part_ref[here, gp:] = out


def prepare_kernel(
    grid_hbm, mesh_hbm, table_hbm, win_hbm, wout_hbm, index_ref, pq_ref, sea_ref, speed_ref,
    part_ref, hot_ref, weight_ref, band_ref, win_ref, wout_ref,
    grid_ref, mesh_ref, layer_ref, state_ref, near_ref, pack_ref, sem,
):
    fr, dr = lax.axis_index("fr"), lax.axis_index("dr")
    rows, cols = sea_ref.shape
    gp = rows * cols
    padded = state_ref.shape[0]
    bands = grid_ref.shape[0] // rows
    copies = [
        pltpu.make_async_copy(table_hbm.at[fr, dr], band_ref, sem.at[0]),
        pltpu.make_async_copy(mesh_hbm, mesh_ref, sem.at[1]),
        pltpu.make_async_copy(grid_hbm, grid_ref, sem.at[2]),
        pltpu.make_async_copy(win_hbm, layer_ref.at[0], sem.at[3]),
        pltpu.make_async_copy(wout_hbm, layer_ref.at[1], sem.at[4]),
    ]
    for copy in copies:
        copy.start()
    neighbours = index_ref.shape[0]
    for k in range(neighbours):
        hot_ref[k] = one_hot(index_ref[k : k + 1, :], hot_ref.shape[1])
    copies[0].wait()
    for c in range(padded // CHUNK):
        here = slice(c * CHUNK, (c + 1) * CHUNK)
        cx = band_ref[here, 0:1]
        cy = band_ref[here, 1:2]
        for k in range(neighbours):
            w = cx * pq_ref[k : k + 1, :] + cy * pq_ref[neighbours + k : neighbours + k + 1, :]
            weight_ref[k, here, :] = jnp.maximum(w, 0.0)
    copies[1].wait()
    pack_rows(mesh_ref, state_ref, gp)
    own_mesh(state_ref, hot_ref, weight_ref, part_ref, near_ref)
    copies[2].wait()
    state_ref[bands:, :gp] = jnp.zeros((padded - bands, gp), F32)
    for x in range(rows):
        state_ref[:bands, x * cols : (x + 1) * cols] = grid_ref[pl.ds(x, bands, stride=rows), :]
    own_grid(state_ref, band_ref, sea_ref, speed_ref, part_ref)
    half = pack_ref.shape[1] // 2
    copies[3].wait()
    pack_rows(layer_ref.at[0], pack_ref, 0)
    one, two = pack_ref[:, :half].T.astype(BF16), pack_ref[:, half:].T.astype(BF16)
    win_ref[:half, :] = jnp.where(dr == 0, one, two)
    win_ref[half:, :] = jnp.where(dr == 0, two, one)
    copies[4].wait()
    pack_rows(layer_ref.at[1], pack_ref, 0)
    one, two = pack_ref[:, :half].astype(BF16), pack_ref[:, half:].astype(BF16)
    wout_ref[:, :half] = jnp.where(dr == 0, one, two)
    wout_ref[:, half:] = jnp.where(dr == 0, two, one)


def own_kernel(state_ref, hot_ref, weight_ref, band_ref, sea_ref, speed_ref, part_ref, near_ref):
    own_mesh(state_ref, hot_ref, weight_ref, part_ref, near_ref)
    own_grid(state_ref, band_ref, sea_ref, speed_ref, part_ref)


def halo_kernel(
    part_ref, even_ref, odd_ref, hot_ref, weight_ref, band_ref, sea_ref, speed_ref, win_ref,
    moved_ref, keep_ref, send_ref, ext_ref, near_ref, feat_ref,
):
    neighbours, padded, nodes = weight_ref.shape
    rows, cols = sea_ref.shape
    gp = rows * cols
    listed = even_ref.shape[1] - cols
    even = on_even()
    ext_ref[:, :listed] = jnp.where(even, odd_ref[:, cols:], even_ref[:, cols:])
    ext_ref[:, listed:] = jnp.where(even, even_ref[:, cols:], odd_ref[:, cols:])
    for k in range(neighbours):
        near_ref[k] = dot(ext_ref[...], hot_ref[k, nodes:, :])
    scale = sea_ref[...].astype(F32) * speed_ref[...]
    for c in range(padded // CHUNK):
        here = slice(c * CHUNK, (c + 1) * CHUNK)
        cx = band_ref[here, 0:1]
        a, b = even_ref[here, :cols].astype(F32), odd_ref[here, :cols].astype(F32)
        for x in range(rows):
            cut = slice(x * cols, (x + 1) * cols)
            out = part_ref[here, cut]
            if x == 0:
                out = out + jnp.maximum(cx, 0.0) * scale[x : x + 1, :] * jnp.where(even, b, a)
            if x == rows - 1:
                out = out + jnp.maximum(-cx, 0.0) * scale[x : x + 1, :] * jnp.where(even, a, b)
            moved_ref[here, cut] = out
            feat_ref[here, cut] = out.astype(BF16)
        out = part_ref[here, gp:]
        for k in range(neighbours):
            out = out + weight_ref[k, here, :] * near_ref[k, here, :]
        moved_ref[here, gp:] = out
        feat_ref[here, gp:] = out.astype(BF16)
    half = keep_ref.shape[0]
    keep_ref[...] = dot(win_ref[:half, :], feat_ref[...])
    send_ref[...] = dot(win_ref[half:, :], feat_ref[...]).astype(BF16)


def add_transfer(moved_ref, mine_ref, other_ref, wout_ref, hid_ref, state_ref):
    half = mine_ref.shape[0]
    hid_ref[:half, :] = mine_ref[...]
    hid_ref[half:, :] = other_ref[...]
    state_ref[...] = moved_ref[...] + DT_STEP * dot(wout_ref[...], hid_ref[...])


def next_kernel(
    moved_ref, mine_ref, other_ref, wout_ref, halo_ref, state_ref, even_ref, odd_ref, hid_ref,
    *, grid_points, cols,
):
    add_transfer(moved_ref, mine_ref, other_ref, wout_ref, hid_ref, state_ref)
    messages(
        state_ref[:, grid_points:].astype(BF16),
        state_ref[:, :cols].astype(BF16),
        state_ref[:, grid_points - cols : grid_points].astype(BF16),
        halo_ref,
        even_ref,
        odd_ref,
    )


def slots_kernel(
    gi_ref, gw_ref, gc_ref, gt_ref, mi_ref, mw_ref, mc_ref, mt_ref, after_ref,
    gmix_ref, mmix_ref, sums_ref, gland_ref, mland_ref,
):
    me = lax.axis_index("sp")
    _, _, peers, cap = gi_ref.shape
    groups = (
        (gi_ref, gw_ref, gc_ref, gt_ref, gmix_ref, gland_ref, 0),
        (mi_ref, mw_ref, mc_ref, mt_ref, mmix_ref, mland_ref, 1),
    )
    for index_ref, weight_ref, count_ref, target_ref, mix_ref, land_ref, kind in groups:
        length = mix_ref.shape[0]
        spots = lax.broadcasted_iota(jnp.int32, (length, cap), 0)
        slot = lax.broadcasted_iota(jnp.int32, (1, cap), 1)
        for p in range(peers):
            peer = peer_of(me, peers, p)
            count = jnp.sum(
                jnp.where(
                    lax.broadcasted_iota(jnp.int32, (1, peers), 1) == peer, count_ref[...], 0
                ),
                axis=1,
                keepdims=True,
            )
            live = jnp.where(slot < count, 1.0, 0.0)
            mix = jnp.zeros((length, cap), F32)
            total = jnp.zeros((1, cap), F32)
            for j in range(index_ref.shape[0]):
                scaled = weight_ref[j, 0, pl.ds(peer, 1), :] * live
                mix = mix + jnp.where(spots == index_ref[j, 0, pl.ds(peer, 1), :], scaled, 0.0)
                total = total + scaled
            mix_ref[:, p * cap : (p + 1) * cap] = mix.astype(BF16)
            sums_ref[kind : kind + 1, p * cap : (p + 1) * cap] = total
            land_ref[:, p * cap : (p + 1) * cap] = one_hot(
                target_ref[0, pl.ds(peer, 1), :], land_ref.shape[0]
            )


def mix_kernel(
    moved_ref, mine_ref, other_ref, wout_ref, gmix_ref, mmix_ref, sums_ref, state_ref, *rest,
    bands,
):
    out_refs, hid_ref = rest[:-1], rest[-1]
    add_transfer(moved_ref, mine_ref, other_ref, wout_ref, hid_ref, state_ref)
    gp = gmix_ref.shape[0]
    peers = len(out_refs)
    cap = gmix_ref.shape[1] // peers
    grid = state_ref[:, :gp].astype(BF16)
    mesh = state_ref[:, gp:].astype(BF16)
    row = lax.broadcasted_iota(jnp.int32, (state_ref.shape[0], cap), 0)
    for p in range(peers):
        cut = slice(p * cap, (p + 1) * cap)
        for kind, source, mix_ref in ((0, grid, gmix_ref), (1, mesh, mmix_ref)):
            value = dot(source, mix_ref[:, cut])
            value = jnp.where(row == bands, sums_ref[kind : kind + 1, cut], value)
            out_refs[p][:, kind * cap : (kind + 1) * cap] = value.astype(BF16)


def land(values, land_ref):
    return lax.dot_general(
        values, land_ref[...], (((1,), (1,)), ((), ())), preferred_element_type=F32
    )


def end_kernel(state_ref, gland_ref, mland_ref, sea_ref, *rest, bands):
    got_refs, (grid_ref, mesh_ref, values_ref, sum_ref) = rest[:-4], rest[-4:]
    rows, cols = sea_ref.shape
    gp = rows * cols
    freqs, dirs, _ = mesh_ref.shape
    cap = got_refs[0].shape[1] // 2
    for kind in (0, 1):
        for p, got in enumerate(got_refs):
            values_ref[kind, :, p * cap : (p + 1) * cap] = got[:, kind * cap : (kind + 1) * cap]
    sum_ref[:, :gp] = land(values_ref[1], mland_ref)
    sum_ref[:, gp:] = land(values_ref[0], gland_ref)
    cover = sum_ref[bands : bands + 1, :]
    rate = BLEND_RATE / (1.0 + cover)
    sea = sea_ref[...].astype(F32)
    for x in range(rows):
        cut = slice(x * cols, (x + 1) * cols)
        g = state_ref[:bands, cut]
        out = g + rate[:, cut] * (sum_ref[:bands, cut] - cover[:, cut] * g)
        grid_ref[pl.ds(x, bands, stride=rows), :] = out * sea[x : x + 1, :]
    for f in range(freqs):
        here = slice(f * dirs, (f + 1) * dirs)
        e = state_ref[here, gp:]
        mesh_ref[f] = e + rate[:, gp:] * (sum_ref[here, gp:] - cover[:, gp:] * e)


def band_table(freqs, dirs, n_fr, n_dr, padded):
    speed = (0.7 * np.power(np.float32(1.1), -np.arange(freqs * n_fr, dtype=np.float32))).astype(np.float32)
    total = dirs * n_dr
    heading = (2.0 * np.pi * (np.arange(total, dtype=np.float64) + 0.5) / total)
    table = np.zeros((n_fr, n_dr, padded, 2), np.float32)
    for i in range(n_fr):
        for j in range(n_dr):
            s = speed[i * freqs : (i + 1) * freqs, None]
            h = heading[None, j * dirs : (j + 1) * dirs]
            table[i, j, : freqs * dirs, 0] = (s * np.cos(h)).reshape(-1)
            table[i, j, : freqs * dirs, 1] = (s * np.sin(h)).reshape(-1)
    return table


def core_swap(array):
    return lax.ppermute(array, "dr", [(0, 1), (1, 0)])


def fr_swap(array, step):
    size = lax.axis_size("fr")
    return lax.ppermute(array, "fr", [(i, i ^ step) for i in range(size)])


def silu_kernel(total_ref, got_ref, *rest):
    out_ref = rest[-1]
    total = total_ref[...] + got_ref[...].astype(F32)
    out_ref[...] = (total / (1.0 + jnp.exp(-total))).astype(BF16)


def per_device(
    grid_spec, mesh_spec, grid_sea, grid_speed, nb_index, nb_angle, nb_coef, halo_list, w_in, w_out,
    g2m_index, g2m_weight, g2m_count, g2m_target, m2g_index, m2g_weight, m2g_count, m2g_target,
):
    freqs, dirs, rows, cols = grid_spec.shape
    nodes = mesh_spec.shape[2]
    listed = halo_list.shape[1]
    hid = w_in.shape[2]
    half = hid // 2
    bands = freqs * dirs
    padded = (bands // CHUNK + 1) * CHUNK
    gp = rows * cols
    points = gp + nodes
    neighbours = nb_index.shape[0]
    peers, cap = g2m_index.shape[2:]
    n_fr, n_dr = lax.axis_size("fr"), lax.axis_size("dr")

    message = ((padded, cols + listed), BF16)
    state_shape = ((padded, points), F32)
    half_shape = (half, points)
    hid_scratch = ((hid, points), BF16)
    near_scratch = ((neighbours, padded, nodes), F32)
    grid_flat = grid_spec.reshape(bands * rows, cols)
    even, odd = kernel_call(
        functools.partial(begin_kernel, rows=rows),
        [message, message],
        [
            (grid_flat.shape, F32),
            (mesh_spec.shape, F32),
            (halo_list.shape, jnp.int32),
            ((padded, nodes), F32),
            pltpu.SemaphoreType.DMA((3,)),
        ],
        flops=2 * padded * nodes * 2 * listed,
        spaces=[HBM] * 3,
    )(grid_flat, mesh_spec, halo_list)

    table = jnp.asarray(band_table(freqs, dirs, n_fr, n_dr, padded))
    pq = jnp.concatenate([-nb_coef * jnp.cos(nb_angle), -nb_coef * jnp.sin(nb_angle)], axis=0)
    for substep in range(NSUB):
        from_even = pair_swap(even, "sp", 0)
        from_odd = pair_swap(odd, "sp", 1)
        own_flops = 2 * padded * neighbours * nodes * nodes
        if substep == 0:
            part, hot, weight, band, win, wout = kernel_call(
                prepare_kernel,
                [
                    state_shape,
                    ((neighbours, nodes + 2 * listed, nodes), BF16),
                    near_scratch,
                    ((padded, 2), F32),
                    ((hid, padded), BF16),
                    ((padded, hid), BF16),
                ],
                [
                    (grid_flat.shape, F32),
                    (mesh_spec.shape, F32),
                    ((2,) + w_in.shape, BF16),
                    state_shape,
                    near_scratch,
                    ((padded, hid), F32),
                    pltpu.SemaphoreType.DMA((5,)),
                ],
                flops=3 * own_flops,
                spaces=[HBM] * 5 + [VMEM] * 4,
            )(
                grid_flat, mesh_spec, table, w_in, jnp.transpose(w_out, (1, 2, 0)),
                nb_index, pq, grid_sea, grid_speed,
            )
        else:
            (part,) = kernel_call(own_kernel, [state_shape], [near_scratch], flops=own_flops)(
                state, hot, weight, band, grid_sea, grid_speed
            )
        moved, total, send = kernel_call(
            halo_kernel,
            [state_shape, (half_shape, F32), (half_shape, BF16)],
            [((padded, 2 * listed), BF16), near_scratch, ((padded, points), BF16)],
            flops=2 * padded * (neighbours * nodes * 2 * listed + hid * points),
        )(part, from_even, from_odd, hot, weight, band, grid_sea, grid_speed, win)

        total = total + core_swap(send).astype(F32)
        rounded = total.astype(BF16)
        got = fr_swap(rounded, 1)
        step = 2
        while step < n_fr:
            total = total + got.astype(F32)
            rounded = total.astype(BF16)
            got = fr_swap(rounded, step)
            step *= 2
        extra = []
        if substep == 0:
            gmix, mmix, sums, gland, mland = kernel_call(
                slots_kernel,
                [
                    ((gp, peers * cap), BF16),
                    ((nodes, peers * cap), BF16),
                    ((2, peers * cap), F32),
                    ((nodes, peers * cap), BF16),
                    ((gp, peers * cap), BF16),
                ],
                flops=2 << 30,
                spaces=[VMEM] * 8 + [pl.ANY],
            )(
                g2m_index, g2m_weight, g2m_count, g2m_target,
                m2g_index, m2g_weight, m2g_count, m2g_target, rounded,
            )
            extra = [sums]
        (mine,) = kernel_call(
            silu_kernel, [(half_shape, BF16)], spaces=[VMEM, VMEM] + [pl.ANY] * len(extra)
        )(total, got, *extra)
        other = core_swap(mine)
        if substep < NSUB - 1:
            state, even, odd = kernel_call(
                functools.partial(next_kernel, grid_points=gp, cols=cols),
                [state_shape, message, message],
                [hid_scratch],
                flops=2 * padded * hid * points,
            )(moved, mine, other, wout, halo_list)

    state, *values = kernel_call(
        functools.partial(mix_kernel, bands=bands),
        [state_shape] + [((padded, 2 * cap), BF16)] * peers,
        [hid_scratch],
        flops=2 * padded * (hid * points + points * peers * cap),
    )(moved, mine, other, wout, gmix, mmix, sums)
    got = [
        lax.ppermute(v, "sp", peer_pairs(peers, p)) if p else v for p, v in enumerate(values)
    ]
    if peers & (peers - 1):
        got[0] = lax.ppermute(values[0], "sp", peer_pairs(peers, 0))
    grid_out, mesh_out = kernel_call(
        functools.partial(end_kernel, bands=bands),
        [((bands * rows, cols), F32), ((freqs, dirs, nodes), F32)],
        [((2, padded, peers * cap), BF16), state_shape],
        flops=2 * padded * points * peers * cap,
    )(state, gland, mland, grid_sea, *got)
    return grid_out.reshape(grid_spec.shape), mesh_out


def solution(mesh):
    return jax.shard_map(
        per_device,
        mesh=mesh,
        in_specs=(
            P("fr", "dr", ("grp", "sp"), None),
            P("fr", "dr", ("grp", "sp")),
            P(("grp", "sp"), None),
            P(("grp", "sp"), None),
            P(None, ("grp", "sp")),
            P(None, ("grp", "sp")),
            P(None, ("grp", "sp")),
            P(None, ("grp", "sp")),
            P("fr", "dr", None),
            P(None, "fr", "dr"),
            P(None, ("grp", "sp"), None, None),
            P(None, ("grp", "sp"), None, None),
            P(("grp", "sp"), None),
            P(("grp", "sp"), None, None),
            P(None, ("grp", "sp"), None, None),
            P(None, ("grp", "sp"), None, None),
            P(("grp", "sp"), None),
            P(("grp", "sp"), None, None),
        ),
        out_specs=(P("fr", "dr", ("grp", "sp"), None), P("fr", "dr", ("grp", "sp"))),
        check_vma=False,
    )
```

```python
import functools

import jax
import jax.numpy as jnp
import numpy as np
from jax import lax
from jax.experimental import pallas as pl
from jax.experimental.pallas import tpu as pltpu
from jax.sharding import PartitionSpec as P

NSUB = 2
DT_STEP = 0.1
BLEND_RATE = 0.5
F32 = jnp.float32
BF16 = jnp.bfloat16
CHUNK = 16


VMEM = pltpu.MemorySpace.VMEM
HBM = pltpu.MemorySpace.HBM


def kernel_call(body, outs, scratch=(), flops=0, nbytes=2 << 20, spaces=None, out_space=VMEM):
    def run(*args):
        where = spaces or [VMEM] * len(args)
        args = [
            pltpu.with_memory_space_constraint(a, HBM) if space == HBM else a
            for a, space in zip(args, where)
        ]
        return pl.pallas_call(
            body,
            out_shape=[jax.ShapeDtypeStruct(s, t) for s, t in outs],
            in_specs=[pl.BlockSpec(memory_space=space) for space in where],
            out_specs=[pl.BlockSpec(memory_space=out_space)] * len(outs),
            scratch_shapes=[s if hasattr(s, "dtype") else pltpu.VMEM(*s) for s in scratch],
            compiler_params=pltpu.CompilerParams(vmem_limit_bytes=16 << 20),
            cost_estimate=pl.CostEstimate(flops=flops, bytes_accessed=nbytes, transcendentals=0),
        )(*args)

    return run


def dot(a, b):
    return jnp.dot(a, b, preferred_element_type=F32)


def one_hot(row, length):
    spots = lax.broadcasted_iota(jnp.int32, (length, row.shape[1]), 0)
    return jnp.where(spots == row, 1.0, 0.0).astype(BF16)


def pair_swap(array, axis, first):
    size = lax.axis_size(axis)
    pairs = [(i, i + 1) for i in range(first, size - 1, 2)]
    return lax.ppermute(array, axis, pairs + [(j, i) for i, j in pairs])


def peer_swap(array, axis, step):
    size = lax.axis_size(axis)
    return lax.ppermute(array, axis, [(i, i ^ step) for i in range(size)])


def on_even():
    return lax.rem(lax.axis_index("sp"), 2) == 0


def messages(mesh, low_row, high_row, halo_ref, even_ref, odd_ref):
    even = on_even()
    nodes = mesh.shape[1]
    cols = low_row.shape[1]
    to_lower = dot(mesh, one_hot(halo_ref[0:1, :], nodes)).astype(BF16)
    to_upper = dot(mesh, one_hot(halo_ref[1:2, :], nodes)).astype(BF16)
    even_ref[:, :cols] = jnp.where(even, high_row, low_row)
    odd_ref[:, :cols] = jnp.where(even, low_row, high_row)
    even_ref[:, cols:] = jnp.where(even, to_upper, to_lower)
    odd_ref[:, cols:] = jnp.where(even, to_lower, to_upper)


def pack_rows(source_ref, packed_ref, at):
    freqs, dirs, width = source_ref.shape
    for f in range(freqs):
        packed_ref[f * dirs : (f + 1) * dirs, at : at + width] = source_ref[f].astype(F32)
    packed_ref[freqs * dirs :, at : at + width] = jnp.zeros(
        (packed_ref.shape[0] - freqs * dirs, width), F32
    )


def begin_kernel(
    grid_hbm, mesh_hbm, halo_hbm, even_ref, odd_ref, grid_ref, mesh_ref, halo_ref, packed_ref, sem,
    *, rows,
):
    copies = [
        pltpu.make_async_copy(halo_hbm, halo_ref, sem.at[0]),
        pltpu.make_async_copy(mesh_hbm, mesh_ref, sem.at[1]),
        pltpu.make_async_copy(grid_hbm, grid_ref, sem.at[2]),
    ]
    for copy in copies:
        copy.start()
    bands = grid_ref.shape[0] // rows
    blank = jnp.zeros((packed_ref.shape[0] - bands, grid_ref.shape[1]), F32)
    copies[0].wait()
    copies[1].wait()
    pack_rows(mesh_ref, packed_ref, 0)
    copies[2].wait()
    low = jnp.concatenate([grid_ref[pl.ds(0, bands, stride=rows), :], blank], axis=0)
    high = jnp.concatenate([grid_ref[pl.ds(rows - 1, bands, stride=rows), :], blank], axis=0)
    messages(
        packed_ref[...].astype(BF16), low.astype(BF16), high.astype(BF16), halo_ref, even_ref, odd_ref
    )


def own_grid(state_ref, band_ref, sea_ref, speed_ref, part_ref):
    rows, cols = sea_ref.shape
    sea = sea_ref[...].astype(F32)
    lane = lax.broadcasted_iota(jnp.int32, (CHUNK, cols), 1)
    for c in range(state_ref.shape[0] // CHUNK):
        here = slice(c * CHUNK, (c + 1) * CHUNK)
        cx = band_ref[here, 0:1]
        cy = band_ref[here, 1:2]
        for x in range(rows):
            g = state_ref[here, x * cols : (x + 1) * cols]
            low = 0.0 if x == 0 else state_ref[here, (x - 1) * cols : x * cols]
            high = 0.0 if x == rows - 1 else state_ref[here, (x + 1) * cols : (x + 2) * cols]
            west = jnp.where(lane == 0, 0.0, pltpu.roll(g, 1, 1))
            east = jnp.where(lane == cols - 1, 0.0, pltpu.roll(g, cols - 1, 1))
            out = g - jnp.abs(cx) * speed_ref[x : x + 1, :] * (g - jnp.where(cx > 0, low, high))
            out = out - jnp.abs(cy) * speed_ref[x : x + 1, :] * (g - jnp.where(cy > 0, west, east))
            part_ref[here, x * cols : (x + 1) * cols] = out * sea[x : x + 1, :]


def own_mesh(state_ref, hot_ref, weight_ref, part_ref, near_ref):
    neighbours, padded, nodes = weight_ref.shape
    gp = state_ref.shape[1] - nodes
    mesh = state_ref[:, gp:].astype(BF16)
    for k in range(neighbours):
        near_ref[k] = dot(mesh, hot_ref[k, :nodes, :])
    for c in range(padded // CHUNK):
        here = slice(c * CHUNK, (c + 1) * CHUNK)
        e = state_ref[here, gp:]
        out = e
        for k in range(neighbours):
            out = out + weight_ref[k, here, :] * (near_ref[k, here, :] - e)
        part_ref[here, gp:] = out


def prepare_kernel(
    grid_hbm, mesh_hbm, table_hbm, win_hbm, wout_hbm, index_ref, pq_ref, sea_ref, speed_ref,
    part_ref, hot_ref, weight_ref, band_ref, win_ref, wout_ref,
    grid_ref, mesh_ref, layer_ref, state_ref, near_ref, pack_ref, sem,
):
    fr, dr = lax.axis_index("fr"), lax.axis_index("dr")
    rows, cols = sea_ref.shape
    gp = rows * cols
    padded = state_ref.shape[0]
    bands = grid_ref.shape[0] // rows
    copies = [
        pltpu.make_async_copy(table_hbm.at[fr, dr], band_ref, sem.at[0]),
        pltpu.make_async_copy(mesh_hbm, mesh_ref, sem.at[1]),
        pltpu.make_async_copy(grid_hbm, grid_ref, sem.at[2]),
        pltpu.make_async_copy(win_hbm, layer_ref.at[0], sem.at[3]),
        pltpu.make_async_copy(wout_hbm, layer_ref.at[1], sem.at[4]),
    ]
    for copy in copies:
        copy.start()
    neighbours = index_ref.shape[0]
    for k in range(neighbours):
        hot_ref[k] = one_hot(index_ref[k : k + 1, :], hot_ref.shape[1])
    copies[0].wait()
    for c in range(padded // CHUNK):
        here = slice(c * CHUNK, (c + 1) * CHUNK)
        cx = band_ref[here, 0:1]
        cy = band_ref[here, 1:2]
        for k in range(neighbours):
            w = cx * pq_ref[k : k + 1, :] + cy * pq_ref[neighbours + k : neighbours + k + 1, :]
            weight_ref[k, here, :] = jnp.maximum(w, 0.0)
    copies[1].wait()
    pack_rows(mesh_ref, state_ref, gp)
    own_mesh(state_ref, hot_ref, weight_ref, part_ref, near_ref)
    copies[2].wait()
    state_ref[bands:, :gp] = jnp.zeros((padded - bands, gp), F32)
    for x in range(rows):
        state_ref[:bands, x * cols : (x + 1) * cols] = grid_ref[pl.ds(x, bands, stride=rows), :]
    own_grid(state_ref, band_ref, sea_ref, speed_ref, part_ref)
    half = pack_ref.shape[1] // 2
    copies[3].wait()
    pack_rows(layer_ref.at[0], pack_ref, 0)
    one, two = pack_ref[:, :half].T.astype(BF16), pack_ref[:, half:].T.astype(BF16)
    win_ref[:half, :] = jnp.where(dr == 0, one, two)
    win_ref[half:, :] = jnp.where(dr == 0, two, one)
    copies[4].wait()
    pack_rows(layer_ref.at[1], pack_ref, 0)
    one, two = pack_ref[:, :half].astype(BF16), pack_ref[:, half:].astype(BF16)
    wout_ref[:, :half] = jnp.where(dr == 0, one, two)
    wout_ref[:, half:] = jnp.where(dr == 0, two, one)


def own_kernel(state_ref, hot_ref, weight_ref, band_ref, sea_ref, speed_ref, part_ref, near_ref):
    own_mesh(state_ref, hot_ref, weight_ref, part_ref, near_ref)
    own_grid(state_ref, band_ref, sea_ref, speed_ref, part_ref)


def halo_kernel(
    part_ref, even_ref, odd_ref, hot_ref, weight_ref, band_ref, sea_ref, speed_ref, win_ref,
    moved_ref, keep_ref, send_ref, ext_ref, near_ref, feat_ref,
):
    neighbours, padded, nodes = weight_ref.shape
    rows, cols = sea_ref.shape
    gp = rows * cols
    listed = even_ref.shape[1] - cols
    even = on_even()
    ext_ref[:, :listed] = jnp.where(even, odd_ref[:, cols:], even_ref[:, cols:])
    ext_ref[:, listed:] = jnp.where(even, even_ref[:, cols:], odd_ref[:, cols:])
    for k in range(neighbours):
        near_ref[k] = dot(ext_ref[...], hot_ref[k, nodes:, :])
    scale = sea_ref[...].astype(F32) * speed_ref[...]
    for c in range(padded // CHUNK):
        here = slice(c * CHUNK, (c + 1) * CHUNK)
        cx = band_ref[here, 0:1]
        a, b = even_ref[here, :cols].astype(F32), odd_ref[here, :cols].astype(F32)
        for x in range(rows):
            cut = slice(x * cols, (x + 1) * cols)
            out = part_ref[here, cut]
            if x == 0:
                out = out + jnp.maximum(cx, 0.0) * scale[x : x + 1, :] * jnp.where(even, b, a)
            if x == rows - 1:
                out = out + jnp.maximum(-cx, 0.0) * scale[x : x + 1, :] * jnp.where(even, a, b)
            moved_ref[here, cut] = out
            feat_ref[here, cut] = out.astype(BF16)
        out = part_ref[here, gp:]
        for k in range(neighbours):
            out = out + weight_ref[k, here, :] * near_ref[k, here, :]
        moved_ref[here, gp:] = out
        feat_ref[here, gp:] = out.astype(BF16)
    half = keep_ref.shape[0]
    keep_ref[...] = dot(win_ref[:half, :], feat_ref[...])
    send_ref[...] = dot(win_ref[half:, :], feat_ref[...]).astype(BF16)


def add_transfer(moved_ref, mine_ref, other_ref, wout_ref, hid_ref, state_ref):
    half = mine_ref.shape[0]
    hid_ref[:half, :] = mine_ref[...]
    hid_ref[half:, :] = other_ref[...]
    state_ref[...] = moved_ref[...] + DT_STEP * dot(wout_ref[...], hid_ref[...])


def next_kernel(
    moved_ref, mine_ref, other_ref, wout_ref, halo_ref, state_ref, even_ref, odd_ref, hid_ref,
    *, grid_points, cols,
):
    add_transfer(moved_ref, mine_ref, other_ref, wout_ref, hid_ref, state_ref)
    messages(
        state_ref[:, grid_points:].astype(BF16),
        state_ref[:, :cols].astype(BF16),
        state_ref[:, grid_points - cols : grid_points].astype(BF16),
        halo_ref,
        even_ref,
        odd_ref,
    )


def slots_kernel(
    gi_ref, gw_ref, gc_ref, gt_ref, mi_ref, mw_ref, mc_ref, mt_ref, after_ref,
    gmix_ref, mmix_ref, sums_ref, gland_ref, mland_ref,
):
    me = lax.axis_index("sp")
    _, _, peers, cap = gi_ref.shape
    groups = (
        (gi_ref, gw_ref, gc_ref, gt_ref, gmix_ref, gland_ref, 0),
        (mi_ref, mw_ref, mc_ref, mt_ref, mmix_ref, mland_ref, 1),
    )
    for index_ref, weight_ref, count_ref, target_ref, mix_ref, land_ref, kind in groups:
        length = mix_ref.shape[0]
        spots = lax.broadcasted_iota(jnp.int32, (length, cap), 0)
        slot = lax.broadcasted_iota(jnp.int32, (1, cap), 1)
        for p in range(peers):
            peer = lax.bitwise_xor(me, p)
            count = jnp.sum(
                jnp.where(
                    lax.broadcasted_iota(jnp.int32, (1, peers), 1) == peer, count_ref[...], 0
                ),
                axis=1,
                keepdims=True,
            )
            live = jnp.where(slot < count, 1.0, 0.0)
            mix = jnp.zeros((length, cap), F32)
            total = jnp.zeros((1, cap), F32)
            for j in range(index_ref.shape[0]):
                scaled = weight_ref[j, 0, pl.ds(peer, 1), :] * live
                mix = mix + jnp.where(spots == index_ref[j, 0, pl.ds(peer, 1), :], scaled, 0.0)
                total = total + scaled
            mix_ref[:, p * cap : (p + 1) * cap] = mix.astype(BF16)
            sums_ref[kind : kind + 1, p * cap : (p + 1) * cap] = total
            land_ref[:, p * cap : (p + 1) * cap] = one_hot(
                target_ref[0, pl.ds(peer, 1), :], land_ref.shape[0]
            )


def mix_kernel(
    moved_ref, mine_ref, other_ref, wout_ref, gmix_ref, mmix_ref, sums_ref, state_ref, *rest,
    bands,
):
    out_refs, hid_ref = rest[:-1], rest[-1]
    add_transfer(moved_ref, mine_ref, other_ref, wout_ref, hid_ref, state_ref)
    gp = gmix_ref.shape[0]
    peers = len(out_refs)
    cap = gmix_ref.shape[1] // peers
    grid = state_ref[:, :gp].astype(BF16)
    mesh = state_ref[:, gp:].astype(BF16)
    row = lax.broadcasted_iota(jnp.int32, (state_ref.shape[0], cap), 0)
    for p in range(peers):
        cut = slice(p * cap, (p + 1) * cap)
        for kind, source, mix_ref in ((0, grid, gmix_ref), (1, mesh, mmix_ref)):
            value = dot(source, mix_ref[:, cut])
            value = jnp.where(row == bands, sums_ref[kind : kind + 1, cut], value)
            out_refs[p][:, kind * cap : (kind + 1) * cap] = value.astype(BF16)


def silu_kernel(total_ref, got_ref, *rest):
    total = total_ref[...] + got_ref[...].astype(F32)
    rest[-1][...] = (total / (1.0 + jnp.exp(-total))).astype(BF16)


def land(values, land_ref):
    return lax.dot_general(
        values, land_ref[...], (((1,), (1,)), ((), ())), preferred_element_type=F32
    )


def end_kernel(state_ref, gland_ref, mland_ref, sea_ref, *rest, bands):
    got_refs, rest = rest[-8::-1], rest[-7:]
    grid_hbm, mesh_hbm, values_ref, sum_ref, grid_ref, mesh_ref, sem = rest
    rows, cols = sea_ref.shape
    gp = rows * cols
    freqs, dirs, _ = mesh_ref.shape
    cap = got_refs[0].shape[1] // 2
    for kind in (0, 1):
        for p, got in enumerate(got_refs):
            values_ref[kind, :, p * cap : (p + 1) * cap] = got[:, kind * cap : (kind + 1) * cap]
    sum_ref[:, gp:] = land(values_ref[0], gland_ref)
    cover = sum_ref[bands : bands + 1, gp:]
    rate = BLEND_RATE / (1.0 + cover)
    keep = 1.0 - rate * cover
    for f in range(freqs):
        here = slice(f * dirs, (f + 1) * dirs)
        mesh_ref[f] = keep * state_ref[here, gp:] + rate * sum_ref[here, gp:]
    mesh_copy = pltpu.make_async_copy(mesh_ref, mesh_hbm, sem.at[0])
    mesh_copy.start()
    sum_ref[:, :gp] = land(values_ref[1], mland_ref)
    cover = sum_ref[bands : bands + 1, :gp]
    rate = BLEND_RATE / (1.0 + cover)
    keep = 1.0 - rate * cover
    sea = sea_ref[...].astype(F32)
    for x in range(rows):
        cut = slice(x * cols, (x + 1) * cols)
        wet = sea[x : x + 1, :]
        out = keep[:, cut] * wet * state_ref[:bands, cut] + rate[:, cut] * wet * sum_ref[:bands, cut]
        grid_ref[pl.ds(x, bands, stride=rows), :] = out
    grid_copy = pltpu.make_async_copy(grid_ref, grid_hbm, sem.at[1])
    grid_copy.start()
    mesh_copy.wait()
    grid_copy.wait()


def band_table(freqs, dirs, n_fr, n_dr, padded):
    speed = (0.7 * np.power(np.float32(1.1), -np.arange(freqs * n_fr, dtype=np.float32))).astype(np.float32)
    total = dirs * n_dr
    heading = (2.0 * np.pi * (np.arange(total, dtype=np.float64) + 0.5) / total)
    table = np.zeros((n_fr, n_dr, padded, 2), np.float32)
    for i in range(n_fr):
        for j in range(n_dr):
            s = speed[i * freqs : (i + 1) * freqs, None]
            h = heading[None, j * dirs : (j + 1) * dirs]
            table[i, j, : freqs * dirs, 0] = (s * np.cos(h)).reshape(-1)
            table[i, j, : freqs * dirs, 1] = (s * np.sin(h)).reshape(-1)
    return table


def core_swap(array):
    return lax.ppermute(array, "dr", [(0, 1), (1, 0)])


def per_device(
    grid_spec, mesh_spec, grid_sea, grid_speed, nb_index, nb_angle, nb_coef, halo_list, w_in, w_out,
    g2m_index, g2m_weight, g2m_count, g2m_target, m2g_index, m2g_weight, m2g_count, m2g_target,
):
    freqs, dirs, rows, cols = grid_spec.shape
    nodes = mesh_spec.shape[2]
    listed = halo_list.shape[1]
    hid = w_in.shape[2]
    half = hid // 2
    bands = freqs * dirs
    padded = (bands // CHUNK + 1) * CHUNK
    gp = rows * cols
    points = gp + nodes
    neighbours = nb_index.shape[0]
    peers, cap = g2m_index.shape[2:]
    n_fr, n_dr = lax.axis_size("fr"), lax.axis_size("dr")

    message = ((padded, cols + listed), BF16)
    state_shape = ((padded, points), F32)
    half_shape = (half, points)
    hid_scratch = ((hid, points), BF16)
    near_scratch = ((neighbours, padded, nodes), F32)
    grid_flat = grid_spec.reshape(bands * rows, cols)
    even, odd = kernel_call(
        functools.partial(begin_kernel, rows=rows),
        [message, message],
        [
            (grid_flat.shape, F32),
            (mesh_spec.shape, F32),
            (halo_list.shape, jnp.int32),
            ((padded, nodes), F32),
            pltpu.SemaphoreType.DMA((3,)),
        ],
        flops=2 * padded * nodes * 2 * listed,
        spaces=[HBM] * 3,
    )(grid_flat, mesh_spec, halo_list)

    table = jnp.asarray(band_table(freqs, dirs, n_fr, n_dr, padded))
    pq = jnp.concatenate([-nb_coef * jnp.cos(nb_angle), -nb_coef * jnp.sin(nb_angle)], axis=0)
    for substep in range(NSUB):
        from_even = pair_swap(even, "sp", 0)
        from_odd = pair_swap(odd, "sp", 1)
        own_flops = 2 * padded * neighbours * nodes * nodes
        if substep == 0:
            part, hot, weight, band, win, wout = kernel_call(
                prepare_kernel,
                [
                    state_shape,
                    ((neighbours, nodes + 2 * listed, nodes), BF16),
                    near_scratch,
                    ((padded, 2), F32),
                    ((hid, padded), BF16),
                    ((padded, hid), BF16),
                ],
                [
                    (grid_flat.shape, F32),
                    (mesh_spec.shape, F32),
                    ((2,) + w_in.shape, BF16),
                    state_shape,
                    near_scratch,
                    ((padded, hid), F32),
                    pltpu.SemaphoreType.DMA((5,)),
                ],
                flops=3 * own_flops,
                spaces=[HBM] * 5 + [VMEM] * 4,
            )(
                grid_flat, mesh_spec, table, w_in, jnp.transpose(w_out, (1, 2, 0)),
                nb_index, pq, grid_sea, grid_speed,
            )
        else:
            (part,) = kernel_call(own_kernel, [state_shape], [near_scratch], flops=own_flops)(
                state, hot, weight, band, grid_sea, grid_speed
            )
        moved, total, send = kernel_call(
            halo_kernel,
            [state_shape, (half_shape, F32), (half_shape, BF16)],
            [((padded, 2 * listed), BF16), near_scratch, ((padded, points), BF16)],
            flops=2 * padded * (neighbours * nodes * 2 * listed + hid * points),
        )(part, from_even, from_odd, hot, weight, band, grid_sea, grid_speed, win)

        total = total + core_swap(send).astype(F32)
        rounded = total.astype(BF16)
        got = peer_swap(rounded, "fr", 1)
        step = 2
        while step < n_fr:
            total = total + got.astype(F32)
            rounded = total.astype(BF16)
            got = peer_swap(rounded, "fr", step)
            step *= 2
        extra = []
        if substep == 0:
            gmix, mmix, sums, gland, mland = kernel_call(
                slots_kernel,
                [
                    ((gp, peers * cap), BF16),
                    ((nodes, peers * cap), BF16),
                    ((2, peers * cap), F32),
                    ((nodes, peers * cap), BF16),
                    ((gp, peers * cap), BF16),
                ],
                flops=2 << 30,
                spaces=[VMEM] * 8 + [pl.ANY],
            )(
                g2m_index, g2m_weight, g2m_count, g2m_target,
                m2g_index, m2g_weight, m2g_count, m2g_target, rounded,
            )
            extra = [sums]
        (mine,) = kernel_call(
            silu_kernel, [(half_shape, BF16)], spaces=[VMEM, VMEM] + [pl.ANY] * len(extra)
        )(total, got, *extra)
        other = core_swap(mine)
        if substep < NSUB - 1:
            state, even, odd = kernel_call(
                functools.partial(next_kernel, grid_points=gp, cols=cols),
                [state_shape, message, message],
                [hid_scratch],
                flops=2 * padded * hid * points,
            )(moved, mine, other, wout, halo_list)

    state, *values = kernel_call(
        functools.partial(mix_kernel, bands=bands),
        [state_shape] + [((padded, 2 * cap), BF16)] * peers,
        [hid_scratch],
        flops=2 * padded * (hid * points + points * peers * cap),
    )(moved, mine, other, wout, gmix, mmix, sums)
    for p in reversed(range(1, peers)):
        values[p] = peer_swap(values[p], "sp", p)
    grid_out, mesh_out = kernel_call(
        functools.partial(end_kernel, bands=bands),
        [(grid_flat.shape, F32), (mesh_spec.shape, F32)],
        [
            ((2, padded, peers * cap), BF16),
            state_shape,
            (grid_flat.shape, F32),
            (mesh_spec.shape, F32),
            pltpu.SemaphoreType.DMA((2,)),
        ],
        flops=2 * padded * points * peers * cap,
        out_space=pl.ANY,
    )(state, gland, mland, grid_sea, *values[::-1])
    return grid_out.reshape(grid_spec.shape), mesh_out


def solution(mesh):
    return jax.shard_map(
        per_device,
        mesh=mesh,
        in_specs=(
            P("fr", "dr", ("grp", "sp"), None),
            P("fr", "dr", ("grp", "sp")),
            P(("grp", "sp"), None),
            P(("grp", "sp"), None),
            P(None, ("grp", "sp")),
            P(None, ("grp", "sp")),
            P(None, ("grp", "sp")),
            P(None, ("grp", "sp")),
            P("fr", "dr", None),
            P(None, "fr", "dr"),
            P(None, ("grp", "sp"), None, None),
            P(None, ("grp", "sp"), None, None),
            P(("grp", "sp"), None),
            P(("grp", "sp"), None, None),
            P(None, ("grp", "sp"), None, None),
            P(None, ("grp", "sp"), None, None),
            P(("grp", "sp"), None),
            P(("grp", "sp"), None, None),
        ),
        out_specs=(P("fr", "dr", ("grp", "sp"), None), P("fr", "dr", ("grp", "sp"))),
        check_vma=False,
    )
```

```python
import functools

import jax
import jax.numpy as jnp
import numpy as np
from jax import lax
from jax.experimental import pallas as pl
from jax.experimental.pallas import tpu as pltpu
from jax.sharding import PartitionSpec as P

NSUB = 2
DT_STEP = 0.1
BLEND_RATE = 0.5
F32 = jnp.float32
BF16 = jnp.bfloat16
CHUNK = 16


VMEM = pltpu.MemorySpace.VMEM
HBM = pltpu.MemorySpace.HBM


def kernel_call(body, outs, scratch=(), flops=0, nbytes=2 << 20, spaces=None, out_space=VMEM):
    def run(*args):
        where = spaces or [VMEM] * len(args)
        args = [
            pltpu.with_memory_space_constraint(a, HBM) if space == HBM else a
            for a, space in zip(args, where)
        ]
        return pl.pallas_call(
            body,
            out_shape=[jax.ShapeDtypeStruct(s, t) for s, t in outs],
            in_specs=[pl.BlockSpec(memory_space=space) for space in where],
            out_specs=[pl.BlockSpec(memory_space=out_space)] * len(outs),
            scratch_shapes=[s if hasattr(s, "dtype") else pltpu.VMEM(*s) for s in scratch],
            compiler_params=pltpu.CompilerParams(vmem_limit_bytes=16 << 20),
            cost_estimate=pl.CostEstimate(flops=flops, bytes_accessed=nbytes, transcendentals=0),
        )(*args)

    return run


def dot(a, b):
    return jnp.dot(a, b, preferred_element_type=F32)


def one_hot(row, length):
    spots = lax.broadcasted_iota(jnp.int32, (length, row.shape[1]), 0)
    return jnp.where(spots == row, 1.0, 0.0).astype(BF16)


def pair_swap(array, axis, first):
    size = lax.axis_size(axis)
    pairs = [(i, i + 1) for i in range(first, size - 1, 2)]
    return lax.ppermute(array, axis, pairs + [(j, i) for i, j in pairs])


def peer_swap(array, axis, step):
    size = lax.axis_size(axis)
    return lax.ppermute(array, axis, [(i, i ^ step) for i in range(size)])


def on_even():
    return lax.rem(lax.axis_index("sp"), 2) == 0


def messages(mesh, low_row, high_row, halo_ref, even_ref, odd_ref):
    even = on_even()
    nodes = mesh.shape[1]
    cols = low_row.shape[1]
    to_lower = dot(mesh, one_hot(halo_ref[0:1, :], nodes)).astype(BF16)
    to_upper = dot(mesh, one_hot(halo_ref[1:2, :], nodes)).astype(BF16)
    even_ref[:, :cols] = jnp.where(even, high_row, low_row)
    odd_ref[:, :cols] = jnp.where(even, low_row, high_row)
    even_ref[:, cols:] = jnp.where(even, to_upper, to_lower)
    odd_ref[:, cols:] = jnp.where(even, to_lower, to_upper)


def pack_rows(source_ref, packed_ref, at):
    freqs, dirs, width = source_ref.shape
    for f in range(freqs):
        packed_ref[f * dirs : (f + 1) * dirs, at : at + width] = source_ref[f].astype(F32)
    packed_ref[freqs * dirs :, at : at + width] = jnp.zeros(
        (packed_ref.shape[0] - freqs * dirs, width), F32
    )


def begin_kernel(
    grid_hbm, mesh_hbm, halo_hbm, even_ref, odd_ref, grid_ref, mesh_ref, halo_ref, packed_ref, sem,
    *, rows,
):
    copies = [
        pltpu.make_async_copy(halo_hbm, halo_ref, sem.at[0]),
        pltpu.make_async_copy(mesh_hbm, mesh_ref, sem.at[1]),
        pltpu.make_async_copy(grid_hbm, grid_ref, sem.at[2]),
    ]
    for copy in copies:
        copy.start()
    bands = grid_ref.shape[0] // rows
    blank = jnp.zeros((packed_ref.shape[0] - bands, grid_ref.shape[1]), F32)
    copies[0].wait()
    copies[1].wait()
    pack_rows(mesh_ref, packed_ref, 0)
    copies[2].wait()
    low = jnp.concatenate([grid_ref[pl.ds(0, bands, stride=rows), :], blank], axis=0)
    high = jnp.concatenate([grid_ref[pl.ds(rows - 1, bands, stride=rows), :], blank], axis=0)
    messages(
        packed_ref[...].astype(BF16), low.astype(BF16), high.astype(BF16), halo_ref, even_ref, odd_ref
    )


def own_grid(state_ref, band_ref, sea_ref, speed_ref, part_ref):
    rows, cols = sea_ref.shape
    sea = sea_ref[...].astype(F32)
    lane = lax.broadcasted_iota(jnp.int32, (CHUNK, cols), 1)
    for c in range(state_ref.shape[0] // CHUNK):
        here = slice(c * CHUNK, (c + 1) * CHUNK)
        cx = band_ref[here, 0:1]
        cy = band_ref[here, 1:2]
        for x in range(rows):
            g = state_ref[here, x * cols : (x + 1) * cols]
            low = 0.0 if x == 0 else state_ref[here, (x - 1) * cols : x * cols]
            high = 0.0 if x == rows - 1 else state_ref[here, (x + 1) * cols : (x + 2) * cols]
            west = jnp.where(lane == 0, 0.0, pltpu.roll(g, 1, 1))
            east = jnp.where(lane == cols - 1, 0.0, pltpu.roll(g, cols - 1, 1))
            out = g - jnp.abs(cx) * speed_ref[x : x + 1, :] * (g - jnp.where(cx > 0, low, high))
            out = out - jnp.abs(cy) * speed_ref[x : x + 1, :] * (g - jnp.where(cy > 0, west, east))
            part_ref[here, x * cols : (x + 1) * cols] = out * sea[x : x + 1, :]


def own_mesh(state_ref, hot_ref, weight_ref, part_ref, near_ref):
    neighbours, padded, nodes = weight_ref.shape
    gp = state_ref.shape[1] - nodes
    mesh = state_ref[:, gp:].astype(BF16)
    for k in range(neighbours):
        near_ref[k] = dot(mesh, hot_ref[k, :nodes, :])
    for c in range(padded // CHUNK):
        here = slice(c * CHUNK, (c + 1) * CHUNK)
        e = state_ref[here, gp:]
        out = e
        for k in range(neighbours):
            out = out + weight_ref[k, here, :] * (near_ref[k, here, :] - e)
        part_ref[here, gp:] = out


def prepare_kernel(
    grid_hbm, mesh_hbm, table_hbm, win_hbm, wout_hbm, index_ref, pq_ref, sea_ref, speed_ref,
    part_ref, hot_ref, weight_ref, band_ref, win_ref, wout_ref,
    grid_ref, mesh_ref, layer_ref, state_ref, near_ref, pack_ref, sem,
):
    fr, dr = lax.axis_index("fr"), lax.axis_index("dr")
    rows, cols = sea_ref.shape
    gp = rows * cols
    padded = state_ref.shape[0]
    bands = grid_ref.shape[0] // rows
    copies = [
        pltpu.make_async_copy(table_hbm.at[fr, dr], band_ref, sem.at[0]),
        pltpu.make_async_copy(mesh_hbm, mesh_ref, sem.at[1]),
        pltpu.make_async_copy(grid_hbm, grid_ref, sem.at[2]),
        pltpu.make_async_copy(win_hbm, layer_ref.at[0], sem.at[3]),
        pltpu.make_async_copy(wout_hbm, layer_ref.at[1], sem.at[4]),
    ]
    for copy in copies:
        copy.start()
    neighbours = index_ref.shape[0]
    for k in range(neighbours):
        hot_ref[k] = one_hot(index_ref[k : k + 1, :], hot_ref.shape[1])
    copies[0].wait()
    for c in range(padded // CHUNK):
        here = slice(c * CHUNK, (c + 1) * CHUNK)
        cx = band_ref[here, 0:1]
        cy = band_ref[here, 1:2]
        for k in range(neighbours):
            w = cx * pq_ref[k : k + 1, :] + cy * pq_ref[neighbours + k : neighbours + k + 1, :]
            weight_ref[k, here, :] = jnp.maximum(w, 0.0)
    copies[1].wait()
    pack_rows(mesh_ref, state_ref, gp)
    own_mesh(state_ref, hot_ref, weight_ref, part_ref, near_ref)
    copies[2].wait()
    state_ref[bands:, :gp] = jnp.zeros((padded - bands, gp), F32)
    for x in range(rows):
        state_ref[:bands, x * cols : (x + 1) * cols] = grid_ref[pl.ds(x, bands, stride=rows), :]
    own_grid(state_ref, band_ref, sea_ref, speed_ref, part_ref)
    half = pack_ref.shape[1] // 2
    copies[3].wait()
    pack_rows(layer_ref.at[0], pack_ref, 0)
    one, two = pack_ref[:, :half].T.astype(BF16), pack_ref[:, half:].T.astype(BF16)
    win_ref[:half, :] = jnp.where(dr == 0, one, two)
    win_ref[half:, :] = jnp.where(dr == 0, two, one)
    copies[4].wait()
    pack_rows(layer_ref.at[1], pack_ref, 0)
    one, two = pack_ref[:, :half].astype(BF16), pack_ref[:, half:].astype(BF16)
    wout_ref[:, :half] = jnp.where(dr == 0, one, two)
    wout_ref[:, half:] = jnp.where(dr == 0, two, one)


def own_kernel(state_ref, hot_ref, weight_ref, band_ref, sea_ref, speed_ref, part_ref, near_ref):
    own_mesh(state_ref, hot_ref, weight_ref, part_ref, near_ref)
    own_grid(state_ref, band_ref, sea_ref, speed_ref, part_ref)


def halo_kernel(
    part_ref, even_ref, odd_ref, hot_ref, weight_ref, band_ref, sea_ref, speed_ref, win_ref,
    moved_ref, keep_ref, send_ref, ext_ref, near_ref, feat_ref,
):
    neighbours, padded, nodes = weight_ref.shape
    rows, cols = sea_ref.shape
    gp = rows * cols
    listed = even_ref.shape[1] - cols
    even = on_even()
    ext_ref[:, :listed] = jnp.where(even, odd_ref[:, cols:], even_ref[:, cols:])
    ext_ref[:, listed:] = jnp.where(even, even_ref[:, cols:], odd_ref[:, cols:])
    for k in range(neighbours):
        near_ref[k] = dot(ext_ref[...], hot_ref[k, nodes:, :])
    scale = sea_ref[...].astype(F32) * speed_ref[...]
    for c in range(padded // CHUNK):
        here = slice(c * CHUNK, (c + 1) * CHUNK)
        cx = band_ref[here, 0:1]
        a, b = even_ref[here, :cols].astype(F32), odd_ref[here, :cols].astype(F32)
        for x in range(rows):
            cut = slice(x * cols, (x + 1) * cols)
            out = part_ref[here, cut]
            if x == 0:
                out = out + jnp.maximum(cx, 0.0) * scale[x : x + 1, :] * jnp.where(even, b, a)
            if x == rows - 1:
                out = out + jnp.maximum(-cx, 0.0) * scale[x : x + 1, :] * jnp.where(even, a, b)
            moved_ref[here, cut] = out
            feat_ref[here, cut] = out.astype(BF16)
        out = part_ref[here, gp:]
        for k in range(neighbours):
            out = out + weight_ref[k, here, :] * near_ref[k, here, :]
        moved_ref[here, gp:] = out
        feat_ref[here, gp:] = out.astype(BF16)
    half = keep_ref.shape[0]
    keep_ref[...] = dot(win_ref[:half, :], feat_ref[...])
    send_ref[...] = dot(win_ref[half:, :], feat_ref[...]).astype(BF16)


def add_transfer(moved_ref, mine_ref, other_ref, wout_ref, hid_ref, state_ref):
    half = mine_ref.shape[0]
    hid_ref[:half, :] = mine_ref[...]
    hid_ref[half:, :] = other_ref[...]
    state_ref[...] = moved_ref[...] + DT_STEP * dot(wout_ref[...], hid_ref[...])


def next_kernel(
    moved_ref, mine_ref, other_ref, wout_ref, halo_ref, state_ref, even_ref, odd_ref, hid_ref,
    *, grid_points, cols,
):
    add_transfer(moved_ref, mine_ref, other_ref, wout_ref, hid_ref, state_ref)
    messages(
        state_ref[:, grid_points:].astype(BF16),
        state_ref[:, :cols].astype(BF16),
        state_ref[:, grid_points - cols : grid_points].astype(BF16),
        halo_ref,
        even_ref,
        odd_ref,
    )


def slots_kernel(
    gi_ref, gw_ref, gc_ref, gt_ref, mi_ref, mw_ref, mc_ref, mt_ref, after_ref,
    gmix_ref, mmix_ref, sums_ref, gland_ref, mland_ref,
):
    me = lax.axis_index("sp")
    _, _, peers, cap = gi_ref.shape
    groups = (
        (gi_ref, gw_ref, gc_ref, gt_ref, gmix_ref, gland_ref, 0),
        (mi_ref, mw_ref, mc_ref, mt_ref, mmix_ref, mland_ref, 1),
    )
    for index_ref, weight_ref, count_ref, target_ref, mix_ref, land_ref, kind in groups:
        length = mix_ref.shape[0]
        spots = lax.broadcasted_iota(jnp.int32, (length, cap), 0)
        slot = lax.broadcasted_iota(jnp.int32, (1, cap), 1)
        for p in range(peers):
            peer = lax.bitwise_xor(me, p)
            count = jnp.sum(
                jnp.where(
                    lax.broadcasted_iota(jnp.int32, (1, peers), 1) == peer, count_ref[...], 0
                ),
                axis=1,
                keepdims=True,
            )
            live = jnp.where(slot < count, 1.0, 0.0)
            mix = jnp.zeros((length, cap), F32)
            total = jnp.zeros((1, cap), F32)
            for j in range(index_ref.shape[0]):
                scaled = weight_ref[j, 0, pl.ds(peer, 1), :] * live
                mix = mix + jnp.where(spots == index_ref[j, 0, pl.ds(peer, 1), :], scaled, 0.0)
                total = total + scaled
            mix_ref[:, p * cap : (p + 1) * cap] = mix.astype(BF16)
            sums_ref[kind : kind + 1, p * cap : (p + 1) * cap] = total
            land_ref[:, p * cap : (p + 1) * cap] = one_hot(
                target_ref[0, pl.ds(peer, 1), :], land_ref.shape[0]
            )


def slot_values(source_refs, mix_refs, sums_ref, p, cap, bands, out_ref):
    cut = slice(p * cap, (p + 1) * cap)
    for kind in (0, 1):
        value = dot(source_refs[kind], mix_refs[kind][:, cut])
        if bands is not None:
            row = lax.broadcasted_iota(jnp.int32, value.shape, 0)
            value = jnp.where(row == bands, sums_ref[kind : kind + 1, cut], value)
        out_ref[:, kind * cap : (kind + 1) * cap] = value.astype(BF16)


def early_kernel(moved_ref, gmix_ref, mmix_ref, sums_ref, out_ref, *, bands, peer):
    gp = gmix_ref.shape[0]
    cap = out_ref.shape[1] // 2
    parts = (moved_ref[:, :gp].astype(BF16), moved_ref[:, gp:].astype(BF16))
    slot_values(parts, (gmix_ref, mmix_ref), sums_ref, peer, cap, bands, out_ref)


def mix_kernel(
    moved_ref, mine_ref, other_ref, wout_ref, gmix_ref, mmix_ref, sums_ref, state_ref, *rest,
    bands, which,
):
    out_refs, hid_ref = rest[:-1], rest[-1]
    add_transfer(moved_ref, mine_ref, other_ref, wout_ref, hid_ref, state_ref)
    gp = gmix_ref.shape[0]
    cap = out_refs[0].shape[1] // 2
    parts = (state_ref[:, :gp].astype(BF16), state_ref[:, gp:].astype(BF16))
    for p, out_ref in zip(which, out_refs):
        slot_values(parts, (gmix_ref, mmix_ref), sums_ref, p, cap, bands, out_ref)


def silu(total_ref, got_ref):
    total = total_ref[...] + got_ref[...].astype(F32)
    return (total / (1.0 + jnp.exp(-total))).astype(BF16)


def silu_kernel(total_ref, got_ref, *rest):
    rest[-1][...] = silu(total_ref, got_ref)


def silu_mix_kernel(
    total_ref, got_ref, gmix_ref, mmix_ref, after_ref, mine_ref, mixed_ref, *, peer
):
    gp = gmix_ref.shape[0]
    cap = mixed_ref.shape[1] // 2
    mine_ref[...] = silu(total_ref, got_ref)
    parts = (mine_ref[:, :gp], mine_ref[:, gp:])
    slot_values(parts, (gmix_ref, mmix_ref), None, peer, cap, None, mixed_ref)


def join_kernel(early_ref, mine_ref, other_ref, wout_ref, out_ref):
    half = mine_ref.shape[0]
    moved = dot(wout_ref[:, :half], mine_ref[...]) + dot(wout_ref[:, half:], other_ref[...])
    out_ref[...] = (early_ref[...].astype(F32) + DT_STEP * moved).astype(BF16)


def land(values, land_ref):
    return lax.dot_general(
        values, land_ref[...], (((1,), (1,)), ((), ())), preferred_element_type=F32
    )


def end_kernel(state_ref, gland_ref, mland_ref, sea_ref, *rest, bands):
    got_refs, rest = rest[-8::-1], rest[-7:]
    grid_hbm, mesh_hbm, values_ref, sum_ref, grid_ref, mesh_ref, sem = rest
    rows, cols = sea_ref.shape
    gp = rows * cols
    freqs, dirs, _ = mesh_ref.shape
    cap = got_refs[0].shape[1] // 2
    for kind in (0, 1):
        for p, got in enumerate(got_refs):
            values_ref[kind, :, p * cap : (p + 1) * cap] = got[:, kind * cap : (kind + 1) * cap]
    sum_ref[:, gp:] = land(values_ref[0], gland_ref)
    cover = sum_ref[bands : bands + 1, gp:]
    rate = BLEND_RATE / (1.0 + cover)
    keep = 1.0 - rate * cover
    for f in range(freqs):
        here = slice(f * dirs, (f + 1) * dirs)
        mesh_ref[f] = keep * state_ref[here, gp:] + rate * sum_ref[here, gp:]
    mesh_copy = pltpu.make_async_copy(mesh_ref, mesh_hbm, sem.at[0])
    mesh_copy.start()
    sum_ref[:, :gp] = land(values_ref[1], mland_ref)
    cover = sum_ref[bands : bands + 1, :gp]
    rate = BLEND_RATE / (1.0 + cover)
    keep = 1.0 - rate * cover
    sea = sea_ref[...].astype(F32)
    for x in range(rows):
        cut = slice(x * cols, (x + 1) * cols)
        wet = sea[x : x + 1, :]
        out = keep[:, cut] * wet * state_ref[:bands, cut] + rate[:, cut] * wet * sum_ref[:bands, cut]
        grid_ref[pl.ds(x, bands, stride=rows), :] = out
    grid_copy = pltpu.make_async_copy(grid_ref, grid_hbm, sem.at[1])
    grid_copy.start()
    mesh_copy.wait()
    grid_copy.wait()


def band_table(freqs, dirs, n_fr, n_dr, padded):
    speed = (0.7 * np.power(np.float32(1.1), -np.arange(freqs * n_fr, dtype=np.float32))).astype(np.float32)
    total = dirs * n_dr
    heading = (2.0 * np.pi * (np.arange(total, dtype=np.float64) + 0.5) / total)
    table = np.zeros((n_fr, n_dr, padded, 2), np.float32)
    for i in range(n_fr):
        for j in range(n_dr):
            s = speed[i * freqs : (i + 1) * freqs, None]
            h = heading[None, j * dirs : (j + 1) * dirs]
            table[i, j, : freqs * dirs, 0] = (s * np.cos(h)).reshape(-1)
            table[i, j, : freqs * dirs, 1] = (s * np.sin(h)).reshape(-1)
    return table


def core_swap(array):
    return lax.ppermute(array, "dr", [(0, 1), (1, 0)])


def per_device(
    grid_spec, mesh_spec, grid_sea, grid_speed, nb_index, nb_angle, nb_coef, halo_list, w_in, w_out,
    g2m_index, g2m_weight, g2m_count, g2m_target, m2g_index, m2g_weight, m2g_count, m2g_target,
):
    freqs, dirs, rows, cols = grid_spec.shape
    nodes = mesh_spec.shape[2]
    listed = halo_list.shape[1]
    hid = w_in.shape[2]
    half = hid // 2
    bands = freqs * dirs
    padded = (bands // CHUNK + 1) * CHUNK
    gp = rows * cols
    points = gp + nodes
    neighbours = nb_index.shape[0]
    peers, cap = g2m_index.shape[2:]
    n_fr, n_dr = lax.axis_size("fr"), lax.axis_size("dr")

    message = ((padded, cols + listed), BF16)
    state_shape = ((padded, points), F32)
    half_shape = (half, points)
    hid_scratch = ((hid, points), BF16)
    near_scratch = ((neighbours, padded, nodes), F32)
    grid_flat = grid_spec.reshape(bands * rows, cols)
    even, odd = kernel_call(
        functools.partial(begin_kernel, rows=rows),
        [message, message],
        [
            (grid_flat.shape, F32),
            (mesh_spec.shape, F32),
            (halo_list.shape, jnp.int32),
            ((padded, nodes), F32),
            pltpu.SemaphoreType.DMA((3,)),
        ],
        flops=2 * padded * nodes * 2 * listed,
        spaces=[HBM] * 3,
    )(grid_flat, mesh_spec, halo_list)

    table = jnp.asarray(band_table(freqs, dirs, n_fr, n_dr, padded))
    pq = jnp.concatenate([-nb_coef * jnp.cos(nb_angle), -nb_coef * jnp.sin(nb_angle)], axis=0)
    for substep in range(NSUB):
        from_even = pair_swap(even, "sp", 0)
        from_odd = pair_swap(odd, "sp", 1)
        own_flops = 2 * padded * neighbours * nodes * nodes
        if substep == 0:
            part, hot, weight, band, win, wout = kernel_call(
                prepare_kernel,
                [
                    state_shape,
                    ((neighbours, nodes + 2 * listed, nodes), BF16),
                    near_scratch,
                    ((padded, 2), F32),
                    ((hid, padded), BF16),
                    ((padded, hid), BF16),
                ],
                [
                    (grid_flat.shape, F32),
                    (mesh_spec.shape, F32),
                    ((2,) + w_in.shape, BF16),
                    state_shape,
                    near_scratch,
                    ((padded, hid), F32),
                    pltpu.SemaphoreType.DMA((5,)),
                ],
                flops=3 * own_flops,
                spaces=[HBM] * 5 + [VMEM] * 4,
            )(
                grid_flat, mesh_spec, table, w_in, jnp.transpose(w_out, (1, 2, 0)),
                nb_index, pq, grid_sea, grid_speed,
            )
        else:
            (part,) = kernel_call(own_kernel, [state_shape], [near_scratch], flops=own_flops)(
                state, hot, weight, band, grid_sea, grid_speed
            )
        moved, total, send = kernel_call(
            halo_kernel,
            [state_shape, (half_shape, F32), (half_shape, BF16)],
            [((padded, 2 * listed), BF16), near_scratch, ((padded, points), BF16)],
            flops=2 * padded * (neighbours * nodes * 2 * listed + hid * points),
        )(part, from_even, from_odd, hot, weight, band, grid_sea, grid_speed, win)

        total = total + core_swap(send).astype(F32)
        rounded = total.astype(BF16)
        got = peer_swap(rounded, "fr", 1)
        step = 2
        while step < n_fr:
            total = total + got.astype(F32)
            rounded = total.astype(BF16)
            got = peer_swap(rounded, "fr", step)
            step *= 2
        extra = []
        if substep == 0:
            gmix, mmix, sums, gland, mland = kernel_call(
                slots_kernel,
                [
                    ((gp, peers * cap), BF16),
                    ((nodes, peers * cap), BF16),
                    ((2, peers * cap), F32),
                    ((nodes, peers * cap), BF16),
                    ((gp, peers * cap), BF16),
                ],
                flops=2 << 30,
                spaces=[VMEM] * 8 + [pl.ANY],
            )(
                g2m_index, g2m_weight, g2m_count, g2m_target,
                m2g_index, m2g_weight, m2g_count, m2g_target, rounded,
            )
            extra = [sums]
        if substep < NSUB - 1:
            (mine,) = kernel_call(
                silu_kernel, [(half_shape, BF16)], spaces=[VMEM, VMEM] + [pl.ANY] * len(extra)
            )(total, got, *extra)
            other = core_swap(mine)
            state, even, odd = kernel_call(
                functools.partial(next_kernel, grid_points=gp, cols=cols),
                [state_shape, message, message],
                [hid_scratch],
                flops=2 * padded * hid * points,
            )(moved, mine, other, wout, halo_list)

    split = peers // 2
    slot_shape = ((padded, 2 * cap), BF16)
    (early,) = kernel_call(
        functools.partial(early_kernel, bands=bands, peer=split),
        [slot_shape],
        flops=2 * padded * points * cap,
    )(moved, gmix, mmix, sums)
    early = peer_swap(early, "sp", split)
    mine, mixed = kernel_call(
        functools.partial(silu_mix_kernel, peer=split),
        [(half_shape, BF16), ((half, 2 * cap), BF16)],
        flops=2 * half * points * cap,
        spaces=[VMEM] * 4 + [pl.ANY],
    )(total, got, gmix, mmix, early)
    other = core_swap(mine)
    mixed = peer_swap(mixed, "sp", split)
    which = [p for p in range(peers) if p != split]
    state, *values = kernel_call(
        functools.partial(mix_kernel, bands=bands, which=which),
        [state_shape] + [slot_shape] * len(which),
        [hid_scratch],
        flops=2 * padded * (hid * points + points * len(which) * cap),
    )(moved, mine, other, wout, gmix, mmix, sums)
    values = dict(zip(which, values))
    mixed, state = lax.optimization_barrier((mixed, state))
    for p in which[1:]:
        values[p] = peer_swap(values[p], "sp", p)
    (values[split],) = kernel_call(join_kernel, [slot_shape], flops=900 << 20)(
        early, mixed, core_swap(mixed), wout
    )
    values = [values[p] for p in range(peers)]
    grid_out, mesh_out = kernel_call(
        functools.partial(end_kernel, bands=bands),
        [(grid_flat.shape, F32), (mesh_spec.shape, F32)],
        [
            ((2, padded, peers * cap), BF16),
            state_shape,
            (grid_flat.shape, F32),
            (mesh_spec.shape, F32),
            pltpu.SemaphoreType.DMA((2,)),
        ],
        flops=2 * padded * points * peers * cap,
        out_space=pl.ANY,
    )(state, gland, mland, grid_sea, *values[::-1])
    return grid_out.reshape(grid_spec.shape), mesh_out


def solution(mesh):
    return jax.shard_map(
        per_device,
        mesh=mesh,
        in_specs=(
            P("fr", "dr", ("grp", "sp"), None),
            P("fr", "dr", ("grp", "sp")),
            P(("grp", "sp"), None),
            P(("grp", "sp"), None),
            P(None, ("grp", "sp")),
            P(None, ("grp", "sp")),
            P(None, ("grp", "sp")),
            P(None, ("grp", "sp")),
            P("fr", "dr", None),
            P(None, "fr", "dr"),
            P(None, ("grp", "sp"), None, None),
            P(None, ("grp", "sp"), None, None),
            P(("grp", "sp"), None),
            P(("grp", "sp"), None, None),
            P(None, ("grp", "sp"), None, None),
            P(None, ("grp", "sp"), None, None),
            P(("grp", "sp"), None),
            P(("grp", "sp"), None, None),
        ),
        out_specs=(P("fr", "dr", ("grp", "sp"), None), P("fr", "dr", ("grp", "sp"))),
        check_vma=False,
    )
```

```python
import functools

import jax
import jax.numpy as jnp
import numpy as np
from jax import lax
from jax.experimental import pallas as pl
from jax.experimental.pallas import tpu as pltpu
from jax.sharding import PartitionSpec as P

NSUB = 2
DT_STEP = 0.1
BLEND_RATE = 0.5
F32 = jnp.float32
BF16 = jnp.bfloat16
CHUNK = 16
FLOPS_PER_US = 1.15e9


VMEM = pltpu.MemorySpace.VMEM
HBM = pltpu.MemorySpace.HBM


def kernel_call(body, outs, scratch, expected_us, spaces=None, out_space=VMEM):
    def run(*args):
        where = spaces or [VMEM] * len(args)
        args = [
            pltpu.with_memory_space_constraint(a, HBM) if space == HBM else a
            for a, space in zip(args, where)
        ]
        return pl.pallas_call(
            body,
            out_shape=[jax.ShapeDtypeStruct(s, t) for s, t in outs],
            in_specs=[pl.BlockSpec(memory_space=space) for space in where],
            out_specs=[pl.BlockSpec(memory_space=out_space)] * len(outs),
            scratch_shapes=[s if hasattr(s, "dtype") else pltpu.VMEM(*s) for s in scratch],
            compiler_params=pltpu.CompilerParams(vmem_limit_bytes=16 << 20),
            cost_estimate=pl.CostEstimate(
                flops=int(expected_us * FLOPS_PER_US), bytes_accessed=0, transcendentals=0
            ),
        )(*args)

    return run


def dot(a, b):
    return jnp.dot(a, b, preferred_element_type=F32)


def one_hot(row, length):
    spots = lax.broadcasted_iota(jnp.int32, (length, row.shape[1]), 0)
    return jnp.where(spots == row, 1.0, 0.0).astype(BF16)


def pair_swap(array, axis, first):
    size = lax.axis_size(axis)
    pairs = [(i, i + 1) for i in range(first, size - 1, 2)]
    return lax.ppermute(array, axis, pairs + [(j, i) for i, j in pairs])


def peer_swap(array, axis, step):
    size = lax.axis_size(axis)
    return lax.ppermute(array, axis, [(i, i ^ step) for i in range(size)])


def on_even():
    return lax.rem(lax.axis_index("sp"), 2) == 0


def messages(mesh, low_row, high_row, halo_ref, even_ref, odd_ref):
    even = on_even()
    nodes = mesh.shape[1]
    cols = low_row.shape[1]
    to_lower = dot(mesh, one_hot(halo_ref[0:1, :], nodes)).astype(BF16)
    to_upper = dot(mesh, one_hot(halo_ref[1:2, :], nodes)).astype(BF16)
    even_ref[:, :cols] = jnp.where(even, high_row, low_row)
    odd_ref[:, :cols] = jnp.where(even, low_row, high_row)
    even_ref[:, cols:] = jnp.where(even, to_upper, to_lower)
    odd_ref[:, cols:] = jnp.where(even, to_lower, to_upper)


def pack_rows(source_ref, packed_ref, at):
    freqs, dirs, width = source_ref.shape
    for f in range(freqs):
        packed_ref[f * dirs : (f + 1) * dirs, at : at + width] = source_ref[f].astype(F32)
    packed_ref[freqs * dirs :, at : at + width] = jnp.zeros(
        (packed_ref.shape[0] - freqs * dirs, width), F32
    )


def begin_kernel(
    grid_hbm, mesh_hbm, halo_hbm, even_ref, odd_ref, grid_ref, mesh_ref, halo_ref, packed_ref, sem,
    *, rows,
):
    copies = [
        pltpu.make_async_copy(halo_hbm, halo_ref, sem.at[0]),
        pltpu.make_async_copy(mesh_hbm, mesh_ref, sem.at[1]),
        pltpu.make_async_copy(grid_hbm, grid_ref, sem.at[2]),
    ]
    for copy in copies:
        copy.start()
    bands = grid_ref.shape[0] // rows
    blank = jnp.zeros((packed_ref.shape[0] - bands, grid_ref.shape[1]), F32)
    copies[0].wait()
    copies[1].wait()
    pack_rows(mesh_ref, packed_ref, 0)
    copies[2].wait()
    low = jnp.concatenate([grid_ref[pl.ds(0, bands, stride=rows), :], blank], axis=0)
    high = jnp.concatenate([grid_ref[pl.ds(rows - 1, bands, stride=rows), :], blank], axis=0)
    messages(
        packed_ref[...].astype(BF16), low.astype(BF16), high.astype(BF16), halo_ref, even_ref, odd_ref
    )


def own_grid(state_ref, band_ref, sea_ref, speed_ref, part_ref):
    rows, cols = sea_ref.shape
    sea = sea_ref[...].astype(F32)
    lane = lax.broadcasted_iota(jnp.int32, (CHUNK, cols), 1)
    for c in range(state_ref.shape[0] // CHUNK):
        here = slice(c * CHUNK, (c + 1) * CHUNK)
        cx = band_ref[here, 0:1]
        cy = band_ref[here, 1:2]
        for x in range(rows):
            g = state_ref[here, x * cols : (x + 1) * cols]
            low = 0.0 if x == 0 else state_ref[here, (x - 1) * cols : x * cols]
            high = 0.0 if x == rows - 1 else state_ref[here, (x + 1) * cols : (x + 2) * cols]
            west = jnp.where(lane == 0, 0.0, pltpu.roll(g, 1, 1))
            east = jnp.where(lane == cols - 1, 0.0, pltpu.roll(g, cols - 1, 1))
            out = g - jnp.abs(cx) * speed_ref[x : x + 1, :] * (g - jnp.where(cx > 0, low, high))
            out = out - jnp.abs(cy) * speed_ref[x : x + 1, :] * (g - jnp.where(cy > 0, west, east))
            part_ref[here, x * cols : (x + 1) * cols] = out * sea[x : x + 1, :]


def own_mesh(mesh, hot_ref, weight_ref, mesh_ref, part_ref, near_ref):
    neighbours, padded, nodes = weight_ref.shape
    for k in range(neighbours):
        near_ref[k] = dot(mesh, hot_ref[k, :nodes, :])
    for c in range(padded // CHUNK):
        here = slice(c * CHUNK, (c + 1) * CHUNK)
        e = mesh_ref[here, :]
        out = e
        for k in range(neighbours):
            out = out + weight_ref[k, here, :] * (near_ref[k, here, :] - e)
        part_ref[here, :] = out


def prepare_kernel(
    grid_hbm, mesh_hbm, table_hbm, win_hbm, wout_hbm, index_ref, pq_ref, sea_ref, speed_ref,
    gpart_ref, mpart_ref, hot_ref, weight_ref, band_ref, win_ref, wout_ref,
    grid_ref, mesh_ref, layer_ref, gstate_ref, mstate_ref, near_ref, pack_ref, sem,
):
    fr, dr = lax.axis_index("fr"), lax.axis_index("dr")
    rows, cols = sea_ref.shape
    padded = gstate_ref.shape[0]
    bands = grid_ref.shape[0] // rows
    copies = [
        pltpu.make_async_copy(table_hbm.at[fr, dr], band_ref, sem.at[0]),
        pltpu.make_async_copy(mesh_hbm, mesh_ref, sem.at[1]),
        pltpu.make_async_copy(grid_hbm, grid_ref, sem.at[2]),
        pltpu.make_async_copy(win_hbm, layer_ref.at[0], sem.at[3]),
        pltpu.make_async_copy(wout_hbm, layer_ref.at[1], sem.at[4]),
    ]
    for copy in copies:
        copy.start()
    neighbours = index_ref.shape[0]
    for k in range(neighbours):
        hot_ref[k] = one_hot(index_ref[k : k + 1, :], hot_ref.shape[1])
    copies[0].wait()
    for c in range(padded // CHUNK):
        here = slice(c * CHUNK, (c + 1) * CHUNK)
        cx = band_ref[here, 0:1]
        cy = band_ref[here, 1:2]
        for k in range(neighbours):
            w = cx * pq_ref[k : k + 1, :] + cy * pq_ref[neighbours + k : neighbours + k + 1, :]
            weight_ref[k, here, :] = jnp.maximum(w, 0.0)
    copies[1].wait()
    pack_rows(mesh_ref, mstate_ref, 0)
    own_mesh(mstate_ref[...].astype(BF16), hot_ref, weight_ref, mstate_ref, mpart_ref, near_ref)
    copies[2].wait()
    gstate_ref[bands:, :] = jnp.zeros((padded - bands, gstate_ref.shape[1]), F32)
    for x in range(rows):
        gstate_ref[:bands, x * cols : (x + 1) * cols] = grid_ref[pl.ds(x, bands, stride=rows), :]
    own_grid(gstate_ref, band_ref, sea_ref, speed_ref, gpart_ref)
    half = pack_ref.shape[1] // 2
    copies[3].wait()
    pack_rows(layer_ref.at[0], pack_ref, 0)
    one, two = pack_ref[:, :half].T.astype(BF16), pack_ref[:, half:].T.astype(BF16)
    win_ref[:half, :] = jnp.where(dr == 0, one, two)
    win_ref[half:, :] = jnp.where(dr == 0, two, one)
    copies[4].wait()
    pack_rows(layer_ref.at[1], pack_ref, 0)
    one, two = pack_ref[:, :half].astype(BF16), pack_ref[:, half:].astype(BF16)
    wout_ref[:, :half] = jnp.where(dr == 0, one, two)
    wout_ref[:, half:] = jnp.where(dr == 0, two, one)


def own_mesh_kernel(state_ref, hot_ref, weight_ref, part_ref, near_ref):
    own_mesh(state_ref[...].astype(BF16), hot_ref, weight_ref, state_ref, part_ref, near_ref)


def first_layer(win_ref, feat_ref, keep_ref, send_ref):
    half = keep_ref.shape[0]
    send_ref[...] = dot(win_ref[half:, :], feat_ref[...]).astype(BF16)
    keep_ref[...] = dot(win_ref[:half, :], feat_ref[...])


def halo_grid_kernel(
    part_ref, even_ref, odd_ref, band_ref, sea_ref, speed_ref, win_ref,
    moved_ref, keep_ref, send_ref, feat_ref,
):
    rows, cols = sea_ref.shape
    even = on_even()
    scale = sea_ref[...].astype(F32) * speed_ref[...]
    for c in range(part_ref.shape[0] // CHUNK):
        here = slice(c * CHUNK, (c + 1) * CHUNK)
        cx = band_ref[here, 0:1]
        a, b = even_ref[here, :cols].astype(F32), odd_ref[here, :cols].astype(F32)
        for x in range(rows):
            cut = slice(x * cols, (x + 1) * cols)
            out = part_ref[here, cut]
            if x == 0:
                out = out + jnp.maximum(cx, 0.0) * scale[x : x + 1, :] * jnp.where(even, b, a)
            if x == rows - 1:
                out = out + jnp.maximum(-cx, 0.0) * scale[x : x + 1, :] * jnp.where(even, a, b)
            moved_ref[here, cut] = out
            feat_ref[here, cut] = out.astype(BF16)
    first_layer(win_ref, feat_ref, keep_ref, send_ref)


def halo_mesh_kernel(
    part_ref, even_ref, odd_ref, hot_ref, weight_ref, win_ref, after_ref,
    moved_ref, keep_ref, send_ref, ext_ref, near_ref, feat_ref,
):
    neighbours, padded, nodes = weight_ref.shape
    listed = ext_ref.shape[1] // 2
    first = even_ref.shape[1] - listed
    even = on_even()
    ext_ref[:, :listed] = jnp.where(even, odd_ref[:, first:], even_ref[:, first:])
    ext_ref[:, listed:] = jnp.where(even, even_ref[:, first:], odd_ref[:, first:])
    for k in range(neighbours):
        near_ref[k] = dot(ext_ref[...], hot_ref[k, nodes:, :])
    for c in range(padded // CHUNK):
        here = slice(c * CHUNK, (c + 1) * CHUNK)
        out = part_ref[here, :]
        for k in range(neighbours):
            out = out + weight_ref[k, here, :] * near_ref[k, here, :]
        moved_ref[here, :] = out
        feat_ref[here, :] = out.astype(BF16)
    first_layer(win_ref, feat_ref, keep_ref, send_ref)


def transferred(moved_ref, mine_ref, other_ref, wout_ref, hid_ref):
    half = mine_ref.shape[0]
    hid_ref[:half, :] = mine_ref[...]
    hid_ref[half:, :] = other_ref[...]
    return moved_ref[...] + DT_STEP * dot(wout_ref[...], hid_ref[...])


def next_grid_kernel(
    moved_ref, mine_ref, other_ref, wout_ref, state_ref, even_ref, odd_ref, hid_ref
):
    state_ref[...] = transferred(moved_ref, mine_ref, other_ref, wout_ref, hid_ref)
    even = on_even()
    cols = even_ref.shape[1]
    low, high = state_ref[:, :cols], state_ref[:, state_ref.shape[1] - cols :]
    even_ref[...] = jnp.where(even, high, low).astype(BF16)
    odd_ref[...] = jnp.where(even, low, high).astype(BF16)


def next_mesh_kernel(
    moved_ref, mine_ref, other_ref, wout_ref, halo_ref, state_ref, even_ref, odd_ref, hid_ref
):
    state_ref[...] = transferred(moved_ref, mine_ref, other_ref, wout_ref, hid_ref)
    even = on_even()
    mesh = state_ref[...].astype(BF16)
    nodes = mesh.shape[1]
    to_lower = dot(mesh, one_hot(halo_ref[0:1, :], nodes))
    to_upper = dot(mesh, one_hot(halo_ref[1:2, :], nodes))
    even_ref[...] = jnp.where(even, to_upper, to_lower).astype(BF16)
    odd_ref[...] = jnp.where(even, to_lower, to_upper).astype(BF16)


def state_kernel(moved_ref, mine_ref, other_ref, wout_ref, state_ref, hid_ref):
    state_ref[...] = transferred(moved_ref, mine_ref, other_ref, wout_ref, hid_ref)


def slots_kernel(
    gi_ref, gw_ref, gc_ref, gt_ref, mi_ref, mw_ref, mc_ref, mt_ref, after_ref,
    gmix_ref, mmix_ref, sums_ref, gland_ref, mland_ref,
):
    me = lax.axis_index("sp")
    _, _, peers, cap = gi_ref.shape
    groups = (
        (gi_ref, gw_ref, gc_ref, gt_ref, gmix_ref, gland_ref, 0),
        (mi_ref, mw_ref, mc_ref, mt_ref, mmix_ref, mland_ref, 1),
    )
    for index_ref, weight_ref, count_ref, target_ref, mix_ref, land_ref, kind in groups:
        length = mix_ref.shape[0]
        spots = lax.broadcasted_iota(jnp.int32, (length, cap), 0)
        slot = lax.broadcasted_iota(jnp.int32, (1, cap), 1)
        for p in range(peers):
            peer = lax.bitwise_xor(me, p)
            count = jnp.sum(
                jnp.where(
                    lax.broadcasted_iota(jnp.int32, (1, peers), 1) == peer, count_ref[...], 0
                ),
                axis=1,
                keepdims=True,
            )
            live = jnp.where(slot < count, 1.0, 0.0)
            mix = jnp.zeros((length, cap), F32)
            total = jnp.zeros((1, cap), F32)
            for j in range(index_ref.shape[0]):
                scaled = weight_ref[j, 0, pl.ds(peer, 1), :] * live
                mix = mix + jnp.where(spots == index_ref[j, 0, pl.ds(peer, 1), :], scaled, 0.0)
                total = total + scaled
            mix_ref[:, p * cap : (p + 1) * cap] = mix.astype(BF16)
            sums_ref[kind : kind + 1, p * cap : (p + 1) * cap] = total
            land_ref[:, p * cap : (p + 1) * cap] = one_hot(
                target_ref[0, pl.ds(peer, 1), :], land_ref.shape[0]
            )


def slot_values(source_refs, mix_refs, sums_ref, p, cap, bands, out_ref):
    cut = slice(p * cap, (p + 1) * cap)
    for kind in (0, 1):
        value = dot(source_refs[kind][...], mix_refs[kind][:, cut])
        if bands is not None:
            row = lax.broadcasted_iota(jnp.int32, value.shape, 0)
            value = jnp.where(row == bands, sums_ref[kind : kind + 1, cut], value)
        out_ref[:, kind * cap : (kind + 1) * cap] = value.astype(BF16)


def early_kernel(grid_ref, mesh_ref, gmix_ref, mmix_ref, sums_ref, out_ref, *, bands, peer):
    cap = out_ref.shape[1] // 2
    parts = (grid_ref[...].astype(BF16), mesh_ref[...].astype(BF16))
    slot_values(parts, (gmix_ref, mmix_ref), sums_ref, peer, cap, bands, out_ref)


def mix_kernel(
    grid_ref, moved_ref, mine_ref, other_ref, wout_ref, gmix_ref, mmix_ref, sums_ref, state_ref,
    *rest, bands, which,
):
    out_refs, hid_ref = rest[:-1], rest[-1]
    state_ref[...] = transferred(moved_ref, mine_ref, other_ref, wout_ref, hid_ref)
    cap = out_refs[0].shape[1] // 2
    parts = (grid_ref[...].astype(BF16), state_ref[...].astype(BF16))
    for p, out_ref in zip(which, out_refs):
        slot_values(parts, (gmix_ref, mmix_ref), sums_ref, p, cap, bands, out_ref)


def silu(total_ref, got_ref):
    total = total_ref[...] + got_ref[...].astype(F32)
    return (total / (1.0 + jnp.exp(-total))).astype(BF16)


def silu_kernel(total_ref, got_ref, *rest):
    rest[-1][...] = silu(total_ref, got_ref)


def silu_mix_kernel(
    total_ref, got_ref, grid_ref, gmix_ref, mmix_ref, after_ref, mine_ref, mixed_ref, *, peer
):
    cap = mixed_ref.shape[1] // 2
    mine_ref[...] = silu(total_ref, got_ref)
    slot_values((grid_ref, mine_ref[...]), (gmix_ref, mmix_ref), None, peer, cap, None, mixed_ref)


def join_kernel(early_ref, mine_ref, other_ref, wout_ref, out_ref):
    half = mine_ref.shape[0]
    moved = dot(wout_ref[:, :half], mine_ref[...]) + dot(wout_ref[:, half:], other_ref[...])
    out_ref[...] = (early_ref[...].astype(F32) + DT_STEP * moved).astype(BF16)


def land(values, land_ref):
    return lax.dot_general(
        values, land_ref[...], (((1,), (1,)), ((), ())), preferred_element_type=F32
    )


def end_kernel(gstate_ref, mstate_ref, gland_ref, mland_ref, sea_ref, *rest, bands):
    got_refs, rest = rest[-8::-1], rest[-7:]
    grid_hbm, mesh_hbm, values_ref, sum_ref, grid_ref, mesh_ref, sem = rest
    rows, cols = sea_ref.shape
    gp = rows * cols
    freqs, dirs, _ = mesh_ref.shape
    cap = got_refs[0].shape[1] // 2
    for kind in (0, 1):
        for p, got in enumerate(got_refs):
            values_ref[kind, :, p * cap : (p + 1) * cap] = got[:, kind * cap : (kind + 1) * cap]
    sum_ref[:, gp:] = land(values_ref[0], gland_ref)
    cover = sum_ref[bands : bands + 1, gp:]
    rate = BLEND_RATE / (1.0 + cover)
    keep = 1.0 - rate * cover
    for f in range(freqs):
        here = slice(f * dirs, (f + 1) * dirs)
        mesh_ref[f] = keep * mstate_ref[here, :] + rate * sum_ref[here, gp:]
    mesh_copy = pltpu.make_async_copy(mesh_ref, mesh_hbm, sem.at[0])
    mesh_copy.start()
    sum_ref[:, :gp] = land(values_ref[1], mland_ref)
    cover = sum_ref[bands : bands + 1, :gp]
    rate = BLEND_RATE / (1.0 + cover)
    keep = 1.0 - rate * cover
    sea = sea_ref[...].astype(F32)
    for x in range(rows):
        cut = slice(x * cols, (x + 1) * cols)
        wet = sea[x : x + 1, :]
        out = keep[:, cut] * wet * gstate_ref[:bands, cut] + rate[:, cut] * wet * sum_ref[:bands, cut]
        grid_ref[pl.ds(x, bands, stride=rows), :] = out
    grid_copy = pltpu.make_async_copy(grid_ref, grid_hbm, sem.at[1])
    grid_copy.start()
    mesh_copy.wait()
    grid_copy.wait()


def band_table(freqs, dirs, n_fr, n_dr, padded):
    speed = (0.7 * np.power(np.float32(1.1), -np.arange(freqs * n_fr, dtype=np.float32))).astype(np.float32)
    total = dirs * n_dr
    heading = (2.0 * np.pi * (np.arange(total, dtype=np.float64) + 0.5) / total)
    table = np.zeros((n_fr, n_dr, padded, 2), np.float32)
    for i in range(n_fr):
        for j in range(n_dr):
            s = speed[i * freqs : (i + 1) * freqs, None]
            h = heading[None, j * dirs : (j + 1) * dirs]
            table[i, j, : freqs * dirs, 0] = (s * np.cos(h)).reshape(-1)
            table[i, j, : freqs * dirs, 1] = (s * np.sin(h)).reshape(-1)
    return table


def core_swap(array):
    return lax.ppermute(array, "dr", [(0, 1), (1, 0)])


def per_device(
    grid_spec, mesh_spec, grid_sea, grid_speed, nb_index, nb_angle, nb_coef, halo_list, w_in, w_out,
    g2m_index, g2m_weight, g2m_count, g2m_target, m2g_index, m2g_weight, m2g_count, m2g_target,
):
    freqs, dirs, rows, cols = grid_spec.shape
    nodes = mesh_spec.shape[2]
    listed = halo_list.shape[1]
    hid = w_in.shape[2]
    half = hid // 2
    bands = freqs * dirs
    padded = (bands // CHUNK + 1) * CHUNK
    gp = rows * cols
    points = gp + nodes
    neighbours = nb_index.shape[0]
    peers, cap = g2m_index.shape[2:]
    n_fr, n_dr = lax.axis_size("fr"), lax.axis_size("dr")

    message = ((padded, cols + listed), BF16)
    grid_shape = ((padded, gp), F32)
    mesh_shape = ((padded, nodes), F32)
    near_scratch = ((neighbours, padded, nodes), F32)
    grid_flat = grid_spec.reshape(bands * rows, cols)
    even, odd = kernel_call(
        functools.partial(begin_kernel, rows=rows),
        [message, message],
        [
            (grid_flat.shape, F32),
            (mesh_spec.shape, F32),
            (halo_list.shape, jnp.int32),
            mesh_shape,
            pltpu.SemaphoreType.DMA((3,)),
        ],
        1.8,
        spaces=[HBM] * 3,
    )(grid_flat, mesh_spec, halo_list)
    table = jnp.asarray(band_table(freqs, dirs, n_fr, n_dr, padded))
    pq = jnp.concatenate([-nb_coef * jnp.cos(nb_angle), -nb_coef * jnp.sin(nb_angle)], axis=0)
    from_even = pair_swap(even, "sp", 0)
    from_odd = pair_swap(odd, "sp", 1)
    gfrom, mfrom = (from_even, from_odd), (from_even, from_odd)
    gpart, mpart, hot, weight, band, win, wout = kernel_call(
        prepare_kernel,
        [
            grid_shape,
            mesh_shape,
            ((neighbours, nodes + 2 * listed, nodes), BF16),
            near_scratch,
            ((padded, 2), F32),
            ((hid, padded), BF16),
            ((padded, hid), BF16),
        ],
        [
            (grid_flat.shape, F32),
            (mesh_spec.shape, F32),
            ((2,) + w_in.shape, BF16),
            grid_shape,
            mesh_shape,
            near_scratch,
            ((padded, hid), F32),
            pltpu.SemaphoreType.DMA((5,)),
        ],
        3.4,
        spaces=[HBM] * 5 + [VMEM] * 4,
    )(
        grid_flat, mesh_spec, table, w_in, jnp.transpose(w_out, (1, 2, 0)),
        nb_index, pq, grid_sea, grid_speed,
    )

    def summed(total, send):
        total = total + core_swap(send).astype(F32)
        rounded = total.astype(BF16)
        got = peer_swap(rounded, "fr", 1)
        step = 2
        while step < n_fr:
            total = total + got.astype(F32)
            rounded = total.astype(BF16)
            got = peer_swap(rounded, "fr", step)
            step *= 2
        return total, rounded, got

    def activated(total, got, *after):
        (mine,) = kernel_call(
            silu_kernel, [(total.shape, BF16)], (), 0.1, spaces=[VMEM] * 2 + [pl.ANY] * len(after)
        )(total, got, *after)
        return mine

    for substep in range(NSUB):
        gmoved, gtotal, gsend = kernel_call(
            halo_grid_kernel,
            [grid_shape, ((half, gp), F32), ((half, gp), BF16)],
            [((padded, gp), BF16)],
            0.4,
        )(gpart, *gfrom, band, grid_sea, grid_speed, win)
        gtotal, ground, ggot = summed(gtotal, gsend)
        mmoved, mtotal, msend = kernel_call(
            halo_mesh_kernel,
            [mesh_shape, ((half, nodes), F32), ((half, nodes), BF16)],
            [((padded, 2 * listed), BF16), near_scratch, ((padded, nodes), BF16)],
            0.8,
            spaces=[VMEM] * 6 + [pl.ANY],
        )(mpart, *mfrom, hot, weight, win, gsend)
        mtotal, mround, mgot = summed(mtotal, msend)
        if substep < NSUB - 1:
            gmix, mmix, sums, gland, mland = kernel_call(
                slots_kernel,
                [
                    ((gp, peers * cap), BF16),
                    ((nodes, peers * cap), BF16),
                    ((2, peers * cap), F32),
                    ((nodes, peers * cap), BF16),
                    ((gp, peers * cap), BF16),
                ],
                (),
                0.5,
                spaces=[VMEM] * 8 + [pl.ANY],
            )(
                g2m_index, g2m_weight, g2m_count, g2m_target,
                m2g_index, m2g_weight, m2g_count, m2g_target, ground,
            )
            gmine = activated(gtotal, ggot, sums)
            gstate, even, odd = kernel_call(
                next_grid_kernel,
                [grid_shape, ((padded, cols), BF16), ((padded, cols), BF16)],
                [((hid, gp), BF16)],
                0.4,
            )(gmoved, gmine, core_swap(gmine), wout)
            gfrom = (pair_swap(even, "sp", 0), pair_swap(odd, "sp", 1))
            (gpart,) = kernel_call(own_grid, [grid_shape], (), 0.5)(
                gstate, band, grid_sea, grid_speed
            )
            mmine = activated(mtotal, mgot)
            mstate, even, odd = kernel_call(
                next_mesh_kernel,
                [mesh_shape, ((padded, listed), BF16), ((padded, listed), BF16)],
                [((hid, nodes), BF16)],
                0.5,
            )(mmoved, mmine, core_swap(mmine), wout, halo_list)
            mfrom = (pair_swap(even, "sp", 0), pair_swap(odd, "sp", 1))
            (mpart,) = kernel_call(own_mesh_kernel, [mesh_shape], [near_scratch], 1.0)(
                mstate, hot, weight
            )

    split = peers // 2
    slot_shape = ((padded, 2 * cap), BF16)
    (early,) = kernel_call(
        functools.partial(early_kernel, bands=bands, peer=split), [slot_shape], (), 0.4
    )(gmoved, mmoved, gmix, mmix, sums)
    early = peer_swap(early, "sp", split)
    gmine = activated(gtotal, ggot)
    (gstate,) = kernel_call(state_kernel, [grid_shape], [((hid, gp), BF16)], 0.3)(
        gmoved, gmine, core_swap(gmine), wout
    )
    mmine, mixed = kernel_call(
        functools.partial(silu_mix_kernel, peer=split),
        [((half, nodes), BF16), ((half, 2 * cap), BF16)],
        (),
        0.3,
        spaces=[VMEM] * 5 + [pl.ANY],
    )(mtotal, mgot, gmine, gmix, mmix, early)
    mother = core_swap(mmine)
    mixed = peer_swap(mixed, "sp", split)
    which = [p for p in range(peers) if p != split]
    mstate, *values = kernel_call(
        functools.partial(mix_kernel, bands=bands, which=which),
        [mesh_shape] + [slot_shape] * len(which),
        [((hid, nodes), BF16)],
        0.8,
    )(gstate, mmoved, mmine, mother, wout, gmix, mmix, sums)
    values = dict(zip(which, values))
    mixed, mstate = lax.optimization_barrier((mixed, mstate))
    for p in which[1:]:
        values[p] = peer_swap(values[p], "sp", p)
    (values[split],) = kernel_call(join_kernel, [slot_shape], (), 0.85)(
        early, mixed, core_swap(mixed), wout
    )
    values = [values[p] for p in range(peers)]
    grid_out, mesh_out = kernel_call(
        functools.partial(end_kernel, bands=bands),
        [(grid_flat.shape, F32), (mesh_spec.shape, F32)],
        [
            ((2, padded, peers * cap), BF16),
            ((padded, points), F32),
            (grid_flat.shape, F32),
            (mesh_spec.shape, F32),
            pltpu.SemaphoreType.DMA((2,)),
        ],
        1.9,
        out_space=pl.ANY,
    )(gstate, mstate, gland, mland, grid_sea, *values[::-1])
    return grid_out.reshape(grid_spec.shape), mesh_out


def solution(mesh):
    return jax.shard_map(
        per_device,
        mesh=mesh,
        in_specs=(
            P("fr", "dr", ("grp", "sp"), None),
            P("fr", "dr", ("grp", "sp")),
            P(("grp", "sp"), None),
            P(("grp", "sp"), None),
            P(None, ("grp", "sp")),
            P(None, ("grp", "sp")),
            P(None, ("grp", "sp")),
            P(None, ("grp", "sp")),
            P("fr", "dr", None),
            P(None, "fr", "dr"),
            P(None, ("grp", "sp"), None, None),
            P(None, ("grp", "sp"), None, None),
            P(("grp", "sp"), None),
            P(("grp", "sp"), None, None),
            P(None, ("grp", "sp"), None, None),
            P(None, ("grp", "sp"), None, None),
            P(("grp", "sp"), None),
            P(("grp", "sp"), None, None),
        ),
        out_specs=(P("fr", "dr", ("grp", "sp"), None), P("fr", "dr", ("grp", "sp"))),
        check_vma=False,
    )
```

```python
import functools

import jax
import jax.numpy as jnp
import numpy as np
from jax import lax
from jax.experimental import pallas as pl
from jax.experimental.pallas import tpu as pltpu
from jax.sharding import PartitionSpec as P

NSUB = 2
DT_STEP = 0.1
BLEND_RATE = 0.5
F32 = jnp.float32
BF16 = jnp.bfloat16
CHUNK = 16
FLOPS_PER_US = 1.15e9


VMEM = pltpu.MemorySpace.VMEM
HBM = pltpu.MemorySpace.HBM


def kernel_call(body, outs, scratch, expected_us, spaces=None, out_space=VMEM):
    def run(*args):
        where = spaces or [VMEM] * len(args)
        args = [
            pltpu.with_memory_space_constraint(a, HBM) if space == HBM else a
            for a, space in zip(args, where)
        ]
        return pl.pallas_call(
            body,
            out_shape=[jax.ShapeDtypeStruct(s, t) for s, t in outs],
            in_specs=[pl.BlockSpec(memory_space=space) for space in where],
            out_specs=[pl.BlockSpec(memory_space=out_space)] * len(outs),
            scratch_shapes=[s if hasattr(s, "dtype") else pltpu.VMEM(*s) for s in scratch],
            compiler_params=pltpu.CompilerParams(vmem_limit_bytes=16 << 20),
            cost_estimate=pl.CostEstimate(
                flops=int(expected_us * FLOPS_PER_US), bytes_accessed=0, transcendentals=0
            ),
        )(*args)

    return run


def dot(a, b):
    return jnp.dot(a, b, preferred_element_type=F32)


def one_hot(row, length):
    spots = lax.broadcasted_iota(jnp.int32, (length, row.shape[1]), 0)
    return jnp.where(spots == row, 1.0, 0.0).astype(BF16)


def pair_swap(array, axis, first):
    size = lax.axis_size(axis)
    pairs = [(i, i + 1) for i in range(first, size - 1, 2)]
    return lax.ppermute(array, axis, pairs + [(j, i) for i, j in pairs])


def peer_swap(array, axis, step):
    size = lax.axis_size(axis)
    return lax.ppermute(array, axis, [(i, i ^ step) for i in range(size)])


def on_even():
    return lax.rem(lax.axis_index("sp"), 2) == 0


def messages(mesh, low_row, high_row, halo_ref, even_ref, odd_ref):
    even = on_even()
    nodes = mesh.shape[1]
    cols = low_row.shape[1]
    to_lower = dot(mesh, one_hot(halo_ref[0:1, :], nodes)).astype(BF16)
    to_upper = dot(mesh, one_hot(halo_ref[1:2, :], nodes)).astype(BF16)
    even_ref[:, :cols] = jnp.where(even, high_row, low_row)
    odd_ref[:, :cols] = jnp.where(even, low_row, high_row)
    even_ref[:, cols:] = jnp.where(even, to_upper, to_lower)
    odd_ref[:, cols:] = jnp.where(even, to_lower, to_upper)


def pack_rows(source_ref, packed_ref, at):
    freqs, dirs, width = source_ref.shape
    for f in range(freqs):
        packed_ref[f * dirs : (f + 1) * dirs, at : at + width] = source_ref[f].astype(F32)
    packed_ref[freqs * dirs :, at : at + width] = jnp.zeros(
        (packed_ref.shape[0] - freqs * dirs, width), F32
    )


def begin_kernel(
    grid_hbm, mesh_hbm, halo_hbm, even_ref, odd_ref, grid_ref, mesh_ref, halo_ref, packed_ref, sem,
    *, rows,
):
    copies = [
        pltpu.make_async_copy(halo_hbm, halo_ref, sem.at[0]),
        pltpu.make_async_copy(mesh_hbm, mesh_ref, sem.at[1]),
        pltpu.make_async_copy(grid_hbm, grid_ref, sem.at[2]),
    ]
    for copy in copies:
        copy.start()
    bands = grid_ref.shape[0] // rows
    blank = jnp.zeros((packed_ref.shape[0] - bands, grid_ref.shape[1]), F32)
    copies[0].wait()
    copies[1].wait()
    pack_rows(mesh_ref, packed_ref, 0)
    copies[2].wait()
    low = jnp.concatenate([grid_ref[pl.ds(0, bands, stride=rows), :], blank], axis=0)
    high = jnp.concatenate([grid_ref[pl.ds(rows - 1, bands, stride=rows), :], blank], axis=0)
    messages(
        packed_ref[...].astype(BF16), low.astype(BF16), high.astype(BF16), halo_ref, even_ref, odd_ref
    )


def own_grid(state_ref, band_ref, sea_ref, speed_ref, part_ref):
    rows, cols = sea_ref.shape
    sea = sea_ref[...].astype(F32)
    lane = lax.broadcasted_iota(jnp.int32, (CHUNK, cols), 1)
    for c in range(state_ref.shape[0] // CHUNK):
        here = slice(c * CHUNK, (c + 1) * CHUNK)
        cx = band_ref[here, 0:1]
        cy = band_ref[here, 1:2]
        for x in range(rows):
            g = state_ref[here, x * cols : (x + 1) * cols]
            low = 0.0 if x == 0 else state_ref[here, (x - 1) * cols : x * cols]
            high = 0.0 if x == rows - 1 else state_ref[here, (x + 1) * cols : (x + 2) * cols]
            west = jnp.where(lane == 0, 0.0, pltpu.roll(g, 1, 1))
            east = jnp.where(lane == cols - 1, 0.0, pltpu.roll(g, cols - 1, 1))
            out = g - jnp.abs(cx) * speed_ref[x : x + 1, :] * (g - jnp.where(cx > 0, low, high))
            out = out - jnp.abs(cy) * speed_ref[x : x + 1, :] * (g - jnp.where(cy > 0, west, east))
            part_ref[here, x * cols : (x + 1) * cols] = out * sea[x : x + 1, :]


def own_mesh(mesh, hot_ref, weight_ref, mesh_ref, part_ref, near_ref):
    neighbours, padded, nodes = weight_ref.shape
    for k in range(neighbours):
        near_ref[k] = dot(mesh, hot_ref[k, :nodes, :])
    for c in range(padded // CHUNK):
        here = slice(c * CHUNK, (c + 1) * CHUNK)
        e = mesh_ref[here, :]
        out = e
        for k in range(neighbours):
            out = out + weight_ref[k, here, :] * (near_ref[k, here, :] - e)
        part_ref[here, :] = out


def prepare_kernel(
    grid_hbm, mesh_hbm, table_hbm, win_hbm, wout_hbm, index_ref, pq_ref, sea_ref, speed_ref,
    gpart_ref, mpart_ref, hot_ref, weight_ref, band_ref, win_ref, wout_ref,
    grid_ref, mesh_ref, layer_ref, gstate_ref, mstate_ref, near_ref, pack_ref, sem,
):
    fr, dr = lax.axis_index("fr"), lax.axis_index("dr")
    rows, cols = sea_ref.shape
    padded = gstate_ref.shape[0]
    bands = grid_ref.shape[0] // rows
    copies = [
        pltpu.make_async_copy(table_hbm.at[fr, dr], band_ref, sem.at[0]),
        pltpu.make_async_copy(mesh_hbm, mesh_ref, sem.at[1]),
        pltpu.make_async_copy(grid_hbm, grid_ref, sem.at[2]),
        pltpu.make_async_copy(win_hbm, layer_ref.at[0], sem.at[3]),
        pltpu.make_async_copy(wout_hbm, layer_ref.at[1], sem.at[4]),
    ]
    for copy in copies:
        copy.start()
    neighbours = index_ref.shape[0]
    for k in range(neighbours):
        hot_ref[k] = one_hot(index_ref[k : k + 1, :], hot_ref.shape[1])
    copies[0].wait()
    for c in range(padded // CHUNK):
        here = slice(c * CHUNK, (c + 1) * CHUNK)
        cx = band_ref[here, 0:1]
        cy = band_ref[here, 1:2]
        for k in range(neighbours):
            w = cx * pq_ref[k : k + 1, :] + cy * pq_ref[neighbours + k : neighbours + k + 1, :]
            weight_ref[k, here, :] = jnp.maximum(w, 0.0)
    copies[1].wait()
    pack_rows(mesh_ref, mstate_ref, 0)
    own_mesh(mstate_ref[...].astype(BF16), hot_ref, weight_ref, mstate_ref, mpart_ref, near_ref)
    copies[2].wait()
    gstate_ref[bands:, :] = jnp.zeros((padded - bands, gstate_ref.shape[1]), F32)
    for x in range(rows):
        gstate_ref[:bands, x * cols : (x + 1) * cols] = grid_ref[pl.ds(x, bands, stride=rows), :]
    own_grid(gstate_ref, band_ref, sea_ref, speed_ref, gpart_ref)
    half = pack_ref.shape[1] // 2
    copies[3].wait()
    pack_rows(layer_ref.at[0], pack_ref, 0)
    one, two = pack_ref[:, :half].T.astype(BF16), pack_ref[:, half:].T.astype(BF16)
    win_ref[:half, :] = jnp.where(dr == 0, one, two)
    win_ref[half:, :] = jnp.where(dr == 0, two, one)
    copies[4].wait()
    pack_rows(layer_ref.at[1], pack_ref, 0)
    one, two = pack_ref[:, :half].astype(BF16), pack_ref[:, half:].astype(BF16)
    wout_ref[:, :half] = jnp.where(dr == 0, one, two)
    wout_ref[:, half:] = jnp.where(dr == 0, two, one)


def own_mesh_kernel(state_ref, hot_ref, weight_ref, part_ref, near_ref):
    own_mesh(state_ref[...].astype(BF16), hot_ref, weight_ref, state_ref, part_ref, near_ref)


def first_layer(win_ref, feat_ref, keep_ref, send_ref):
    half = keep_ref.shape[0]
    send_ref[...] = dot(win_ref[half:, :], feat_ref[...]).astype(BF16)
    keep_ref[...] = dot(win_ref[:half, :], feat_ref[...])


def halo_grid_kernel(
    part_ref, even_ref, odd_ref, band_ref, sea_ref, speed_ref, win_ref,
    moved_ref, keep_ref, send_ref, feat_ref,
):
    rows, cols = sea_ref.shape
    even = on_even()
    scale = sea_ref[...].astype(F32) * speed_ref[...]
    for c in range(part_ref.shape[0] // CHUNK):
        here = slice(c * CHUNK, (c + 1) * CHUNK)
        cx = band_ref[here, 0:1]
        a, b = even_ref[here, :cols].astype(F32), odd_ref[here, :cols].astype(F32)
        for x in range(rows):
            cut = slice(x * cols, (x + 1) * cols)
            out = part_ref[here, cut]
            if x == 0:
                out = out + jnp.maximum(cx, 0.0) * scale[x : x + 1, :] * jnp.where(even, b, a)
            if x == rows - 1:
                out = out + jnp.maximum(-cx, 0.0) * scale[x : x + 1, :] * jnp.where(even, a, b)
            moved_ref[here, cut] = out
            feat_ref[here, cut] = out.astype(BF16)
    first_layer(win_ref, feat_ref, keep_ref, send_ref)


def halo_mesh_kernel(
    part_ref, even_ref, odd_ref, hot_ref, weight_ref, win_ref, after_ref,
    moved_ref, keep_ref, send_ref, ext_ref, near_ref, feat_ref,
):
    neighbours, padded, nodes = weight_ref.shape
    listed = ext_ref.shape[1] // 2
    first = even_ref.shape[1] - listed
    even = on_even()
    ext_ref[:, :listed] = jnp.where(even, odd_ref[:, first:], even_ref[:, first:])
    ext_ref[:, listed:] = jnp.where(even, even_ref[:, first:], odd_ref[:, first:])
    for k in range(neighbours):
        near_ref[k] = dot(ext_ref[...], hot_ref[k, nodes:, :])
    for c in range(padded // CHUNK):
        here = slice(c * CHUNK, (c + 1) * CHUNK)
        out = part_ref[here, :]
        for k in range(neighbours):
            out = out + weight_ref[k, here, :] * near_ref[k, here, :]
        moved_ref[here, :] = out
        feat_ref[here, :] = out.astype(BF16)
    first_layer(win_ref, feat_ref, keep_ref, send_ref)


def transferred(moved_ref, mine_ref, other_ref, wout_ref, hid_ref):
    half = mine_ref.shape[0]
    hid_ref[:half, :] = mine_ref[...]
    hid_ref[half:, :] = other_ref[...]
    return moved_ref[...] + DT_STEP * dot(wout_ref[...], hid_ref[...])


def next_grid_kernel(
    moved_ref, mine_ref, other_ref, wout_ref, state_ref, even_ref, odd_ref, hid_ref
):
    state_ref[...] = transferred(moved_ref, mine_ref, other_ref, wout_ref, hid_ref)
    even = on_even()
    cols = even_ref.shape[1]
    low, high = state_ref[:, :cols], state_ref[:, state_ref.shape[1] - cols :]
    even_ref[...] = jnp.where(even, high, low).astype(BF16)
    odd_ref[...] = jnp.where(even, low, high).astype(BF16)


def next_mesh_kernel(
    moved_ref, mine_ref, other_ref, wout_ref, halo_ref, state_ref, even_ref, odd_ref, hid_ref
):
    state_ref[...] = transferred(moved_ref, mine_ref, other_ref, wout_ref, hid_ref)
    even = on_even()
    mesh = state_ref[...].astype(BF16)
    nodes = mesh.shape[1]
    to_lower = dot(mesh, one_hot(halo_ref[0:1, :], nodes))
    to_upper = dot(mesh, one_hot(halo_ref[1:2, :], nodes))
    even_ref[...] = jnp.where(even, to_upper, to_lower).astype(BF16)
    odd_ref[...] = jnp.where(even, to_lower, to_upper).astype(BF16)


def state_kernel(moved_ref, mine_ref, other_ref, wout_ref, state_ref, hid_ref):
    state_ref[...] = transferred(moved_ref, mine_ref, other_ref, wout_ref, hid_ref)


def slots_kernel(
    gi_ref, gw_ref, gc_ref, gt_ref, mi_ref, mw_ref, mc_ref, mt_ref, after_ref,
    gmix_ref, mmix_ref, sums_ref, gland_ref, mland_ref,
):
    me = lax.axis_index("sp")
    _, _, peers, cap = gi_ref.shape
    groups = (
        (gi_ref, gw_ref, gc_ref, gt_ref, gmix_ref, gland_ref, 0),
        (mi_ref, mw_ref, mc_ref, mt_ref, mmix_ref, mland_ref, 1),
    )
    for index_ref, weight_ref, count_ref, target_ref, mix_ref, land_ref, kind in groups:
        length = mix_ref.shape[0]
        spots = lax.broadcasted_iota(jnp.int32, (length, cap), 0)
        slot = lax.broadcasted_iota(jnp.int32, (1, cap), 1)
        for p in range(peers):
            peer = lax.bitwise_xor(me, p)
            count = jnp.sum(
                jnp.where(
                    lax.broadcasted_iota(jnp.int32, (1, peers), 1) == peer, count_ref[...], 0
                ),
                axis=1,
                keepdims=True,
            )
            live = jnp.where(slot < count, 1.0, 0.0)
            mix = jnp.zeros((length, cap), F32)
            total = jnp.zeros((1, cap), F32)
            for j in range(index_ref.shape[0]):
                scaled = weight_ref[j, 0, pl.ds(peer, 1), :] * live
                mix = mix + jnp.where(spots == index_ref[j, 0, pl.ds(peer, 1), :], scaled, 0.0)
                total = total + scaled
            mix_ref[:, p * cap : (p + 1) * cap] = mix.astype(BF16)
            sums_ref[kind : kind + 1, p * cap : (p + 1) * cap] = total
            land_ref[:, p * cap : (p + 1) * cap] = one_hot(
                target_ref[0, pl.ds(peer, 1), :], land_ref.shape[0]
            )


def slot_values(source_refs, mix_refs, sums_ref, p, cap, bands, out_ref):
    cut = slice(p * cap, (p + 1) * cap)
    for kind in (0, 1):
        value = dot(source_refs[kind][...], mix_refs[kind][:, cut])
        if bands is not None:
            row = lax.broadcasted_iota(jnp.int32, value.shape, 0)
            value = jnp.where(row == bands, sums_ref[kind : kind + 1, cut], value)
        out_ref[:, kind * cap : (kind + 1) * cap] = value.astype(BF16)


def early_kernel(grid_ref, mesh_ref, gmix_ref, mmix_ref, sums_ref, out_ref, *, bands, peer):
    cap = out_ref.shape[1] // 2
    parts = (grid_ref[...].astype(BF16), mesh_ref[...].astype(BF16))
    slot_values(parts, (gmix_ref, mmix_ref), sums_ref, peer, cap, bands, out_ref)


def mix_kernel(
    grid_ref, moved_ref, mine_ref, other_ref, wout_ref, gmix_ref, mmix_ref, sums_ref, state_ref,
    *rest, bands, which,
):
    out_refs, hid_ref = rest[:-1], rest[-1]
    state_ref[...] = transferred(moved_ref, mine_ref, other_ref, wout_ref, hid_ref)
    cap = out_refs[0].shape[1] // 2
    parts = (grid_ref[...].astype(BF16), state_ref[...].astype(BF16))
    for p, out_ref in zip(which, out_refs):
        slot_values(parts, (gmix_ref, mmix_ref), sums_ref, p, cap, bands, out_ref)


def silu(total_ref, got_ref):
    total = total_ref[...] + got_ref[...].astype(F32)
    return (total / (1.0 + jnp.exp(-total))).astype(BF16)


def silu_kernel(total_ref, got_ref, *rest):
    rest[-1][...] = silu(total_ref, got_ref)


def silu_mix_kernel(
    total_ref, got_ref, grid_ref, gmix_ref, mmix_ref, after_ref, mine_ref, mixed_ref, *, peer
):
    cap = mixed_ref.shape[1] // 2
    mine_ref[...] = silu(total_ref, got_ref)
    slot_values((grid_ref, mine_ref[...]), (gmix_ref, mmix_ref), None, peer, cap, None, mixed_ref)


def join_kernel(early_ref, mine_ref, other_ref, wout_ref, out_ref):
    half = mine_ref.shape[0]
    moved = dot(wout_ref[:, :half], mine_ref[...]) + dot(wout_ref[:, half:], other_ref[...])
    out_ref[...] = (early_ref[...].astype(F32) + DT_STEP * moved).astype(BF16)


def land(values, land_ref):
    return lax.dot_general(
        values, land_ref[...], (((1,), (1,)), ((), ())), preferred_element_type=F32
    )


def end_kernel(gstate_ref, mstate_ref, gland_ref, mland_ref, sea_ref, *rest, bands):
    got_refs, rest = rest[-8::-1], rest[-7:]
    grid_hbm, mesh_hbm, values_ref, sum_ref, grid_ref, mesh_ref, sem = rest
    rows, cols = sea_ref.shape
    gp = rows * cols
    freqs, dirs, _ = mesh_ref.shape
    cap = got_refs[0].shape[1] // 2
    for kind in (0, 1):
        for p, got in enumerate(got_refs):
            values_ref[kind, :, p * cap : (p + 1) * cap] = got[:, kind * cap : (kind + 1) * cap]
    sum_ref[:, gp:] = land(values_ref[0], gland_ref)
    cover = sum_ref[bands : bands + 1, gp:]
    rate = BLEND_RATE / (1.0 + cover)
    keep = 1.0 - rate * cover
    for f in range(freqs):
        here = slice(f * dirs, (f + 1) * dirs)
        mesh_ref[f] = keep * mstate_ref[here, :] + rate * sum_ref[here, gp:]
    mesh_copy = pltpu.make_async_copy(mesh_ref, mesh_hbm, sem.at[0])
    mesh_copy.start()
    sum_ref[:, :gp] = land(values_ref[1], mland_ref)
    cover = sum_ref[bands : bands + 1, :gp]
    rate = BLEND_RATE / (1.0 + cover)
    keep = 1.0 - rate * cover
    sea = sea_ref[...].astype(F32)
    for x in range(rows):
        cut = slice(x * cols, (x + 1) * cols)
        wet = sea[x : x + 1, :]
        out = keep[:, cut] * wet * gstate_ref[:bands, cut] + rate[:, cut] * wet * sum_ref[:bands, cut]
        grid_ref[pl.ds(x, bands, stride=rows), :] = out
    grid_copy = pltpu.make_async_copy(grid_ref, grid_hbm, sem.at[1])
    grid_copy.start()
    mesh_copy.wait()
    grid_copy.wait()


def band_table(freqs, dirs, n_fr, n_dr, padded):
    speed = (0.7 * np.power(np.float32(1.1), -np.arange(freqs * n_fr, dtype=np.float32))).astype(np.float32)
    total = dirs * n_dr
    heading = (2.0 * np.pi * (np.arange(total, dtype=np.float64) + 0.5) / total)
    table = np.zeros((n_fr, n_dr, padded, 2), np.float32)
    for i in range(n_fr):
        for j in range(n_dr):
            s = speed[i * freqs : (i + 1) * freqs, None]
            h = heading[None, j * dirs : (j + 1) * dirs]
            table[i, j, : freqs * dirs, 0] = (s * np.cos(h)).reshape(-1)
            table[i, j, : freqs * dirs, 1] = (s * np.sin(h)).reshape(-1)
    return table


def core_swap(array):
    return lax.ppermute(array, "dr", [(0, 1), (1, 0)])


def per_device(
    grid_spec, mesh_spec, grid_sea, grid_speed, nb_index, nb_angle, nb_coef, halo_list, w_in, w_out,
    g2m_index, g2m_weight, g2m_count, g2m_target, m2g_index, m2g_weight, m2g_count, m2g_target,
):
    freqs, dirs, rows, cols = grid_spec.shape
    nodes = mesh_spec.shape[2]
    listed = halo_list.shape[1]
    hid = w_in.shape[2]
    half = hid // 2
    bands = freqs * dirs
    padded = (bands // CHUNK + 1) * CHUNK
    gp = rows * cols
    points = gp + nodes
    neighbours = nb_index.shape[0]
    peers, cap = g2m_index.shape[2:]
    n_fr, n_dr = lax.axis_size("fr"), lax.axis_size("dr")

    message = ((padded, cols + listed), BF16)
    grid_shape = ((padded, gp), F32)
    mesh_shape = ((padded, nodes), F32)
    near_scratch = ((neighbours, padded, nodes), F32)
    grid_flat = grid_spec.reshape(bands * rows, cols)
    even, odd = kernel_call(
        functools.partial(begin_kernel, rows=rows),
        [message, message],
        [
            (grid_flat.shape, F32),
            (mesh_spec.shape, F32),
            (halo_list.shape, jnp.int32),
            mesh_shape,
            pltpu.SemaphoreType.DMA((3,)),
        ],
        1.8,
        spaces=[HBM] * 3,
    )(grid_flat, mesh_spec, halo_list)
    table = jnp.asarray(band_table(freqs, dirs, n_fr, n_dr, padded))
    pq = jnp.concatenate([-nb_coef * jnp.cos(nb_angle), -nb_coef * jnp.sin(nb_angle)], axis=0)
    from_even = pair_swap(even, "sp", 0)
    from_odd = pair_swap(odd, "sp", 1)
    gfrom, mfrom = (from_even, from_odd), (from_even, from_odd)
    gpart, mpart, hot, weight, band, win, wout = kernel_call(
        prepare_kernel,
        [
            grid_shape,
            mesh_shape,
            ((neighbours, nodes + 2 * listed, nodes), BF16),
            near_scratch,
            ((padded, 2), F32),
            ((hid, padded), BF16),
            ((padded, hid), BF16),
        ],
        [
            (grid_flat.shape, F32),
            (mesh_spec.shape, F32),
            ((2,) + w_in.shape, BF16),
            grid_shape,
            mesh_shape,
            near_scratch,
            ((padded, hid), F32),
            pltpu.SemaphoreType.DMA((5,)),
        ],
        3.4,
        spaces=[HBM] * 5 + [VMEM] * 4,
    )(
        grid_flat, mesh_spec, table, w_in, jnp.transpose(w_out, (1, 2, 0)),
        nb_index, pq, grid_sea, grid_speed,
    )

    def summed(total, send):
        total = total + core_swap(send).astype(F32)
        rounded = total.astype(BF16)
        got = peer_swap(rounded, "fr", 1)
        step = 2
        while step < n_fr:
            total = total + got.astype(F32)
            rounded = total.astype(BF16)
            got = peer_swap(rounded, "fr", step)
            step *= 2
        return total, rounded, got

    def activated(total, got, *after):
        (mine,) = kernel_call(
            silu_kernel, [(total.shape, BF16)], (), 0.1, spaces=[VMEM] * 2 + [pl.ANY] * len(after)
        )(total, got, *after)
        return mine

    for substep in range(NSUB):
        gmoved, gtotal, gsend = kernel_call(
            halo_grid_kernel,
            [grid_shape, ((half, gp), F32), ((half, gp), BF16)],
            [((padded, gp), BF16)],
            0.4,
        )(gpart, *gfrom, band, grid_sea, grid_speed, win)
        gtotal, ground, ggot = summed(gtotal, gsend)
        mmoved, mtotal, msend = kernel_call(
            halo_mesh_kernel,
            [mesh_shape, ((half, nodes), F32), ((half, nodes), BF16)],
            [((padded, 2 * listed), BF16), near_scratch, ((padded, nodes), BF16)],
            0.8,
            spaces=[VMEM] * 6 + [pl.ANY],
        )(mpart, *mfrom, hot, weight, win, gsend)
        mtotal, mround, mgot = summed(mtotal, msend)
        if substep < NSUB - 1:
            gmix, mmix, sums, gland, mland = kernel_call(
                slots_kernel,
                [
                    ((gp, peers * cap), BF16),
                    ((nodes, peers * cap), BF16),
                    ((2, peers * cap), F32),
                    ((nodes, peers * cap), BF16),
                    ((gp, peers * cap), BF16),
                ],
                (),
                0.5,
                spaces=[VMEM] * 8 + [pl.ANY],
            )(
                g2m_index, g2m_weight, g2m_count, g2m_target,
                m2g_index, m2g_weight, m2g_count, m2g_target, ground,
            )
            gmine = activated(gtotal, ggot, sums)
            gstate, even, odd = kernel_call(
                next_grid_kernel,
                [grid_shape, ((padded, cols), BF16), ((padded, cols), BF16)],
                [((hid, gp), BF16)],
                0.4,
            )(gmoved, gmine, core_swap(gmine), wout)
            gfrom = (pair_swap(even, "sp", 0), pair_swap(odd, "sp", 1))
            (gpart,) = kernel_call(own_grid, [grid_shape], (), 0.5)(
                gstate, band, grid_sea, grid_speed
            )
            mmine = activated(mtotal, mgot)
            mstate, even, odd = kernel_call(
                next_mesh_kernel,
                [mesh_shape, ((padded, listed), BF16), ((padded, listed), BF16)],
                [((hid, nodes), BF16)],
                0.5,
            )(mmoved, mmine, core_swap(mmine), wout, halo_list)
            mfrom = (pair_swap(even, "sp", 0), pair_swap(odd, "sp", 1))
            (mpart,) = kernel_call(own_mesh_kernel, [mesh_shape], [near_scratch], 1.0)(
                mstate, hot, weight
            )

    split = peers - 1
    slot_shape = ((padded, 2 * cap), BF16)
    (early,) = kernel_call(
        functools.partial(early_kernel, bands=bands, peer=split), [slot_shape], (), 0.4
    )(gmoved, mmoved, gmix, mmix, sums)
    early = peer_swap(early, "sp", split)
    gmine = activated(gtotal, ggot)
    (gstate,) = kernel_call(state_kernel, [grid_shape], [((hid, gp), BF16)], 0.3)(
        gmoved, gmine, core_swap(gmine), wout
    )
    mmine, mixed = kernel_call(
        functools.partial(silu_mix_kernel, peer=split),
        [((half, nodes), BF16), ((half, 2 * cap), BF16)],
        (),
        0.3,
        spaces=[VMEM] * 5 + [pl.ANY],
    )(mtotal, mgot, gmine, gmix, mmix, early)
    mother = core_swap(mmine)
    mixed = peer_swap(mixed, "sp", split)
    which = [p for p in range(peers) if p != split]
    mstate, *values = kernel_call(
        functools.partial(mix_kernel, bands=bands, which=which),
        [mesh_shape] + [slot_shape] * len(which),
        [((hid, nodes), BF16)],
        0.8,
    )(gstate, mmoved, mmine, mother, wout, gmix, mmix, sums)
    values = dict(zip(which, values))
    mixed, mstate = lax.optimization_barrier((mixed, mstate))
    for p in which[1:]:
        values[p] = peer_swap(values[p], "sp", p)
    (values[split],) = kernel_call(join_kernel, [slot_shape], (), 0.85)(
        early, mixed, core_swap(mixed), wout
    )
    values = [values[p] for p in range(peers)]
    grid_out, mesh_out = kernel_call(
        functools.partial(end_kernel, bands=bands),
        [(grid_flat.shape, F32), (mesh_spec.shape, F32)],
        [
            ((2, padded, peers * cap), BF16),
            ((padded, points), F32),
            (grid_flat.shape, F32),
            (mesh_spec.shape, F32),
            pltpu.SemaphoreType.DMA((2,)),
        ],
        1.9,
        out_space=pl.ANY,
    )(gstate, mstate, gland, mland, grid_sea, *values[::-1])
    return grid_out.reshape(grid_spec.shape), mesh_out


def solution(mesh):
    return jax.shard_map(
        per_device,
        mesh=mesh,
        in_specs=(
            P("fr", "dr", ("grp", "sp"), None),
            P("fr", "dr", ("grp", "sp")),
            P(("grp", "sp"), None),
            P(("grp", "sp"), None),
            P(None, ("grp", "sp")),
            P(None, ("grp", "sp")),
            P(None, ("grp", "sp")),
            P(None, ("grp", "sp")),
            P("fr", "dr", None),
            P(None, "fr", "dr"),
            P(None, ("grp", "sp"), None, None),
            P(None, ("grp", "sp"), None, None),
            P(("grp", "sp"), None),
            P(("grp", "sp"), None, None),
            P(None, ("grp", "sp"), None, None),
            P(None, ("grp", "sp"), None, None),
            P(("grp", "sp"), None),
            P(("grp", "sp"), None, None),
        ),
        out_specs=(P("fr", "dr", ("grp", "sp"), None), P("fr", "dr", ("grp", "sp"))),
        check_vma=False,
    )
```

```python
import functools

import jax
import jax.numpy as jnp
import numpy as np
from jax import lax
from jax.experimental import pallas as pl
from jax.experimental.pallas import tpu as pltpu
from jax.sharding import PartitionSpec as P

NSUB = 2
DT_STEP = 0.1
BLEND_RATE = 0.5
F32 = jnp.float32
BF16 = jnp.bfloat16
CHUNK = 16
FLOPS_PER_US = 1.15e9


VMEM = pltpu.MemorySpace.VMEM
HBM = pltpu.MemorySpace.HBM


def kernel_call(body, outs, scratch, expected_us, spaces=None, out_space=VMEM):
    def run(*args):
        where = spaces or [VMEM] * len(args)
        args = [
            pltpu.with_memory_space_constraint(a, HBM) if space == HBM else a
            for a, space in zip(args, where)
        ]
        return pl.pallas_call(
            body,
            out_shape=[jax.ShapeDtypeStruct(s, t) for s, t in outs],
            in_specs=[pl.BlockSpec(memory_space=space) for space in where],
            out_specs=[pl.BlockSpec(memory_space=out_space)] * len(outs),
            scratch_shapes=[s if hasattr(s, "dtype") else pltpu.VMEM(*s) for s in scratch],
            compiler_params=pltpu.CompilerParams(vmem_limit_bytes=16 << 20),
            cost_estimate=pl.CostEstimate(
                flops=int(expected_us * FLOPS_PER_US), bytes_accessed=0, transcendentals=0
            ),
        )(*args)

    return run


def dot(a, b):
    return jnp.dot(a, b, preferred_element_type=F32)


def one_hot(row, length):
    spots = lax.broadcasted_iota(jnp.int32, (length, row.shape[1]), 0)
    return jnp.where(spots == row, 1.0, 0.0).astype(BF16)


def pair_swap(array, axis, first):
    size = lax.axis_size(axis)
    pairs = [(i, i + 1) for i in range(first, size - 1, 2)]
    return lax.ppermute(array, axis, pairs + [(j, i) for i, j in pairs])


def peer_swap(array, axis, step):
    size = lax.axis_size(axis)
    return lax.ppermute(array, axis, [(i, i ^ step) for i in range(size)])


def on_even():
    return lax.rem(lax.axis_index("sp"), 2) == 0


def pack_rows(source_ref, packed_ref, at):
    freqs, dirs, width = source_ref.shape
    for f in range(freqs):
        packed_ref[f * dirs : (f + 1) * dirs, at : at + width] = source_ref[f].astype(F32)
    packed_ref[freqs * dirs :, at : at + width] = jnp.zeros(
        (packed_ref.shape[0] - freqs * dirs, width), F32
    )


def begin_kernel(
    grid_hbm, mesh_hbm, halo_hbm, even_ref, odd_ref, grid_ref, mesh_ref, halo_ref, packed_ref,
    pick_ref, sem, *, rows,
):
    copies = [
        pltpu.make_async_copy(halo_hbm, halo_ref, sem.at[0]),
        pltpu.make_async_copy(mesh_hbm, mesh_ref, sem.at[1]),
        pltpu.make_async_copy(grid_hbm, grid_ref, sem.at[2]),
    ]
    for copy in copies:
        copy.start()
    even = on_even()
    bands = grid_ref.shape[0] // rows
    cols = grid_ref.shape[1]
    listed = halo_ref.shape[1]
    copies[0].wait()
    lower, upper = halo_ref[0:1, :], halo_ref[1:2, :]
    pick_ref[:, :listed] = one_hot(jnp.where(even, upper, lower), pick_ref.shape[0])
    pick_ref[:, listed:] = one_hot(jnp.where(even, lower, upper), pick_ref.shape[0])
    copies[1].wait()
    pack_rows(mesh_ref, packed_ref, 0)
    picked = dot(packed_ref[...].astype(BF16), pick_ref[...]).astype(BF16)
    even_ref[:, cols:] = picked[:, :listed]
    odd_ref[:, cols:] = picked[:, listed:]
    copies[2].wait()
    blank = jnp.zeros((packed_ref.shape[0] - bands, cols), F32)
    low = jnp.concatenate([grid_ref[pl.ds(0, bands, stride=rows), :], blank], axis=0)
    high = jnp.concatenate([grid_ref[pl.ds(rows - 1, bands, stride=rows), :], blank], axis=0)
    even_ref[:, :cols] = jnp.where(even, high, low).astype(BF16)
    odd_ref[:, :cols] = jnp.where(even, low, high).astype(BF16)


def own_grid(state_ref, band_ref, sea_ref, speed_ref, part_ref):
    rows, cols = sea_ref.shape
    sea = sea_ref[...].astype(F32)
    lane = lax.broadcasted_iota(jnp.int32, (CHUNK, cols), 1)
    for c in range(state_ref.shape[0] // CHUNK):
        here = slice(c * CHUNK, (c + 1) * CHUNK)
        cx = band_ref[here, 0:1]
        cy = band_ref[here, 1:2]
        for x in range(rows):
            g = state_ref[here, x * cols : (x + 1) * cols]
            low = 0.0 if x == 0 else state_ref[here, (x - 1) * cols : x * cols]
            high = 0.0 if x == rows - 1 else state_ref[here, (x + 1) * cols : (x + 2) * cols]
            west = jnp.where(lane == 0, 0.0, pltpu.roll(g, 1, 1))
            east = jnp.where(lane == cols - 1, 0.0, pltpu.roll(g, cols - 1, 1))
            out = g - jnp.abs(cx) * speed_ref[x : x + 1, :] * (g - jnp.where(cx > 0, low, high))
            out = out - jnp.abs(cy) * speed_ref[x : x + 1, :] * (g - jnp.where(cy > 0, west, east))
            part_ref[here, x * cols : (x + 1) * cols] = out * sea[x : x + 1, :]


def own_mesh(mesh, hot_ref, weight_ref, mesh_ref, part_ref, near_ref):
    neighbours, padded, nodes = weight_ref.shape
    for k in range(neighbours):
        near_ref[k] = dot(mesh, hot_ref[k, :nodes, :])
    for c in range(padded // CHUNK):
        here = slice(c * CHUNK, (c + 1) * CHUNK)
        e = mesh_ref[here, :]
        out = e
        for k in range(neighbours):
            out = out + weight_ref[k, here, :] * (near_ref[k, here, :] - e)
        part_ref[here, :] = out


def prepare_kernel(
    grid_hbm, mesh_hbm, table_hbm, win_hbm, wout_hbm, index_ref, pq_ref, sea_ref, speed_ref,
    gpart_ref, mpart_ref, hot_ref, weight_ref, band_ref, win_ref, wout_ref,
    grid_ref, mesh_ref, layer_ref, gstate_ref, mstate_ref, near_ref, pack_ref, sem,
):
    fr, dr = lax.axis_index("fr"), lax.axis_index("dr")
    rows, cols = sea_ref.shape
    padded = gstate_ref.shape[0]
    bands = grid_ref.shape[0] // rows
    copies = [
        pltpu.make_async_copy(table_hbm.at[fr, dr], band_ref, sem.at[0]),
        pltpu.make_async_copy(mesh_hbm, mesh_ref, sem.at[1]),
        pltpu.make_async_copy(grid_hbm, grid_ref, sem.at[2]),
        pltpu.make_async_copy(win_hbm, layer_ref.at[0], sem.at[3]),
        pltpu.make_async_copy(wout_hbm, layer_ref.at[1], sem.at[4]),
    ]
    for copy in copies:
        copy.start()
    neighbours = index_ref.shape[0]
    for k in range(neighbours):
        hot_ref[k] = one_hot(index_ref[k : k + 1, :], hot_ref.shape[1])
    copies[0].wait()
    for c in range(padded // CHUNK):
        here = slice(c * CHUNK, (c + 1) * CHUNK)
        cx = band_ref[here, 0:1]
        cy = band_ref[here, 1:2]
        for k in range(neighbours):
            w = cx * pq_ref[k : k + 1, :] + cy * pq_ref[neighbours + k : neighbours + k + 1, :]
            weight_ref[k, here, :] = jnp.maximum(w, 0.0)
    copies[1].wait()
    pack_rows(mesh_ref, mstate_ref, 0)
    own_mesh(mstate_ref[...].astype(BF16), hot_ref, weight_ref, mstate_ref, mpart_ref, near_ref)
    copies[2].wait()
    gstate_ref[bands:, :] = jnp.zeros((padded - bands, gstate_ref.shape[1]), F32)
    for x in range(rows):
        gstate_ref[:bands, x * cols : (x + 1) * cols] = grid_ref[pl.ds(x, bands, stride=rows), :]
    own_grid(gstate_ref, band_ref, sea_ref, speed_ref, gpart_ref)
    half = pack_ref.shape[1] // 2
    copies[3].wait()
    pack_rows(layer_ref.at[0], pack_ref, 0)
    one, two = pack_ref[:, :half].T.astype(BF16), pack_ref[:, half:].T.astype(BF16)
    win_ref[:half, :] = jnp.where(dr == 0, one, two)
    win_ref[half:, :] = jnp.where(dr == 0, two, one)
    copies[4].wait()
    pack_rows(layer_ref.at[1], pack_ref, 0)
    one, two = pack_ref[:, :half].astype(BF16), pack_ref[:, half:].astype(BF16)
    wout_ref[:, :half] = jnp.where(dr == 0, one, two)
    wout_ref[:, half:] = jnp.where(dr == 0, two, one)


def own_mesh_kernel(state_ref, hot_ref, weight_ref, part_ref, near_ref):
    own_mesh(state_ref[...].astype(BF16), hot_ref, weight_ref, state_ref, part_ref, near_ref)


def first_layer(win_ref, feat_ref, keep_ref, send_ref):
    half = keep_ref.shape[0]
    send_ref[...] = dot(win_ref[half:, :], feat_ref[...]).astype(BF16)
    keep_ref[...] = dot(win_ref[:half, :], feat_ref[...])


def halo_grid_kernel(
    part_ref, even_ref, odd_ref, band_ref, sea_ref, speed_ref, win_ref,
    moved_ref, keep_ref, send_ref, feat_ref,
):
    rows, cols = sea_ref.shape
    even = on_even()
    scale = sea_ref[...].astype(F32) * speed_ref[...]
    for c in range(part_ref.shape[0] // CHUNK):
        here = slice(c * CHUNK, (c + 1) * CHUNK)
        cx = band_ref[here, 0:1]
        a, b = even_ref[here, :cols].astype(F32), odd_ref[here, :cols].astype(F32)
        for x in range(rows):
            cut = slice(x * cols, (x + 1) * cols)
            out = part_ref[here, cut]
            if x == 0:
                out = out + jnp.maximum(cx, 0.0) * scale[x : x + 1, :] * jnp.where(even, b, a)
            if x == rows - 1:
                out = out + jnp.maximum(-cx, 0.0) * scale[x : x + 1, :] * jnp.where(even, a, b)
            moved_ref[here, cut] = out
            feat_ref[here, cut] = out.astype(BF16)
    first_layer(win_ref, feat_ref, keep_ref, send_ref)


def halo_mesh_kernel(
    part_ref, even_ref, odd_ref, hot_ref, weight_ref, win_ref, after_ref,
    moved_ref, keep_ref, send_ref, ext_ref, near_ref, feat_ref,
):
    neighbours, padded, nodes = weight_ref.shape
    listed = ext_ref.shape[1] // 2
    first = even_ref.shape[1] - listed
    even = on_even()
    ext_ref[:, :listed] = jnp.where(even, odd_ref[:, first:], even_ref[:, first:])
    ext_ref[:, listed:] = jnp.where(even, even_ref[:, first:], odd_ref[:, first:])
    for k in range(neighbours):
        near_ref[k] = dot(ext_ref[...], hot_ref[k, nodes:, :])
    for c in range(padded // CHUNK):
        here = slice(c * CHUNK, (c + 1) * CHUNK)
        out = part_ref[here, :]
        for k in range(neighbours):
            out = out + weight_ref[k, here, :] * near_ref[k, here, :]
        moved_ref[here, :] = out
        feat_ref[here, :] = out.astype(BF16)
    first_layer(win_ref, feat_ref, keep_ref, send_ref)


def transferred(moved_ref, mine_ref, other_ref, wout_ref, hid_ref):
    half = mine_ref.shape[0]
    hid_ref[:half, :] = mine_ref[...]
    hid_ref[half:, :] = other_ref[...]
    return moved_ref[...] + DT_STEP * dot(wout_ref[...], hid_ref[...])


def next_grid_kernel(
    moved_ref, mine_ref, other_ref, wout_ref, state_ref, even_ref, odd_ref, hid_ref
):
    state_ref[...] = transferred(moved_ref, mine_ref, other_ref, wout_ref, hid_ref)
    even = on_even()
    cols = even_ref.shape[1]
    low, high = state_ref[:, :cols], state_ref[:, state_ref.shape[1] - cols :]
    even_ref[...] = jnp.where(even, high, low).astype(BF16)
    odd_ref[...] = jnp.where(even, low, high).astype(BF16)


def next_mesh_kernel(
    moved_ref, mine_ref, other_ref, wout_ref, halo_ref, state_ref, even_ref, odd_ref, hid_ref
):
    state_ref[...] = transferred(moved_ref, mine_ref, other_ref, wout_ref, hid_ref)
    even = on_even()
    mesh = state_ref[...].astype(BF16)
    nodes = mesh.shape[1]
    to_lower = dot(mesh, one_hot(halo_ref[0:1, :], nodes))
    to_upper = dot(mesh, one_hot(halo_ref[1:2, :], nodes))
    even_ref[...] = jnp.where(even, to_upper, to_lower).astype(BF16)
    odd_ref[...] = jnp.where(even, to_lower, to_upper).astype(BF16)


def state_kernel(moved_ref, mine_ref, other_ref, wout_ref, state_ref, hid_ref):
    state_ref[...] = transferred(moved_ref, mine_ref, other_ref, wout_ref, hid_ref)


def slots_kernel(
    gi_ref, gw_ref, gc_ref, gt_ref, mi_ref, mw_ref, mc_ref, mt_ref, after_ref,
    gmix_ref, mmix_ref, sums_ref, gland_ref, mland_ref,
):
    me = lax.axis_index("sp")
    _, _, peers, cap = gi_ref.shape
    groups = (
        (gi_ref, gw_ref, gc_ref, gt_ref, gmix_ref, gland_ref, 0),
        (mi_ref, mw_ref, mc_ref, mt_ref, mmix_ref, mland_ref, 1),
    )
    for index_ref, weight_ref, count_ref, target_ref, mix_ref, land_ref, kind in groups:
        length = mix_ref.shape[0]
        spots = lax.broadcasted_iota(jnp.int32, (length, cap), 0)
        slot = lax.broadcasted_iota(jnp.int32, (1, cap), 1)
        for p in range(peers):
            peer = lax.bitwise_xor(me, p)
            count = jnp.sum(
                jnp.where(
                    lax.broadcasted_iota(jnp.int32, (1, peers), 1) == peer, count_ref[...], 0
                ),
                axis=1,
                keepdims=True,
            )
            live = jnp.where(slot < count, 1.0, 0.0)
            mix = jnp.zeros((length, cap), F32)
            total = jnp.zeros((1, cap), F32)
            for j in range(index_ref.shape[0]):
                scaled = weight_ref[j, 0, pl.ds(peer, 1), :] * live
                mix = mix + jnp.where(spots == index_ref[j, 0, pl.ds(peer, 1), :], scaled, 0.0)
                total = total + scaled
            mix_ref[:, p * cap : (p + 1) * cap] = mix.astype(BF16)
            sums_ref[kind : kind + 1, p * cap : (p + 1) * cap] = total
            hit = lax.broadcasted_iota(jnp.int32, (land_ref.shape[1], cap), 0)
            hit = jnp.where(hit == target_ref[0, pl.ds(peer, 1), :], 1.0, 0.0)
            land_ref[p * cap : (p + 1) * cap, :] = hit.T.astype(BF16)


def slot_values(source_refs, mix_refs, sums_ref, p, cap, bands, out_ref):
    cut = slice(p * cap, (p + 1) * cap)
    for kind in (0, 1):
        value = dot(source_refs[kind][...], mix_refs[kind][:, cut])
        if bands is not None:
            row = lax.broadcasted_iota(jnp.int32, value.shape, 0)
            value = jnp.where(row == bands, sums_ref[kind : kind + 1, cut], value)
        out_ref[:, kind * cap : (kind + 1) * cap] = value.astype(BF16)


def early_kernel(grid_ref, mesh_ref, gmix_ref, mmix_ref, sums_ref, out_ref, *, bands, peer):
    cap = out_ref.shape[1] // 2
    parts = (grid_ref[...].astype(BF16), mesh_ref[...].astype(BF16))
    slot_values(parts, (gmix_ref, mmix_ref), sums_ref, peer, cap, bands, out_ref)


def mix_kernel(
    grid_ref, moved_ref, mine_ref, other_ref, wout_ref, gmix_ref, mmix_ref, sums_ref, state_ref,
    *rest, bands, which,
):
    out_refs, hid_ref = rest[:-1], rest[-1]
    state_ref[...] = transferred(moved_ref, mine_ref, other_ref, wout_ref, hid_ref)
    cap = out_refs[0].shape[1] // 2
    parts = (grid_ref[...].astype(BF16), state_ref[...].astype(BF16))
    for p, out_ref in zip(which, out_refs):
        slot_values(parts, (gmix_ref, mmix_ref), sums_ref, p, cap, bands, out_ref)


def silu(total_ref, got_ref):
    total = total_ref[...] + got_ref[...].astype(F32)
    return (total / (1.0 + jnp.exp(-total))).astype(BF16)


def silu_kernel(total_ref, got_ref, *rest):
    rest[-1][...] = silu(total_ref, got_ref)


def silu_mix_kernel(
    total_ref, got_ref, grid_ref, gmix_ref, mmix_ref, after_ref, mine_ref, mixed_ref, *, peer
):
    cap = mixed_ref.shape[1] // 2
    mine_ref[...] = silu(total_ref, got_ref)
    slot_values((grid_ref, mine_ref[...]), (gmix_ref, mmix_ref), None, peer, cap, None, mixed_ref)


def join_kernel(early_ref, mine_ref, other_ref, wout_ref, out_ref):
    half = mine_ref.shape[0]
    moved = dot(wout_ref[:, :half], mine_ref[...]) + dot(wout_ref[:, half:], other_ref[...])
    out_ref[...] = (early_ref[...].astype(F32) + DT_STEP * moved).astype(BF16)


def end_kernel(gstate_ref, mstate_ref, gland_ref, mland_ref, sea_ref, *rest, bands):
    got_refs, rest = rest[-8::-1], rest[-7:]
    grid_hbm, mesh_hbm, values_ref, sum_ref, grid_ref, mesh_ref, sem = rest
    rows, cols = sea_ref.shape
    gp = rows * cols
    freqs, dirs, _ = mesh_ref.shape
    cap = got_refs[0].shape[1] // 2
    for kind in (0, 1):
        for p, got in enumerate(got_refs):
            values_ref[kind, :, p * cap : (p + 1) * cap] = got[:, kind * cap : (kind + 1) * cap]
    sum_ref[:, gp:] = dot(values_ref[0], gland_ref[...])
    cover = sum_ref[bands : bands + 1, gp:]
    rate = BLEND_RATE / (1.0 + cover)
    keep = 1.0 - rate * cover
    sum_ref[:, gp:] = keep * mstate_ref[...] + rate * sum_ref[:, gp:]
    for f in range(freqs):
        mesh_ref[f] = sum_ref[f * dirs : (f + 1) * dirs, gp:]
    mesh_copy = pltpu.make_async_copy(mesh_ref, mesh_hbm, sem.at[0])
    mesh_copy.start()
    sum_ref[:, :gp] = dot(values_ref[1], mland_ref[...])
    cover = sum_ref[bands : bands + 1, :gp]
    rate = BLEND_RATE / (1.0 + cover)
    keep = 1.0 - rate * cover
    sea = sea_ref[...].astype(F32)
    for x in range(rows):
        cut = slice(x * cols, (x + 1) * cols)
        wet = sea[x : x + 1, :]
        out = keep[:, cut] * wet * gstate_ref[:bands, cut] + rate[:, cut] * wet * sum_ref[:bands, cut]
        grid_ref[pl.ds(x, bands, stride=rows), :] = out
    grid_copy = pltpu.make_async_copy(grid_ref, grid_hbm, sem.at[1])
    grid_copy.start()
    mesh_copy.wait()
    grid_copy.wait()


def band_table(freqs, dirs, n_fr, n_dr, padded):
    speed = (0.7 * np.power(np.float32(1.1), -np.arange(freqs * n_fr, dtype=np.float32))).astype(np.float32)
    total = dirs * n_dr
    heading = (2.0 * np.pi * (np.arange(total, dtype=np.float64) + 0.5) / total)
    table = np.zeros((n_fr, n_dr, padded, 2), np.float32)
    for i in range(n_fr):
        for j in range(n_dr):
            s = speed[i * freqs : (i + 1) * freqs, None]
            h = heading[None, j * dirs : (j + 1) * dirs]
            table[i, j, : freqs * dirs, 0] = (s * np.cos(h)).reshape(-1)
            table[i, j, : freqs * dirs, 1] = (s * np.sin(h)).reshape(-1)
    return table


def core_swap(array):
    return lax.ppermute(array, "dr", [(0, 1), (1, 0)])


def per_device(
    grid_spec, mesh_spec, grid_sea, grid_speed, nb_index, nb_angle, nb_coef, halo_list, w_in, w_out,
    g2m_index, g2m_weight, g2m_count, g2m_target, m2g_index, m2g_weight, m2g_count, m2g_target,
):
    freqs, dirs, rows, cols = grid_spec.shape
    nodes = mesh_spec.shape[2]
    listed = halo_list.shape[1]
    hid = w_in.shape[2]
    half = hid // 2
    bands = freqs * dirs
    padded = (bands // CHUNK + 1) * CHUNK
    gp = rows * cols
    points = gp + nodes
    neighbours = nb_index.shape[0]
    peers, cap = g2m_index.shape[2:]
    n_fr, n_dr = lax.axis_size("fr"), lax.axis_size("dr")

    message = ((padded, cols + listed), BF16)
    grid_shape = ((padded, gp), F32)
    mesh_shape = ((padded, nodes), F32)
    near_scratch = ((neighbours, padded, nodes), F32)
    grid_flat = grid_spec.reshape(bands * rows, cols)
    even, odd = kernel_call(
        functools.partial(begin_kernel, rows=rows),
        [message, message],
        [
            (grid_flat.shape, F32),
            (mesh_spec.shape, F32),
            (halo_list.shape, jnp.int32),
            mesh_shape,
            ((nodes, 2 * listed), BF16),
            pltpu.SemaphoreType.DMA((3,)),
        ],
        1.8,
        spaces=[HBM] * 3,
    )(grid_flat, mesh_spec, halo_list)
    table = jnp.asarray(band_table(freqs, dirs, n_fr, n_dr, padded))
    pq = jnp.concatenate([-nb_coef * jnp.cos(nb_angle), -nb_coef * jnp.sin(nb_angle)], axis=0)
    from_even = pair_swap(even, "sp", 0)
    from_odd = pair_swap(odd, "sp", 1)
    gfrom, mfrom = (from_even, from_odd), (from_even, from_odd)
    gpart, mpart, hot, weight, band, win, wout = kernel_call(
        prepare_kernel,
        [
            grid_shape,
            mesh_shape,
            ((neighbours, nodes + 2 * listed, nodes), BF16),
            near_scratch,
            ((padded, 2), F32),
            ((hid, padded), BF16),
            ((padded, hid), BF16),
        ],
        [
            (grid_flat.shape, F32),
            (mesh_spec.shape, F32),
            ((2,) + w_in.shape, BF16),
            grid_shape,
            mesh_shape,
            near_scratch,
            ((padded, hid), F32),
            pltpu.SemaphoreType.DMA((5,)),
        ],
        3.4,
        spaces=[HBM] * 5 + [VMEM] * 4,
    )(
        grid_flat, mesh_spec, table, w_in, jnp.transpose(w_out, (1, 2, 0)),
        nb_index, pq, grid_sea, grid_speed,
    )

    def summed(total, send):
        total = total + core_swap(send).astype(F32)
        rounded = total.astype(BF16)
        got = peer_swap(rounded, "fr", 1)
        step = 2
        while step < n_fr:
            total = total + got.astype(F32)
            rounded = total.astype(BF16)
            got = peer_swap(rounded, "fr", step)
            step *= 2
        return total, rounded, got

    def activated(total, got, *after):
        (mine,) = kernel_call(
            silu_kernel, [(total.shape, BF16)], (), 0.1, spaces=[VMEM] * 2 + [pl.ANY] * len(after)
        )(total, got, *after)
        return mine

    for substep in range(NSUB):
        gmoved, gtotal, gsend = kernel_call(
            halo_grid_kernel,
            [grid_shape, ((half, gp), F32), ((half, gp), BF16)],
            [((padded, gp), BF16)],
            0.4,
        )(gpart, *gfrom, band, grid_sea, grid_speed, win)
        gtotal, ground, ggot = summed(gtotal, gsend)
        mmoved, mtotal, msend = kernel_call(
            halo_mesh_kernel,
            [mesh_shape, ((half, nodes), F32), ((half, nodes), BF16)],
            [((padded, 2 * listed), BF16), near_scratch, ((padded, nodes), BF16)],
            0.8,
            spaces=[VMEM] * 6 + [pl.ANY],
        )(mpart, *mfrom, hot, weight, win, gsend)
        mtotal, mround, mgot = summed(mtotal, msend)
        if substep < NSUB - 1:
            gmix, mmix, sums, gland, mland = kernel_call(
                slots_kernel,
                [
                    ((gp, peers * cap), BF16),
                    ((nodes, peers * cap), BF16),
                    ((2, peers * cap), F32),
                    ((peers * cap, nodes), BF16),
                    ((peers * cap, gp), BF16),
                ],
                (),
                0.5,
                spaces=[VMEM] * 8 + [pl.ANY],
            )(
                g2m_index, g2m_weight, g2m_count, g2m_target,
                m2g_index, m2g_weight, m2g_count, m2g_target, ground,
            )
            gmine = activated(gtotal, ggot, sums)
            gstate, even, odd = kernel_call(
                next_grid_kernel,
                [grid_shape, ((padded, cols), BF16), ((padded, cols), BF16)],
                [((hid, gp), BF16)],
                0.4,
            )(gmoved, gmine, core_swap(gmine), wout)
            gfrom = (pair_swap(even, "sp", 0), pair_swap(odd, "sp", 1))
            (gpart,) = kernel_call(own_grid, [grid_shape], (), 0.5)(
                gstate, band, grid_sea, grid_speed
            )
            mmine = activated(mtotal, mgot)
            mstate, even, odd = kernel_call(
                next_mesh_kernel,
                [mesh_shape, ((padded, listed), BF16), ((padded, listed), BF16)],
                [((hid, nodes), BF16)],
                0.5,
            )(mmoved, mmine, core_swap(mmine), wout, halo_list)
            mfrom = (pair_swap(even, "sp", 0), pair_swap(odd, "sp", 1))
            (mpart,) = kernel_call(own_mesh_kernel, [mesh_shape], [near_scratch], 1.0)(
                mstate, hot, weight
            )

    split = peers - 1
    slot_shape = ((padded, 2 * cap), BF16)
    (early,) = kernel_call(
        functools.partial(early_kernel, bands=bands, peer=split), [slot_shape], (), 0.4
    )(gmoved, mmoved, gmix, mmix, sums)
    early = peer_swap(early, "sp", split)
    gmine = activated(gtotal, ggot)
    (gstate,) = kernel_call(state_kernel, [grid_shape], [((hid, gp), BF16)], 0.3)(
        gmoved, gmine, core_swap(gmine), wout
    )
    mmine, mixed = kernel_call(
        functools.partial(silu_mix_kernel, peer=split),
        [((half, nodes), BF16), ((half, 2 * cap), BF16)],
        (),
        0.3,
        spaces=[VMEM] * 5 + [pl.ANY],
    )(mtotal, mgot, gmine, gmix, mmix, early)
    mother = core_swap(mmine)
    mixed = peer_swap(mixed, "sp", split)
    which = [p for p in range(peers) if p != split]
    mstate, *values = kernel_call(
        functools.partial(mix_kernel, bands=bands, which=which),
        [mesh_shape] + [slot_shape] * len(which),
        [((hid, nodes), BF16)],
        0.8,
    )(gstate, mmoved, mmine, mother, wout, gmix, mmix, sums)
    values = dict(zip(which, values))
    mixed, mstate = lax.optimization_barrier((mixed, mstate))
    for p in which[1:]:
        values[p] = peer_swap(values[p], "sp", p)
    (values[split],) = kernel_call(join_kernel, [slot_shape], (), 0.85)(
        early, mixed, core_swap(mixed), wout
    )
    values = [values[p] for p in range(peers)]
    grid_out, mesh_out = kernel_call(
        functools.partial(end_kernel, bands=bands),
        [(grid_flat.shape, F32), (mesh_spec.shape, F32)],
        [
            ((2, padded, peers * cap), BF16),
            ((padded, points), F32),
            (grid_flat.shape, F32),
            (mesh_spec.shape, F32),
            pltpu.SemaphoreType.DMA((2,)),
        ],
        1.9,
        out_space=pl.ANY,
    )(gstate, mstate, gland, mland, grid_sea, *values[::-1])
    return grid_out.reshape(grid_spec.shape), mesh_out


def solution(mesh):
    return jax.shard_map(
        per_device,
        mesh=mesh,
        in_specs=(
            P("fr", "dr", ("grp", "sp"), None),
            P("fr", "dr", ("grp", "sp")),
            P(("grp", "sp"), None),
            P(("grp", "sp"), None),
            P(None, ("grp", "sp")),
            P(None, ("grp", "sp")),
            P(None, ("grp", "sp")),
            P(None, ("grp", "sp")),
            P("fr", "dr", None),
            P(None, "fr", "dr"),
            P(None, ("grp", "sp"), None, None),
            P(None, ("grp", "sp"), None, None),
            P(("grp", "sp"), None),
            P(("grp", "sp"), None, None),
            P(None, ("grp", "sp"), None, None),
            P(None, ("grp", "sp"), None, None),
            P(("grp", "sp"), None),
            P(("grp", "sp"), None, None),
        ),
        out_specs=(P("fr", "dr", ("grp", "sp"), None), P("fr", "dr", ("grp", "sp"))),
        check_vma=False,
    )
```

```python
import functools

import jax
import jax.numpy as jnp
import numpy as np
from jax import lax
from jax.experimental import pallas as pl
from jax.experimental.pallas import tpu as pltpu
from jax.sharding import PartitionSpec as P

NSUB = 2
DT_STEP = 0.1
BLEND_RATE = 0.5
F32 = jnp.float32
BF16 = jnp.bfloat16
CHUNK = 16
FLOPS_PER_US = 1.15e9


VMEM = pltpu.MemorySpace.VMEM
HBM = pltpu.MemorySpace.HBM


def kernel_call(body, outs, scratch, expected_us, spaces=None, out_space=VMEM):
    def run(*args):
        where = spaces or [VMEM] * len(args)
        args = [
            pltpu.with_memory_space_constraint(a, HBM) if space == HBM else a
            for a, space in zip(args, where)
        ]
        return pl.pallas_call(
            body,
            out_shape=[jax.ShapeDtypeStruct(s, t) for s, t in outs],
            in_specs=[pl.BlockSpec(memory_space=space) for space in where],
            out_specs=[pl.BlockSpec(memory_space=out_space)] * len(outs),
            scratch_shapes=[s if hasattr(s, "dtype") else pltpu.VMEM(*s) for s in scratch],
            compiler_params=pltpu.CompilerParams(vmem_limit_bytes=16 << 20),
            cost_estimate=pl.CostEstimate(
                flops=int(expected_us * FLOPS_PER_US), bytes_accessed=0, transcendentals=0
            ),
        )(*args)

    return run


def dot(a, b):
    return jnp.dot(a, b, preferred_element_type=F32)


def one_hot(row, length):
    spots = lax.broadcasted_iota(jnp.int32, (length, row.shape[1]), 0)
    return jnp.where(spots == row, 1.0, 0.0).astype(BF16)


def pair_swap(array, axis, first):
    size = lax.axis_size(axis)
    pairs = [(i, i + 1) for i in range(first, size - 1, 2)]
    return lax.ppermute(array, axis, pairs + [(j, i) for i, j in pairs])


def peer_swap(array, axis, step):
    size = lax.axis_size(axis)
    return lax.ppermute(array, axis, [(i, i ^ step) for i in range(size)])


def on_even():
    return lax.rem(lax.axis_index("sp"), 2) == 0


def pack_rows(source_ref, packed_ref, at):
    freqs, dirs, width = source_ref.shape
    for f in range(freqs):
        packed_ref[f * dirs : (f + 1) * dirs, at : at + width] = source_ref[f].astype(F32)
    packed_ref[freqs * dirs :, at : at + width] = jnp.zeros(
        (packed_ref.shape[0] - freqs * dirs, width), F32
    )


def begin_kernel(
    grid_hbm, mesh_hbm, halo_hbm, even_ref, odd_ref, grid_ref, mesh_ref, halo_ref, packed_ref,
    pick_ref, sem, *, rows,
):
    copies = [
        pltpu.make_async_copy(halo_hbm, halo_ref, sem.at[0]),
        pltpu.make_async_copy(mesh_hbm, mesh_ref, sem.at[1]),
        pltpu.make_async_copy(grid_hbm, grid_ref, sem.at[2]),
    ]
    for copy in copies:
        copy.start()
    even = on_even()
    bands = grid_ref.shape[0] // rows
    cols = grid_ref.shape[1]
    listed = halo_ref.shape[1]
    copies[0].wait()
    lower, upper = halo_ref[0:1, :], halo_ref[1:2, :]
    pick_ref[:, :listed] = one_hot(jnp.where(even, upper, lower), pick_ref.shape[0])
    pick_ref[:, listed:] = one_hot(jnp.where(even, lower, upper), pick_ref.shape[0])
    copies[1].wait()
    pack_rows(mesh_ref, packed_ref, 0)
    picked = dot(packed_ref[...].astype(BF16), pick_ref[...]).astype(BF16)
    even_ref[:, cols:] = picked[:, :listed]
    odd_ref[:, cols:] = picked[:, listed:]
    copies[2].wait()
    blank = jnp.zeros((packed_ref.shape[0] - bands, cols), F32)
    low = jnp.concatenate([grid_ref[pl.ds(0, bands, stride=rows), :], blank], axis=0)
    high = jnp.concatenate([grid_ref[pl.ds(rows - 1, bands, stride=rows), :], blank], axis=0)
    even_ref[:, :cols] = jnp.where(even, high, low).astype(BF16)
    odd_ref[:, :cols] = jnp.where(even, low, high).astype(BF16)


def own_grid(state_ref, band_ref, sea_ref, speed_ref, part_ref):
    rows, cols = sea_ref.shape
    sea = sea_ref[...].astype(F32)
    lane = lax.broadcasted_iota(jnp.int32, (CHUNK, cols), 1)
    for c in range(state_ref.shape[0] // CHUNK):
        here = slice(c * CHUNK, (c + 1) * CHUNK)
        cx = band_ref[here, 0:1]
        cy = band_ref[here, 1:2]
        for x in range(rows):
            g = state_ref[here, x * cols : (x + 1) * cols]
            low = 0.0 if x == 0 else state_ref[here, (x - 1) * cols : x * cols]
            high = 0.0 if x == rows - 1 else state_ref[here, (x + 1) * cols : (x + 2) * cols]
            west = jnp.where(lane == 0, 0.0, pltpu.roll(g, 1, 1))
            east = jnp.where(lane == cols - 1, 0.0, pltpu.roll(g, cols - 1, 1))
            out = g - jnp.abs(cx) * speed_ref[x : x + 1, :] * (g - jnp.where(cx > 0, low, high))
            out = out - jnp.abs(cy) * speed_ref[x : x + 1, :] * (g - jnp.where(cy > 0, west, east))
            part_ref[here, x * cols : (x + 1) * cols] = out * sea[x : x + 1, :]


def own_mesh(mesh, hot_ref, weight_ref, mesh_ref, part_ref, near_ref):
    neighbours, padded, nodes = weight_ref.shape
    for k in range(neighbours):
        near_ref[k] = dot(mesh, hot_ref[k, :nodes, :])
    for c in range(padded // CHUNK):
        here = slice(c * CHUNK, (c + 1) * CHUNK)
        e = mesh_ref[here, :]
        out = e
        for k in range(neighbours):
            out = out + weight_ref[k, here, :] * (near_ref[k, here, :] - e)
        part_ref[here, :] = out


def prepare_kernel(
    grid_hbm, mesh_hbm, table_hbm, first_ref, second_ref, index_ref, pq_ref, sea_ref, speed_ref,
    gpart_ref, mpart_ref, hot_ref, weight_ref, band_ref, win_ref, wout_ref,
    grid_ref, mesh_ref, gstate_ref, mstate_ref, near_ref, pack_ref, sem,
):
    fr, dr = lax.axis_index("fr"), lax.axis_index("dr")
    rows, cols = sea_ref.shape
    padded = gstate_ref.shape[0]
    bands = grid_ref.shape[0] // rows
    copies = [
        pltpu.make_async_copy(table_hbm.at[fr, dr], band_ref, sem.at[0]),
        pltpu.make_async_copy(mesh_hbm, mesh_ref, sem.at[1]),
        pltpu.make_async_copy(grid_hbm, grid_ref, sem.at[2]),
    ]
    for copy in copies:
        copy.start()
    neighbours = index_ref.shape[0]
    for k in range(neighbours):
        hot_ref[k] = one_hot(index_ref[k : k + 1, :], hot_ref.shape[1])
    copies[0].wait()
    for c in range(padded // CHUNK):
        here = slice(c * CHUNK, (c + 1) * CHUNK)
        cx = band_ref[here, 0:1]
        cy = band_ref[here, 1:2]
        for k in range(neighbours):
            w = cx * pq_ref[k : k + 1, :] + cy * pq_ref[neighbours + k : neighbours + k + 1, :]
            weight_ref[k, here, :] = jnp.maximum(w, 0.0)
    copies[1].wait()
    pack_rows(mesh_ref, mstate_ref, 0)
    own_mesh(mstate_ref[...].astype(BF16), hot_ref, weight_ref, mstate_ref, mpart_ref, near_ref)
    copies[2].wait()
    gstate_ref[bands:, :] = jnp.zeros((padded - bands, gstate_ref.shape[1]), F32)
    for x in range(rows):
        gstate_ref[:bands, x * cols : (x + 1) * cols] = grid_ref[pl.ds(x, bands, stride=rows), :]
    own_grid(gstate_ref, band_ref, sea_ref, speed_ref, gpart_ref)
    half = pack_ref.shape[1] // 2
    pack_rows(first_ref, pack_ref, 0)
    one, two = pack_ref[:, :half].T.astype(BF16), pack_ref[:, half:].T.astype(BF16)
    win_ref[:half, :] = jnp.where(dr == 0, one, two)
    win_ref[half:, :] = jnp.where(dr == 0, two, one)
    pack_rows(second_ref, pack_ref, 0)
    one, two = pack_ref[:, :half].astype(BF16), pack_ref[:, half:].astype(BF16)
    wout_ref[:, :half] = jnp.where(dr == 0, one, two)
    wout_ref[:, half:] = jnp.where(dr == 0, two, one)


def own_mesh_kernel(state_ref, hot_ref, weight_ref, part_ref, near_ref):
    own_mesh(state_ref[...].astype(BF16), hot_ref, weight_ref, state_ref, part_ref, near_ref)


def first_layer(win_ref, feat_ref, keep_ref, send_ref):
    half = keep_ref.shape[0]
    send_ref[...] = dot(win_ref[half:, :], feat_ref[...]).astype(BF16)
    keep_ref[...] = dot(win_ref[:half, :], feat_ref[...])


def halo_grid_kernel(
    part_ref, even_ref, odd_ref, band_ref, sea_ref, speed_ref, win_ref,
    moved_ref, keep_ref, send_ref, feat_ref,
):
    rows, cols = sea_ref.shape
    even = on_even()
    scale = sea_ref[...].astype(F32) * speed_ref[...]
    for c in range(part_ref.shape[0] // CHUNK):
        here = slice(c * CHUNK, (c + 1) * CHUNK)
        cx = band_ref[here, 0:1]
        a, b = even_ref[here, :cols].astype(F32), odd_ref[here, :cols].astype(F32)
        for x in range(rows):
            cut = slice(x * cols, (x + 1) * cols)
            out = part_ref[here, cut]
            if x == 0:
                out = out + jnp.maximum(cx, 0.0) * scale[x : x + 1, :] * jnp.where(even, b, a)
            if x == rows - 1:
                out = out + jnp.maximum(-cx, 0.0) * scale[x : x + 1, :] * jnp.where(even, a, b)
            moved_ref[here, cut] = out
            feat_ref[here, cut] = out.astype(BF16)
    first_layer(win_ref, feat_ref, keep_ref, send_ref)


def halo_mesh_kernel(
    part_ref, even_ref, odd_ref, hot_ref, weight_ref, win_ref, after_ref,
    moved_ref, keep_ref, send_ref, ext_ref, near_ref, feat_ref,
):
    neighbours, padded, nodes = weight_ref.shape
    listed = ext_ref.shape[1] // 2
    first = even_ref.shape[1] - listed
    even = on_even()
    ext_ref[:, :listed] = jnp.where(even, odd_ref[:, first:], even_ref[:, first:])
    ext_ref[:, listed:] = jnp.where(even, even_ref[:, first:], odd_ref[:, first:])
    for k in range(neighbours):
        near_ref[k] = dot(ext_ref[...], hot_ref[k, nodes:, :])
    for c in range(padded // CHUNK):
        here = slice(c * CHUNK, (c + 1) * CHUNK)
        out = part_ref[here, :]
        for k in range(neighbours):
            out = out + weight_ref[k, here, :] * near_ref[k, here, :]
        moved_ref[here, :] = out
        feat_ref[here, :] = out.astype(BF16)
    first_layer(win_ref, feat_ref, keep_ref, send_ref)


def transferred(moved_ref, mine_ref, other_ref, wout_ref, hid_ref):
    half = mine_ref.shape[0]
    hid_ref[:half, :] = mine_ref[...]
    hid_ref[half:, :] = other_ref[...]
    return moved_ref[...] + DT_STEP * dot(wout_ref[...], hid_ref[...])


def next_grid_kernel(
    moved_ref, mine_ref, other_ref, wout_ref, state_ref, even_ref, odd_ref, hid_ref
):
    state_ref[...] = transferred(moved_ref, mine_ref, other_ref, wout_ref, hid_ref)
    even = on_even()
    cols = even_ref.shape[1]
    low, high = state_ref[:, :cols], state_ref[:, state_ref.shape[1] - cols :]
    even_ref[...] = jnp.where(even, high, low).astype(BF16)
    odd_ref[...] = jnp.where(even, low, high).astype(BF16)


def next_mesh_kernel(
    moved_ref, mine_ref, other_ref, wout_ref, halo_ref, state_ref, even_ref, odd_ref, hid_ref
):
    state_ref[...] = transferred(moved_ref, mine_ref, other_ref, wout_ref, hid_ref)
    even = on_even()
    mesh = state_ref[...].astype(BF16)
    nodes = mesh.shape[1]
    to_lower = dot(mesh, one_hot(halo_ref[0:1, :], nodes))
    to_upper = dot(mesh, one_hot(halo_ref[1:2, :], nodes))
    even_ref[...] = jnp.where(even, to_upper, to_lower).astype(BF16)
    odd_ref[...] = jnp.where(even, to_lower, to_upper).astype(BF16)


def state_kernel(moved_ref, mine_ref, other_ref, wout_ref, state_ref, hid_ref):
    state_ref[...] = transferred(moved_ref, mine_ref, other_ref, wout_ref, hid_ref)


def slots_kernel(
    gi_ref, gw_ref, gc_ref, gt_ref, mi_ref, mw_ref, mc_ref, mt_ref, after_ref,
    gmix_ref, mmix_ref, sums_ref, gland_ref, mland_ref,
):
    me = lax.axis_index("sp")
    _, _, peers, cap = gi_ref.shape
    groups = (
        (gi_ref, gw_ref, gc_ref, gt_ref, gmix_ref, gland_ref, 0),
        (mi_ref, mw_ref, mc_ref, mt_ref, mmix_ref, mland_ref, 1),
    )
    for index_ref, weight_ref, count_ref, target_ref, mix_ref, land_ref, kind in groups:
        length = mix_ref.shape[0]
        spots = lax.broadcasted_iota(jnp.int32, (length, cap), 0)
        slot = lax.broadcasted_iota(jnp.int32, (1, cap), 1)
        for p in range(peers):
            peer = lax.bitwise_xor(me, p)
            count = jnp.sum(
                jnp.where(
                    lax.broadcasted_iota(jnp.int32, (1, peers), 1) == peer, count_ref[...], 0
                ),
                axis=1,
                keepdims=True,
            )
            live = jnp.where(slot < count, 1.0, 0.0)
            mix = jnp.zeros((length, cap), F32)
            total = jnp.zeros((1, cap), F32)
            for j in range(index_ref.shape[0]):
                scaled = weight_ref[j, 0, pl.ds(peer, 1), :] * live
                mix = mix + jnp.where(spots == index_ref[j, 0, pl.ds(peer, 1), :], scaled, 0.0)
                total = total + scaled
            mix_ref[:, p * cap : (p + 1) * cap] = mix.astype(BF16)
            sums_ref[kind : kind + 1, p * cap : (p + 1) * cap] = total
            hit = lax.broadcasted_iota(jnp.int32, (land_ref.shape[1], cap), 0)
            hit = jnp.where(hit == target_ref[0, pl.ds(peer, 1), :], 1.0, 0.0)
            land_ref[p * cap : (p + 1) * cap, :] = hit.T.astype(BF16)


def slot_values(source_refs, mix_refs, sums_ref, p, cap, bands, out_ref):
    cut = slice(p * cap, (p + 1) * cap)
    for kind in (0, 1):
        value = dot(source_refs[kind][...], mix_refs[kind][:, cut])
        if bands is not None:
            row = lax.broadcasted_iota(jnp.int32, value.shape, 0)
            value = jnp.where(row == bands, sums_ref[kind : kind + 1, cut], value)
        out_ref[:, kind * cap : (kind + 1) * cap] = value.astype(BF16)


def early_kernel(grid_ref, mesh_ref, gmix_ref, mmix_ref, sums_ref, out_ref, *, bands, peer):
    cap = out_ref.shape[1] // 2
    parts = (grid_ref[...].astype(BF16), mesh_ref[...].astype(BF16))
    slot_values(parts, (gmix_ref, mmix_ref), sums_ref, peer, cap, bands, out_ref)


def mix_kernel(
    grid_ref, moved_ref, mine_ref, other_ref, wout_ref, gmix_ref, mmix_ref, sums_ref, state_ref,
    *rest, bands, which,
):
    out_refs, hid_ref = rest[:-1], rest[-1]
    state_ref[...] = transferred(moved_ref, mine_ref, other_ref, wout_ref, hid_ref)
    cap = out_refs[0].shape[1] // 2
    parts = (grid_ref[...].astype(BF16), state_ref[...].astype(BF16))
    for p, out_ref in zip(which, out_refs):
        slot_values(parts, (gmix_ref, mmix_ref), sums_ref, p, cap, bands, out_ref)


def silu(total_ref, got_ref):
    total = total_ref[...] + got_ref[...].astype(F32)
    return (total / (1.0 + jnp.exp(-total))).astype(BF16)


def silu_kernel(total_ref, got_ref, *rest):
    rest[-1][...] = silu(total_ref, got_ref)


def silu_mix_kernel(
    total_ref, got_ref, grid_ref, gmix_ref, mmix_ref, after_ref, mine_ref, mixed_ref, *, peer
):
    cap = mixed_ref.shape[1] // 2
    mine_ref[...] = silu(total_ref, got_ref)
    slot_values((grid_ref, mine_ref[...]), (gmix_ref, mmix_ref), None, peer, cap, None, mixed_ref)


def join_kernel(early_ref, mine_ref, other_ref, wout_ref, out_ref):
    half = mine_ref.shape[0]
    moved = dot(wout_ref[:, :half], mine_ref[...]) + dot(wout_ref[:, half:], other_ref[...])
    out_ref[...] = (early_ref[...].astype(F32) + DT_STEP * moved).astype(BF16)


def end_kernel(gstate_ref, mstate_ref, gland_ref, mland_ref, sea_ref, *rest, bands):
    got_refs, rest = rest[-8::-1], rest[-7:]
    grid_hbm, mesh_hbm, values_ref, sum_ref, grid_ref, mesh_ref, sem = rest
    rows, cols = sea_ref.shape
    gp = rows * cols
    freqs, dirs, _ = mesh_ref.shape
    cap = got_refs[0].shape[1] // 2
    for kind in (0, 1):
        for p, got in enumerate(got_refs):
            values_ref[kind, :, p * cap : (p + 1) * cap] = got[:, kind * cap : (kind + 1) * cap]
    sum_ref[:, gp:] = dot(values_ref[0], gland_ref[...])
    cover = sum_ref[bands : bands + 1, gp:]
    rate = BLEND_RATE / (1.0 + cover)
    keep = 1.0 - rate * cover
    sum_ref[:, gp:] = keep * mstate_ref[...] + rate * sum_ref[:, gp:]
    for f in range(freqs):
        mesh_ref[f] = sum_ref[f * dirs : (f + 1) * dirs, gp:]
    mesh_copy = pltpu.make_async_copy(mesh_ref, mesh_hbm, sem.at[0])
    mesh_copy.start()
    sum_ref[:, :gp] = dot(values_ref[1], mland_ref[...])
    cover = sum_ref[bands : bands + 1, :gp]
    rate = BLEND_RATE / (1.0 + cover)
    keep = 1.0 - rate * cover
    sea = sea_ref[...].astype(F32)
    for x in range(rows):
        cut = slice(x * cols, (x + 1) * cols)
        wet = sea[x : x + 1, :]
        out = keep[:, cut] * wet * gstate_ref[:bands, cut] + rate[:, cut] * wet * sum_ref[:bands, cut]
        grid_ref[pl.ds(x, bands, stride=rows), :] = out
    grid_copy = pltpu.make_async_copy(grid_ref, grid_hbm, sem.at[1])
    grid_copy.start()
    mesh_copy.wait()
    grid_copy.wait()


def band_table(freqs, dirs, n_fr, n_dr, padded):
    speed = (0.7 * np.power(np.float32(1.1), -np.arange(freqs * n_fr, dtype=np.float32))).astype(np.float32)
    total = dirs * n_dr
    heading = (2.0 * np.pi * (np.arange(total, dtype=np.float64) + 0.5) / total)
    table = np.zeros((n_fr, n_dr, padded, 2), np.float32)
    for i in range(n_fr):
        for j in range(n_dr):
            s = speed[i * freqs : (i + 1) * freqs, None]
            h = heading[None, j * dirs : (j + 1) * dirs]
            table[i, j, : freqs * dirs, 0] = (s * np.cos(h)).reshape(-1)
            table[i, j, : freqs * dirs, 1] = (s * np.sin(h)).reshape(-1)
    return table


def core_swap(array):
    return lax.ppermute(array, "dr", [(0, 1), (1, 0)])


def per_device(
    grid_spec, mesh_spec, grid_sea, grid_speed, nb_index, nb_angle, nb_coef, halo_list, w_in, w_out,
    g2m_index, g2m_weight, g2m_count, g2m_target, m2g_index, m2g_weight, m2g_count, m2g_target,
):
    freqs, dirs, rows, cols = grid_spec.shape
    nodes = mesh_spec.shape[2]
    listed = halo_list.shape[1]
    hid = w_in.shape[2]
    half = hid // 2
    bands = freqs * dirs
    padded = (bands // CHUNK + 1) * CHUNK
    gp = rows * cols
    points = gp + nodes
    neighbours = nb_index.shape[0]
    peers, cap = g2m_index.shape[2:]
    n_fr, n_dr = lax.axis_size("fr"), lax.axis_size("dr")

    message = ((padded, cols + listed), BF16)
    grid_shape = ((padded, gp), F32)
    mesh_shape = ((padded, nodes), F32)
    near_scratch = ((neighbours, padded, nodes), F32)
    grid_flat = grid_spec.reshape(bands * rows, cols)
    even, odd = kernel_call(
        functools.partial(begin_kernel, rows=rows),
        [message, message],
        [
            (grid_flat.shape, F32),
            (mesh_spec.shape, F32),
            (halo_list.shape, jnp.int32),
            mesh_shape,
            ((nodes, 2 * listed), BF16),
            pltpu.SemaphoreType.DMA((3,)),
        ],
        1.8,
        spaces=[HBM] * 3,
    )(grid_flat, mesh_spec, halo_list)
    table = jnp.asarray(band_table(freqs, dirs, n_fr, n_dr, padded))
    pq = jnp.concatenate([-nb_coef * jnp.cos(nb_angle), -nb_coef * jnp.sin(nb_angle)], axis=0)
    from_even = pair_swap(even, "sp", 0)
    from_odd = pair_swap(odd, "sp", 1)
    gfrom, mfrom = (from_even, from_odd), (from_even, from_odd)
    gpart, mpart, hot, weight, band, win, wout = kernel_call(
        prepare_kernel,
        [
            grid_shape,
            mesh_shape,
            ((neighbours, nodes + 2 * listed, nodes), BF16),
            near_scratch,
            ((padded, 2), F32),
            ((hid, padded), BF16),
            ((padded, hid), BF16),
        ],
        [
            (grid_flat.shape, F32),
            (mesh_spec.shape, F32),
            grid_shape,
            mesh_shape,
            near_scratch,
            ((padded, hid), F32),
            pltpu.SemaphoreType.DMA((3,)),
        ],
        3.4,
        spaces=[HBM] * 3 + [VMEM] * 6,
    )(
        grid_flat, mesh_spec, table, w_in, jnp.transpose(w_out, (1, 2, 0)),
        nb_index, pq, grid_sea, grid_speed,
    )

    def summed(total, send):
        total = total + core_swap(send).astype(F32)
        rounded = total.astype(BF16)
        got = peer_swap(rounded, "fr", 1)
        step = 2
        while step < n_fr:
            total = total + got.astype(F32)
            rounded = total.astype(BF16)
            got = peer_swap(rounded, "fr", step)
            step *= 2
        return total, rounded, got

    def activated(total, got, *after):
        (mine,) = kernel_call(
            silu_kernel, [(total.shape, BF16)], (), 0.1, spaces=[VMEM] * 2 + [pl.ANY] * len(after)
        )(total, got, *after)
        return mine

    for substep in range(NSUB):
        gmoved, gtotal, gsend = kernel_call(
            halo_grid_kernel,
            [grid_shape, ((half, gp), F32), ((half, gp), BF16)],
            [((padded, gp), BF16)],
            0.4,
        )(gpart, *gfrom, band, grid_sea, grid_speed, win)
        gtotal, ground, ggot = summed(gtotal, gsend)
        mmoved, mtotal, msend = kernel_call(
            halo_mesh_kernel,
            [mesh_shape, ((half, nodes), F32), ((half, nodes), BF16)],
            [((padded, 2 * listed), BF16), near_scratch, ((padded, nodes), BF16)],
            0.8,
            spaces=[VMEM] * 6 + [pl.ANY],
        )(mpart, *mfrom, hot, weight, win, gsend)
        mtotal, mround, mgot = summed(mtotal, msend)
        if substep < NSUB - 1:
            gmix, mmix, sums, gland, mland = kernel_call(
                slots_kernel,
                [
                    ((gp, peers * cap), BF16),
                    ((nodes, peers * cap), BF16),
                    ((2, peers * cap), F32),
                    ((peers * cap, nodes), BF16),
                    ((peers * cap, gp), BF16),
                ],
                (),
                0.5,
                spaces=[VMEM] * 8 + [pl.ANY],
            )(
                g2m_index, g2m_weight, g2m_count, g2m_target,
                m2g_index, m2g_weight, m2g_count, m2g_target, ground,
            )
            gmine = activated(gtotal, ggot, sums)
            gstate, even, odd = kernel_call(
                next_grid_kernel,
                [grid_shape, ((padded, cols), BF16), ((padded, cols), BF16)],
                [((hid, gp), BF16)],
                0.4,
            )(gmoved, gmine, core_swap(gmine), wout)
            gfrom = (pair_swap(even, "sp", 0), pair_swap(odd, "sp", 1))
            (gpart,) = kernel_call(own_grid, [grid_shape], (), 0.5)(
                gstate, band, grid_sea, grid_speed
            )
            mmine = activated(mtotal, mgot)
            mstate, even, odd = kernel_call(
                next_mesh_kernel,
                [mesh_shape, ((padded, listed), BF16), ((padded, listed), BF16)],
                [((hid, nodes), BF16)],
                0.5,
            )(mmoved, mmine, core_swap(mmine), wout, halo_list)
            mfrom = (pair_swap(even, "sp", 0), pair_swap(odd, "sp", 1))
            (mpart,) = kernel_call(own_mesh_kernel, [mesh_shape], [near_scratch], 1.0)(
                mstate, hot, weight
            )

    split = peers - 1
    slot_shape = ((padded, 2 * cap), BF16)
    (early,) = kernel_call(
        functools.partial(early_kernel, bands=bands, peer=split), [slot_shape], (), 0.4
    )(gmoved, mmoved, gmix, mmix, sums)
    early = peer_swap(early, "sp", split)
    gmine = activated(gtotal, ggot)
    (gstate,) = kernel_call(state_kernel, [grid_shape], [((hid, gp), BF16)], 0.3)(
        gmoved, gmine, core_swap(gmine), wout
    )
    mmine, mixed = kernel_call(
        functools.partial(silu_mix_kernel, peer=split),
        [((half, nodes), BF16), ((half, 2 * cap), BF16)],
        (),
        0.3,
        spaces=[VMEM] * 5 + [pl.ANY],
    )(mtotal, mgot, gmine, gmix, mmix, early)
    mother = core_swap(mmine)
    mixed = peer_swap(mixed, "sp", split)
    which = [p for p in range(peers) if p != split]
    mstate, *values = kernel_call(
        functools.partial(mix_kernel, bands=bands, which=which),
        [mesh_shape] + [slot_shape] * len(which),
        [((hid, nodes), BF16)],
        0.8,
    )(gstate, mmoved, mmine, mother, wout, gmix, mmix, sums)
    values = dict(zip(which, values))
    mixed, mstate = lax.optimization_barrier((mixed, mstate))
    for p in which[1:]:
        values[p] = peer_swap(values[p], "sp", p)
    (values[split],) = kernel_call(join_kernel, [slot_shape], (), 0.85)(
        early, mixed, core_swap(mixed), wout
    )
    values = [values[p] for p in range(peers)]
    grid_out, mesh_out = kernel_call(
        functools.partial(end_kernel, bands=bands),
        [(grid_flat.shape, F32), (mesh_spec.shape, F32)],
        [
            ((2, padded, peers * cap), BF16),
            ((padded, points), F32),
            (grid_flat.shape, F32),
            (mesh_spec.shape, F32),
            pltpu.SemaphoreType.DMA((2,)),
        ],
        1.9,
        out_space=pl.ANY,
    )(gstate, mstate, gland, mland, grid_sea, *values[::-1])
    return grid_out.reshape(grid_spec.shape), mesh_out


def solution(mesh):
    return jax.shard_map(
        per_device,
        mesh=mesh,
        in_specs=(
            P("fr", "dr", ("grp", "sp"), None),
            P("fr", "dr", ("grp", "sp")),
            P(("grp", "sp"), None),
            P(("grp", "sp"), None),
            P(None, ("grp", "sp")),
            P(None, ("grp", "sp")),
            P(None, ("grp", "sp")),
            P(None, ("grp", "sp")),
            P("fr", "dr", None),
            P(None, "fr", "dr"),
            P(None, ("grp", "sp"), None, None),
            P(None, ("grp", "sp"), None, None),
            P(("grp", "sp"), None),
            P(("grp", "sp"), None, None),
            P(None, ("grp", "sp"), None, None),
            P(None, ("grp", "sp"), None, None),
            P(("grp", "sp"), None),
            P(("grp", "sp"), None, None),
        ),
        out_specs=(P("fr", "dr", ("grp", "sp"), None), P("fr", "dr", ("grp", "sp"))),
        check_vma=False,
    )
```
